128 devices in a mesh: section: 2 (over core), tensor: 4 (over z), dp: 16 (over x, y).
Axes of the slice: x: 4, y: 4, z: 4, core: 2. Of those that a mesh axis runs over, the one named last changes fastest.
Arguments:
- layer_input: bfloat16 [2048, 2560], P('dp'), may hold values from -6 to 6
- cotangent: bfloat16 [2048, 2560], P('dp'), may hold values from -6 to 6
- seq_lengths: int32 [32, 4], P('dp'), may hold values from 0 to 64, as said below
- g_attn: bfloat16 [2, 2560], P('section', 'dp'), may hold values from 0.5 to 1.5
- w_qa: bfloat16 [2, 2560, 768], P('section', 'dp'), may hold values from -0.125 to 0.125
- g_q: bfloat16 [2, 768], P('section', 'dp'), may hold values from 0.5 to 1.5
- w_qb: bfloat16 [2, 768, 3840], P('section', 'dp', 'tensor'), may hold values from -0.21875 to 0.21875
- w_kva: bfloat16 [2, 2560, 288], P('section', 'dp'), may hold values from -0.125 to 0.125
- g_kv: bfloat16 [2, 256], P('section', 'dp'), may hold values from 0.5 to 1.5
- w_kvb: bfloat16 [2, 256, 5120], P('section', 'dp', 'tensor'), may hold values from -0.375 to 0.375
- w_o: bfloat16 [2, 2560, 2560], P('section', 'tensor', 'dp'), may hold values from -2 to 2
- g_ffn: bfloat16 [2, 2560], P('section', 'dp'), may hold values from 0.5 to 1.5
- w_gate: bfloat16 [2, 2560, 6400], P('section', 'dp', 'tensor'), may hold values from -0.125 to 0.125
- w_up: bfloat16 [2, 2560, 6400], P('section', 'dp', 'tensor'), may hold values from -0.125 to 0.125
- w_down: bfloat16 [2, 6400, 2560], P('section', 'tensor', 'dp'), may hold values from -0.625 to 0.625
Outputs:
- layer_out: bfloat16 [2, 2048, 2560], P('section', 'dp')
- input_grad: bfloat16 [2, 2048, 2560], P('section', 'dp')
- g_attn_grad: float32 [2, 2560], P('section', 'dp')
- w_qa_grad: float32 [2, 2560, 768], P('section', 'dp')
- g_q_grad: float32 [2, 768], P('section', 'dp')
- w_qb_grad: float32 [2, 768, 3840], P('section', 'dp', 'tensor')
- w_kva_grad: float32 [2, 2560, 288], P('section', 'dp')
- g_kv_grad: float32 [2, 256], P('section', 'dp')
- w_kvb_grad: float32 [2, 256, 5120], P('section', 'dp', 'tensor')
- w_o_grad: float32 [2, 2560, 2560], P('section', 'tensor', 'dp')
- g_ffn_grad: float32 [2, 2560], P('section', 'dp')
- w_gate_grad: float32 [2, 2560, 6400], P('section', 'dp', 'tensor')
- w_up_grad: float32 [2, 2560, 6400], P('section', 'dp', 'tensor')
- w_down_grad: float32 [2, 6400, 2560], P('section', 'tensor', 'dp')
The draws below stay inside these ranges and needn't reach their ends.
Inputs may be any that keep to these rules, and one draw needn't show every extreme that they name: `seq_lengths`: each row sums to 64; lengths may be 0; in one row, drawn from the seed, a single sequence fills the pack.
All inputs are finite; a program needn't handle non-finite values.
Results may differ from the reference program's by a relative error of at most 0.03.
Values may be sent and summed in bfloat16 or wider, within the bound.
No kernel may reach another device: no remote copies, remote signals or barrier semaphores. Data moves between devices by JAX's collectives and lax.ppermute only.
A program may use at most 256 MiB of HBM per device.

```python
import math
import jax
import jax.numpy as jnp
from jax import lax

D = 2560
H = 40
NOPE = 64
ROPE = 32
VD = 64
QR = 768
KVR = 256
FF = 6400
PACK = 64
MB = 2
SLOTS = 4
TOKENS = 2048
N_DP = 16


def draw_seq_lengths(key, part):
    key = jax.random.fold_in(key, 11)
    cut_key, pick_key = jax.random.split(key)
    pack_count = N_DP * MB
    cut_points = jnp.sort(jax.random.randint(cut_key, (pack_count, SLOTS - 1), 1, PACK), axis=1)
    boundary = jnp.concatenate([jnp.zeros((pack_count, 1), jnp.int32), cut_points.astype(jnp.int32), jnp.full((pack_count, 1), PACK, jnp.int32)], axis=1)
    lengths_all = boundary[:, 1:] - boundary[:, :-1]
    chosen_row = jax.random.randint(pick_key, (), 0, pack_count)
    lone_pack = jnp.concatenate([jnp.full((1,), PACK, jnp.int32), jnp.zeros((SLOTS - 1,), jnp.int32)])
    return jnp.where(jnp.arange(pack_count)[:, None] == chosen_row, lone_pack[None, :], lengths_all).astype(jnp.int32)


def levels(rng, dims, pieces, smallest, largest):
    gain = 1.0
    for axis_at, shards_of in pieces:
        draws = jax.random.uniform(jax.random.fold_in(jax.random.fold_in(rng, 6), axis_at), (shards_of,), jnp.float32, smallest / len(pieces), largest / len(pieces))
        gain = gain * jnp.repeat(jnp.exp(draws), dims[axis_at] // shards_of).reshape((-1,) + (1,) * (len(dims) - 1 - axis_at))
    return gain


def centred(key, shape, spread, most, pieces=(), held_as=jnp.bfloat16):
    result = jax.random.normal(key, shape, jnp.float32) * spread
    if len(pieces) > 0:
        result = levels(key, shape, pieces, -0.22, 0.18) * result
    return jnp.clip(result, min=-most, max=most).astype(held_as)


def setup_inputs(seed: int = 0) -> dict:
    key_of = jax.random.split(jax.random.key(seed), 16)
    return {
        "layer_input": centred(key_of[0], (TOKENS, D), 1.0, 6.0, ((0, 16),)),
        "cotangent": centred(key_of[1], (TOKENS, D), 1.0, 6.0, ((0, 16),)),
        "seq_lengths": draw_seq_lengths(jax.random.fold_in(key_of[15], 71), 0),
        "g_attn": jnp.clip(1.0 + 0.1 * jax.random.normal(key_of[3], (2, D), jnp.float32), 0.5, 1.5).astype(jnp.bfloat16),
        "w_qa": centred(key_of[4], (2, D, QR), D ** -0.5, 0.125, ((0, 2), (1, 16))),
        "g_q": jnp.clip(1.0 + 0.1 * jax.random.normal(key_of[5], (2, QR), jnp.float32), 0.5, 1.5).astype(jnp.bfloat16),
        "w_qb": centred(key_of[6], (2, QR, H * (NOPE + ROPE)), QR ** -0.5, 0.21875, ((0, 2), (1, 16), (2, 4))),
        "w_kva": centred(key_of[7], (2, D, KVR + ROPE), D ** -0.5, 0.125, ((0, 2), (1, 16))),
        "g_kv": jnp.clip(1.0 + 0.1 * jax.random.normal(key_of[8], (2, KVR), jnp.float32), 0.5, 1.5).astype(jnp.bfloat16),
        "w_kvb": centred(key_of[9], (2, KVR, H * (NOPE + VD)), KVR ** -0.5, 0.375, ((0, 2), (1, 16), (2, 4))),
        "w_o": centred(key_of[10], (2, H * VD, D), (H * VD // 400 + 1) ** -0.5, 2.0, ((0, 2), (1, 4), (2, 16))),
        "g_ffn": jnp.clip(1.0 + 0.1 * jax.random.normal(key_of[11], (2, D), jnp.float32), 0.5, 1.5).astype(jnp.bfloat16),
        "w_gate": centred(key_of[12], (2, D, FF), D ** -0.5, 0.125, ((0, 2), (1, 16), (2, 4))),
        "w_up": centred(key_of[13], (2, D, FF), D ** -0.5, 0.125, ((0, 2), (1, 16), (2, 4))),
        "w_down": centred(key_of[14], (2, FF, D), (FF // 80 + 1) ** -0.5, 0.625, ((0, 2), (1, 4), (2, 16))),
    }


RES_SCALE = 1.4 / math.sqrt(62.0)
EPSILON = 1e-05
HIGHEST = lax.Precision.HIGHEST

@jax.custom_vjp
def low(v):
    return lax.optimization_barrier(v.astype(jnp.bfloat16)).astype(jnp.float32)

@jax.custom_vjp
def low_back(v):
    return v

def low_keep(v):
    return (low(v), None)

def low_pass(kept, grad):
    return (grad,)

def back_keep(v):
    return (v, None)

def back_low(kept, grad):
    return (low(grad),)
low.defvjp(low_keep, low_pass)
low_back.defvjp(back_keep, back_low)

def product(left_side, right_side):
    return jnp.dot(left_side, right_side, precision=HIGHEST, preferred_element_type=jnp.float32)

def rms_scale(inputs, gain_vec):
    return inputs * lax.rsqrt(lax.optimization_barrier(jnp.mean(inputs * inputs, axis=-1, keepdims=True)) + EPSILON) * gain_vec

def rotate(inputs, cosine, sine_table):
    half_width = inputs.shape[-1] // 2
    turned = jnp.concatenate([-inputs[..., half_width:], inputs[..., :half_width]], axis=-1)
    return inputs * cosine + turned * sine_table

def pack_tables(seq_row):
    row_index = jnp.arange(PACK, dtype=jnp.int32)
    seq_ends = jnp.cumsum(seq_row).astype(jnp.int32)
    past_end = row_index[:, None] >= seq_ends[None, :]
    segment = lax.optimization_barrier(jnp.sum(past_end.astype(jnp.int32), axis=1))
    seq_start = lax.optimization_barrier(jnp.sum(jnp.where(past_end, seq_row[None, :], 0), axis=1)).astype(jnp.int32)
    position = (row_index - seq_start).astype(jnp.float32)
    frequency = 10000.0 ** (-2.0 * jnp.arange(ROPE // 2, dtype=jnp.float32) / ROPE)
    angles = position[:, None] * frequency[None, :]
    cosine = jnp.concatenate([jnp.cos(angles), jnp.cos(angles)], axis=1)
    sine_table = jnp.concatenate([jnp.sin(angles), jnp.sin(angles)], axis=1)
    allowed = (segment[:, None] == segment[None, :]) & (row_index[None, :] <= row_index[:, None])
    return (cosine, sine_table, allowed)

def layer_apply(block_in, weights, tables):
    g_attn, w_qa, g_q, w_qb, w_kva, g_kv, w_kvb, w_o, g_ffn, w_gate, w_up, w_down = weights
    cosine, sine_table, allowed = tables
    row_count = block_in.shape[0]
    normed = low(rms_scale(block_in, g_attn))
    latent_q = low_back(product(normed, w_qa))
    squeezed = low(rms_scale(latent_q, g_q))
    query_raw = low_back(product(squeezed, w_qb)).reshape(row_count, H, NOPE + ROPE)
    query_all = low(jnp.concatenate([query_raw[..., :NOPE], rotate(query_raw[..., NOPE:], cosine[:, None, :], sine_table[:, None, :])], axis=-1))
    latent_kv = low_back(product(normed, w_kva))
    compact = low(rms_scale(latent_kv[:, :KVR], g_kv))
    key_rope = low(rotate(latent_kv[:, KVR:], cosine, sine_table))
    key_value = low_back(product(compact, w_kvb)).reshape(row_count, H, NOPE + VD)
    key_all = jnp.concatenate([low(key_value[..., :NOPE]), jnp.broadcast_to(key_rope[:, None, :], (row_count, H, ROPE))], axis=-1)
    value_all = low(key_value[..., NOPE:])
    scores = low_back(jnp.einsum('qhd,khd->hqk', query_all, key_all, precision=HIGHEST) * (NOPE + ROPE) ** (-0.5))
    attn_probs = jax.nn.softmax(jnp.where(allowed[None], scores, -1e+30), axis=-1)
    mixed_heads = jnp.einsum('hqk,khd->qhd', low(attn_probs), value_all, precision=HIGHEST).reshape(row_count, H * VD)
    mixed_heads = low(low_back(mixed_heads))
    attended = low_back(product(mixed_heads, w_o))
    middle = block_in + RES_SCALE * attended
    normed_two = low(rms_scale(middle, g_ffn))
    gate_act = low_back(product(normed_two, w_gate))
    up_act = low_back(product(normed_two, w_up))
    hidden = low(jax.nn.silu(gate_act) * up_act)
    return middle + RES_SCALE * low_back(product(hidden, w_down))

def reference(layer_input, cotangent, seq_lengths, g_attn, w_qa, g_q, w_qb, w_kva, g_kv, w_kvb, w_o, g_ffn, w_gate, w_up, w_down):
    weights = tuple((member.astype(jnp.float32) for member in (g_attn, w_qa, g_q, w_qb, w_kva, g_kv, w_kvb, w_o, g_ffn, w_gate, w_up, w_down)))
    pack_count = N_DP * MB
    pack_rows = layer_input.astype(jnp.float32).reshape(pack_count, PACK, D)
    tap_rows = jnp.zeros((pack_count, PACK, D), jnp.float32)

    def forward(pack_rows, tap_rows, weights):

        def one_pack(pack_items):
            block_in, tap_one, seq_row = pack_items
            tables = pack_tables(seq_row)
            first_out = layer_apply(block_in, tuple((member[0] for member in weights)), tables)
            carried = low(low_back(first_out))
            return (carried, layer_apply(carried + tap_one, tuple((member[1] for member in weights)), tables))
        return lax.map(jax.checkpoint(one_pack), (pack_rows, tap_rows, seq_lengths))
    outputs, pullback = jax.vjp(forward, pack_rows, tap_rows, weights)
    first_out, second_out = outputs
    cot_rows = cotangent.astype(jnp.float32).reshape(pack_count, PACK, D)
    d_packs, d_taps, d_weights = pullback((jnp.zeros_like(first_out), cot_rows))
    layer_out = jnp.stack([first_out, second_out]).reshape(2, pack_count * PACK, D).astype(jnp.bfloat16)
    input_grad = jnp.stack([d_packs, d_taps]).reshape(2, pack_count * PACK, D).astype(jnp.bfloat16)
    return (layer_out, input_grad, d_weights[0], d_weights[1], d_weights[2], d_weights[3], d_weights[4], d_weights[5], d_weights[6], d_weights[7], d_weights[8], d_weights[9], d_weights[10], d_weights[11])
```

```python
import math

import jax
import jax.numpy as jnp
from jax import lax
from jax.experimental import pallas as pl
from jax.experimental.pallas import tpu as pltpu
from jax.sharding import PartitionSpec as P

D = 2560
NOPE = 64
ROPE = 32
VD = 64
QR = 768
KVR = 256
PACK = 64
MB = 2
N_DP = 16
N_Z = 4
HEADS = 5
SLICE = D // N_DP
FF_PART = 100
LANES = 128
SHARD = 16
RES_SCALE = 1.4 / math.sqrt(62.0)
EPSILON = 1e-05
SCORE_SCALE = (NOPE + ROPE) ** (-0.5)
BF16 = jnp.bfloat16
F32 = jnp.float32


def dot(a, b):
    return jnp.dot(a, b, preferred_element_type=F32)


def dot_tn(a, b):
    return lax.dot_general(a, b, (((0,), (0,)), ((), ())), preferred_element_type=F32)


def dot_nt(a, b):
    return lax.dot_general(a, b, (((1,), (1,)), ((), ())), preferred_element_type=F32)


def to_core(x):
    return lax.ppermute(x, "section", [(0, 1), (1, 0)])


def z_hop(x, by):
    return lax.ppermute(x, "tensor", [(i, (i + by) % N_Z) for i in range(N_Z)])


def by_core(core, mine, other):
    return jnp.where(core == 0, mine, other), jnp.where(core == 0, other, mine)


def from_here(x):
    return lax.dynamic_slice_in_dim(jnp.concatenate([x, x]), lax.axis_index("tensor"), N_Z, 0)


def from_zero(x):
    at = (N_Z - lax.axis_index("tensor")) % N_Z
    return lax.dynamic_slice_in_dim(jnp.concatenate([x, x]), at, N_Z, 0)


def gather_z(x):
    return [x, z_hop(x, -1), z_hop(x, 2), z_hop(x, 1)]


def gather_tokens(x):
    mine = jnp.concatenate(gather_z(x), axis=0)
    return mine, to_core(mine)


def in_order(mine, other):
    core = lax.axis_index("section")
    shape = (N_Z, SHARD, mine.shape[-1])
    mine, other = from_zero(mine.reshape(shape)), from_zero(other.reshape(shape))
    return jnp.concatenate(by_core(core, mine, other), axis=0).reshape(-1, shape[-1])


def scatter_tokens(part):
    half = part[:PACK].astype(F32) + to_core(part[PACK:]).astype(F32)
    sent = half.astype(BF16)
    total = half[:SHARD]
    for by in (2, 1, 3):
        total = total + z_hop(sent[SHARD * by : SHARD * (by + 1)], by).astype(F32)
    return total


def gather_dp(x):
    copies = jnp.broadcast_to(x[None], (N_DP,) + x.shape)
    return lax.all_to_all(copies, "dp", 0, 0).reshape(N_DP * x.shape[0], x.shape[1])


def scatter_dp(part):
    pieces = lax.all_to_all(part.reshape(N_DP, SHARD, D), "dp", 0, 0)
    return jnp.sum(pieces.astype(F32), axis=0)


def norm_scale(x):
    return lax.rsqrt(jnp.mean(x * x, axis=-1, keepdims=True) + EPSILON)


def norm(x, gain):
    return x * norm_scale(x) * gain


def norm_back(x, gain, d):
    q = norm_scale(x)
    along = jnp.mean(gain * d * x, axis=-1, keepdims=True)
    return q * gain * d - x * (q * q * q) * along, jnp.sum(d * x * q, axis=0)


MATS = 3 * LANES
TOKENS = N_DP * SHARD
FF_VMEM = 56 * 1024 * 1024
FF_SCRATCH = [
    pltpu.VMEM((N_Z, D, MATS), BF16),
    pltpu.VMEM((TOKENS, D), F32),
    pltpu.SemaphoreType.DMA((N_Z,)),
]


def ffn_copies(own_ref, mine, other, w_ref, sems):
    copies = [pltpu.make_async_copy(mine[z], w_ref.at[z], sems.at[z]) for z in range(N_Z)]
    others = [pltpu.make_async_copy(other[z], w_ref.at[z], sems.at[z]) for z in range(N_Z)]

    @pl.when(own_ref[0] == 1)
    def _():
        for copy in copies:
            copy.start()

    @pl.when(own_ref[0] != 1)
    def _():
        for copy in others:
            copy.start()

    return copies


def ffn_forward_kernel(own_ref, n_ref, *refs):
    mine, other = refs[:N_Z], refs[N_Z : 2 * N_Z]
    part_ref, gu_ref, hid_ref, w_ref, acc_ref, sems = refs[2 * N_Z :]
    copies = ffn_copies(own_ref, mine, other, w_ref, sems)
    for z in range(N_Z):
        copies[z].wait()
        gu = dot(n_ref[...], w_ref[z, :, : 2 * LANES])
        gu_ref[:, 2 * LANES * z : 2 * LANES * (z + 1)] = gu
        gate, up = gu[:, :LANES], gu[:, LANES:]
        hidden = (gate * jax.nn.sigmoid(gate) * up).astype(BF16)
        hid_ref[:, LANES * z : LANES * (z + 1)] = hidden
        out = dot_nt(hidden, w_ref[z, :, 2 * LANES :])
        if z == 0:
            acc_ref[...] = out
        elif z < N_Z - 1:
            acc_ref[...] += out
        else:
            part_ref[...] = (acc_ref[...] + out).astype(BF16)


def ffn_specs(arrays):
    vmem = pl.BlockSpec(memory_space=pltpu.VMEM)
    smem = pl.BlockSpec(memory_space=pltpu.SMEM)
    return [smem] + [vmem] * arrays + [pl.BlockSpec(memory_space=pl.ANY)] * (2 * N_Z)


def ffn_forward(own, rows, weights):
    return pl.pallas_call(
        ffn_forward_kernel,
        out_shape=(
            jax.ShapeDtypeStruct((TOKENS, D), BF16),
            jax.ShapeDtypeStruct((TOKENS, 2 * LANES * N_Z), F32),
            jax.ShapeDtypeStruct((TOKENS, LANES * N_Z), BF16),
        ),
        in_specs=ffn_specs(1),
        out_specs=(pl.BlockSpec(memory_space=pltpu.VMEM),) * 3,
        scratch_shapes=FF_SCRATCH,
        compiler_params=pltpu.CompilerParams(vmem_limit_bytes=FF_VMEM),
        name="ffn_forward",
    )(own, rows, *weights)


def ffn_backward_kernel(own_ref, dm_ref, n_ref, gu_ref, hid_ref, *refs):
    mine, other, part_ref = refs[:N_Z], refs[N_Z : 2 * N_Z], refs[2 * N_Z]
    grads = refs[2 * N_Z + 1 : 3 * N_Z + 1]
    w_ref, acc_ref, sems = refs[3 * N_Z + 1 :]
    copies = ffn_copies(own_ref, mine, other, w_ref, sems)
    for z in range(N_Z):
        hidden = hid_ref[:, LANES * z : LANES * (z + 1)]
        grads[z][:, 2 * LANES :] = dot_tn(dm_ref[...], hidden).astype(BF16)
        copies[z].wait()
        d_hidden = dot(dm_ref[...], w_ref[z, :, 2 * LANES :])
        gate = gu_ref[:, 2 * LANES * z : 2 * LANES * z + LANES]
        up = gu_ref[:, 2 * LANES * z + LANES : 2 * LANES * (z + 1)]
        s = jax.nn.sigmoid(gate)
        d_gate = d_hidden * up * (s + gate * s * (1.0 - s))
        d_up = d_hidden * (gate * s)
        d_gu = jnp.concatenate([d_gate.astype(BF16), d_up.astype(BF16)], axis=1)
        grads[z][:, : 2 * LANES] = dot_tn(n_ref[...], d_gu).astype(BF16)
        out = dot_nt(d_gu, w_ref[z, :, : 2 * LANES])
        if z == 0:
            acc_ref[...] = out
        elif z < N_Z - 1:
            acc_ref[...] += out
        else:
            part_ref[...] = (acc_ref[...] + out).astype(BF16)


def ffn_backward(own, d_rows, rows, gu, hidden, weights):
    out = pl.pallas_call(
        ffn_backward_kernel,
        out_shape=(jax.ShapeDtypeStruct((TOKENS, D), BF16),)
        + tuple(jax.ShapeDtypeStruct((D, MATS), BF16) for _ in range(N_Z)),
        in_specs=ffn_specs(4),
        out_specs=(pl.BlockSpec(memory_space=pltpu.VMEM),) * (N_Z + 1),
        scratch_shapes=FF_SCRATCH,
        compiler_params=pltpu.CompilerParams(vmem_limit_bytes=FF_VMEM),
        name="ffn_backward",
    )(own, d_rows, rows, gu, hidden, *weights)
    return out[0], out[1:]


FF = N_DP * FF_PART
WINDOW = 2 * LANES
FF_PADDED = (FF - FF_PART) // LANES * LANES + WINDOW


def identity(n):
    at = lax.broadcasted_iota(jnp.int32, (n, n), 0)
    return jnp.where(at == lax.broadcasted_iota(jnp.int32, (n, n), 1), 1.0, 0.0).astype(BF16)


def ffn_pack_kernel(gate_ref, up_ref, down_ref, out_ref, wide_ref):
    wide_ref[0, :, :FF] = gate_ref[...].astype(F32)
    wide_ref[1, :, :FF] = up_ref[...].astype(F32)
    wide_ref[2, :, :FF] = dot_nt(identity(SLICE), down_ref[...])
    valid = lax.broadcasted_iota(jnp.int32, (SLICE, LANES), 1) < FF_PART
    for p in range(N_DP):
        at = FF_PART * p // LANES * LANES
        by = FF_PART * p - at
        for m in range(3):
            window = wide_ref[m, :, at : at + WINDOW]
            if by > 0:
                window = pltpu.roll(window, WINDOW - by, 1)
            block = jnp.where(valid, window[:, :LANES], 0.0)
            out_ref[p, :, LANES * m : LANES * (m + 1)] = block.astype(BF16)


def ffn_pack(w_gate, w_up, w_down):
    return pl.pallas_call(
        ffn_pack_kernel,
        out_shape=jax.ShapeDtypeStruct((N_DP, SLICE, MATS), BF16),
        scratch_shapes=[pltpu.VMEM((3, SLICE, FF_PADDED), F32)],
        compiler_params=pltpu.CompilerParams(vmem_limit_bytes=FF_VMEM),
        name="ffn_pack",
    )(w_gate, w_up, w_down)


def ffn_unpack_kernel(in_ref, gate_ref, up_ref, down_ref, wide_ref):
    wide_ref[...] = jnp.zeros(wide_ref.shape, F32)
    valid = lax.broadcasted_iota(jnp.int32, (SLICE, LANES), 1) < FF_PART
    for p in range(N_DP):
        at = FF_PART * p // LANES * LANES
        by = FF_PART * p - at
        for m in range(3):
            block = in_ref[p, :, LANES * m : LANES * (m + 1)].astype(F32)
            block = jnp.where(valid, block, 0.0)
            window = jnp.concatenate([block, jnp.zeros_like(block)], axis=1)
            if by > 0:
                window = pltpu.roll(window, by, 1)
            wide_ref[m, :, at : at + WINDOW] += window
    gate_ref[...] = wide_ref[0, :, :FF]
    up_ref[...] = wide_ref[1, :, :FF]
    down_ref[...] = dot_tn(wide_ref[2, :, :FF].astype(BF16), identity(SLICE))


def ffn_unpack(blocks):
    return pl.pallas_call(
        ffn_unpack_kernel,
        out_shape=(
            jax.ShapeDtypeStruct((SLICE, FF), F32),
            jax.ShapeDtypeStruct((SLICE, FF), F32),
            jax.ShapeDtypeStruct((FF, SLICE), F32),
        ),
        scratch_shapes=[pltpu.VMEM((3, SLICE, FF_PADDED), F32)],
        compiler_params=pltpu.CompilerParams(vmem_limit_bytes=FF_VMEM),
        name="ffn_unpack",
    )(blocks)


A_ROWS = SLICE + QR // N_DP + KVR // N_DP
A_COLS = 896
LAT = 640
WO_AT = 512
WO = 384
HEAD = 128
ROWS = MB * PACK
QB_ROWS = slice(SLICE, SLICE + QR // N_DP)
KVB_ROWS = slice(SLICE + QR // N_DP, A_ROWS)
E_ROWS = 2 * A_ROWS - SLICE
ATT_VMEM = 48 * 1024 * 1024


def latent_kernel(mine_ref, other_ref, gain_ref, pack_ref, normed_ref, lat_ref, w_ref, sem):
    copy = pltpu.make_async_copy(pack_ref.at[:, 0:SLICE, 0:LAT], w_ref, sem)
    copy.start()
    normed_ref[:PACK] = norm(mine_ref[...].astype(F32), gain_ref[...]).astype(BF16)
    normed_ref[PACK:] = norm(other_ref[...].astype(F32), gain_ref[...]).astype(BF16)
    copy.wait()
    lat_ref[...] = dot(normed_ref[...], w_ref[...].reshape(D, LAT))


def latents(rows, gain, pack):
    vmem = pl.BlockSpec(memory_space=pltpu.VMEM)
    return pl.pallas_call(
        latent_kernel,
        out_shape=(
            jax.ShapeDtypeStruct((ROWS, D), BF16),
            jax.ShapeDtypeStruct((ROWS, LAT), F32),
        ),
        in_specs=[vmem, vmem, vmem, pl.BlockSpec(memory_space=pl.ANY)],
        out_specs=(vmem, vmem),
        scratch_shapes=[pltpu.VMEM((N_DP, SLICE, LAT), BF16), pltpu.SemaphoreType.DMA],
        compiler_params=pltpu.CompilerParams(vmem_limit_bytes=ATT_VMEM),
        name="latents",
    )(*rows, gain, pack)


def weight_copies(pack_ref, qb_ref, kvb_ref, wo_ref, sems):
    sources = (
        pack_ref.at[:, QB_ROWS, 0:LAT],
        pack_ref.at[:, KVB_ROWS, 0:LAT],
        pack_ref.at[:, 0:SLICE, WO_AT : WO_AT + WO],
    )
    targets = (qb_ref, kvb_ref, wo_ref)
    copies = [pltpu.make_async_copy(a, b, sems.at[i]) for i, (a, b) in enumerate(zip(sources, targets))]
    for copy in copies:
        copy.start()
    return copies


def weight_scratch():
    return [
        pltpu.VMEM((N_DP, QR // N_DP, LAT), BF16),
        pltpu.VMEM((N_DP, KVR // N_DP, LAT), BF16),
        pltpu.VMEM((N_DP, SLICE, WO), BF16),
        pltpu.SemaphoreType.DMA((3,)),
    ]


def lanes_of(x):
    return lax.broadcasted_iota(jnp.int32, x.shape, 1)


def turn(x, tab_ref):
    return (
        x * tab_ref[0]
        + pltpu.roll(x, HEAD - ROPE // 2, 1) * tab_ref[1]
        + pltpu.roll(x, ROPE // 2, 1) * tab_ref[2]
    )


def turn_back(x, tab_ref):
    return (
        x * tab_ref[0]
        - pltpu.roll(x, HEAD - ROPE // 2, 1) * tab_ref[1]
        - pltpu.roll(x, ROPE // 2, 1) * tab_ref[2]
    )


def head_columns(h):
    return slice(HEAD * h, HEAD * (h + 1))


def probs_of(query, key, tab_ref):
    scores = jnp.where(tab_ref[3] < 0.0, -1e30, dot_nt(query, key) * SCORE_SCALE)
    weight = jnp.exp(scores - jnp.max(scores, axis=-1, keepdims=True))
    return weight / jnp.sum(weight, axis=-1, keepdims=True)


def attend_kernel(
    core_ref, mine_ref, other_ref, tab_ref, gq_ref, gkv_ref, pack_ref,
    part_ref, sq_ref, comp_ref, q_ref, kv_ref, kr_ref, mixed_ref, lat_ref,
    qb_ref, kvb_ref, wo_ref, sems,
):
    copies = weight_copies(pack_ref, qb_ref, kvb_ref, wo_ref, sems)
    zero = core_ref[0] == 0
    other = jnp.concatenate([other_ref[PACK:], other_ref[:PACK]], axis=0)
    second = jnp.where(zero, other, mine_ref[...])
    first = jnp.where(zero, mine_ref[:, :512], other[:, :512])
    latent_q = jnp.concatenate([first, second[:, :256]], axis=1)
    lat_ref[:, :QR] = latent_q[:SHARD]
    lat_ref[:, QR:] = second[:SHARD, 256:512]
    sq_ref[...] = norm(latent_q, gq_ref[...]).astype(BF16)
    comp_ref[...] = norm(second[:, 256:512], gkv_ref[...]).astype(BF16)
    rope = pltpu.roll(second[:, 512:640], NOPE, 1)
    rope = jnp.where(lanes_of(rope) < NOPE, 0.0, turn(rope, tab_ref)).astype(BF16)
    kr_ref[...] = rope
    copies[0].wait()
    query = dot(sq_ref[...], qb_ref[...].reshape(QR, LAT))
    for h in range(HEADS):
        q_ref[:, head_columns(h)] = turn(query[:, head_columns(h)], tab_ref).astype(BF16)
    copies[1].wait()
    kv_ref[...] = dot(comp_ref[...], kvb_ref[...].reshape(KVR, LAT)).astype(BF16)
    heads = []
    for h in range(HEADS):
        kv = kv_ref[:, head_columns(h)]
        key = jnp.where(lanes_of(kv) < NOPE, kv, rope)
        probs = probs_of(q_ref[:, head_columns(h)], key, tab_ref)
        heads.append(dot(probs.astype(BF16), kv))
    low = lanes_of(heads[0]) < NOPE
    tiles = [jnp.where(low, 0.0, heads[0])]
    tiles += [jnp.where(low, pltpu.roll(heads[i], NOPE, 1), heads[i + 1]) for i in (1, 3)]
    mixed_ref[...] = jnp.concatenate(tiles, axis=1).astype(BF16)
    copies[2].wait()
    part_ref[...] = dot_nt(mixed_ref[...], wo_ref[...].reshape(D, WO)).astype(BF16)


def attend(core, mine, other, tab, g_q, g_kv, pack):
    vmem = pl.BlockSpec(memory_space=pltpu.VMEM)
    widths = (D, QR, KVR, LAT, LAT, HEAD, WO)
    return pl.pallas_call(
        attend_kernel,
        out_shape=tuple(jax.ShapeDtypeStruct((ROWS, w), BF16) for w in widths)
        + (jax.ShapeDtypeStruct((SHARD, QR + KVR), F32),),
        in_specs=[pl.BlockSpec(memory_space=pltpu.SMEM)] + [vmem] * 5 + [pl.BlockSpec(memory_space=pl.ANY)],
        out_specs=(vmem,) * (len(widths) + 1),
        scratch_shapes=weight_scratch(),
        compiler_params=pltpu.CompilerParams(vmem_limit_bytes=ATT_VMEM),
        name="attend",
    )(core, mine, other, tab, g_q, g_kv, pack)


def attend_back_kernel(
    mine_ref, other_ref, tab_ref, sq_ref, comp_ref, q_ref, kv_ref, kr_ref, mixed_ref, pack_ref,
    part_ref, early_ref,
    dq_ref, dkv_ref, qb_ref, kvb_ref, wo_ref, sems,
):
    copies = weight_copies(pack_ref, qb_ref, kvb_ref, wo_ref, sems)
    d_att = jnp.concatenate([mine_ref[...], other_ref[...]], axis=0)
    wo_grad = dot_tn(d_att, mixed_ref[...]).astype(BF16)
    early_ref[:, :SLICE, :] = wo_grad.reshape(N_DP, SLICE, WO)
    copies[2].wait()
    d_mixed = dot(d_att, wo_ref[...].reshape(D, WO))
    rope = kr_ref[...]
    d_rope = jnp.zeros((ROWS, HEAD), F32)
    for h in range(HEADS):
        kv = kv_ref[:, head_columns(h)]
        low = lanes_of(kv) < NOPE
        key = jnp.where(low, kv, rope)
        query = q_ref[:, head_columns(h)]
        probs = probs_of(query, key, tab_ref)
        tile = d_mixed[:, head_columns((h + 1) // 2)]
        if h % 2 == 1:
            tile = pltpu.roll(tile, NOPE, 1)
        tile = jnp.where(low, 0.0, tile).astype(BF16)
        d_probs = dot_nt(tile, kv)
        d_scores = probs * (d_probs - jnp.sum(probs * d_probs, axis=-1, keepdims=True))
        d_scores = d_scores.astype(BF16)
        d_query = dot(d_scores, key) * SCORE_SCALE
        d_key = dot_tn(d_scores, query) * SCORE_SCALE
        d_value = dot_tn(probs.astype(BF16), tile)
        dq_ref[:, head_columns(h)] = turn_back(d_query, tab_ref).astype(BF16)
        dkv_ref[:, head_columns(h)] = jnp.where(low, d_key, d_value).astype(BF16)
        d_rope = d_rope + d_key
    d_rope = jnp.where(lanes_of(d_rope) < NOPE, 0.0, turn_back(jnp.where(lanes_of(d_rope) < NOPE, 0.0, d_rope), tab_ref))
    copies[0].wait()
    copies[1].wait()
    part_ref[:, :QR] = dot_nt(dq_ref[...], qb_ref[...].reshape(QR, LAT)).astype(BF16)
    part_ref[:, QR : QR + KVR] = dot_nt(dkv_ref[...], kvb_ref[...].reshape(KVR, LAT)).astype(BF16)
    part_ref[:, QR + KVR :] = d_rope.astype(BF16)
    qb_grad = dot_tn(sq_ref[...], dq_ref[...]).astype(BF16).reshape(N_DP, QR // N_DP, LAT)
    kvb_grad = dot_tn(comp_ref[...], dkv_ref[...]).astype(BF16).reshape(N_DP, KVR // N_DP, LAT)
    early_ref[:, QB_ROWS, :] = qb_grad[:, :, :WO]
    early_ref[:, KVB_ROWS, :] = kvb_grad[:, :, :WO]
    more = slice(A_ROWS, A_ROWS + QR // N_DP)
    early_ref[:, more, : LAT - WO] = qb_grad[:, :, WO:]
    early_ref[:, more.stop :, : LAT - WO] = kvb_grad[:, :, WO:]
    early_ref[:, A_ROWS:, LAT - WO :] = jnp.zeros((N_DP, E_ROWS - A_ROWS, 2 * WO - LAT), BF16)


def attend_back(d_attended, tab, saved, pack):
    vmem = pl.BlockSpec(memory_space=pltpu.VMEM)
    return pl.pallas_call(
        attend_back_kernel,
        out_shape=(
            jax.ShapeDtypeStruct((ROWS, QR + KVR + HEAD), BF16),
            jax.ShapeDtypeStruct((N_DP, E_ROWS, WO), BF16),
        ),
        in_specs=[vmem] * 9 + [pl.BlockSpec(memory_space=pl.ANY)],
        out_specs=(vmem,) * 2,
        scratch_shapes=[pltpu.VMEM((ROWS, LAT), BF16), pltpu.VMEM((ROWS, LAT), BF16)] + weight_scratch(),
        compiler_params=pltpu.CompilerParams(vmem_limit_bytes=ATT_VMEM),
        name="attend_back",
    )(*d_attended, tab, *saved, pack)


def normed_back_kernel(d_ref, pack_ref, out_ref, w_ref, sem):
    copy = pltpu.make_async_copy(pack_ref.at[:, 0:SLICE, 0:LAT], w_ref, sem)
    copy.start()
    copy.wait()
    out_ref[...] = dot_nt(d_ref[...], w_ref[...].reshape(D, LAT))


def normed_back(d_latent, pack):
    vmem = pl.BlockSpec(memory_space=pltpu.VMEM)
    return pl.pallas_call(
        normed_back_kernel,
        out_shape=jax.ShapeDtypeStruct((d_latent.shape[0], D), F32),
        in_specs=[vmem, pl.BlockSpec(memory_space=pl.ANY)],
        out_specs=vmem,
        scratch_shapes=[pltpu.VMEM((N_DP, SLICE, LAT), BF16), pltpu.SemaphoreType.DMA],
        compiler_params=pltpu.CompilerParams(vmem_limit_bytes=ATT_VMEM),
        name="normed_back",
    )(d_latent, pack)


def attention_packs(w_qa, w_qb, w_kva, w_kvb, w_o, gains):
    def pad(x, width, at=0):
        return jnp.pad(x, ((0, 0), (at, width - at - x.shape[1])))

    wo_t = w_o.T
    half = HEADS * VD
    latent = (w_qa[:, :512], jnp.concatenate([w_qa[:, 512:], w_kva], axis=1))
    qb = w_qb.reshape(QR // N_DP, 2, HEADS, NOPE + ROPE)
    qb = jnp.pad(qb, ((0, 0), (0, 0), (0, 0), (0, HEAD - NOPE - ROPE)))
    qb = qb.reshape(QR // N_DP, 2, LAT)
    kvb = w_kvb.reshape(KVR // N_DP, 2, LAT)
    packs = []
    for i in range(2):
        wide = jnp.concatenate([pad(latent[i], A_COLS - half), wo_t[:, half * i : half * (i + 1)]], axis=1)
        low = jnp.concatenate([qb[:, i], gains], axis=1)
        packs.append(jnp.concatenate([wide, low, pad(kvb[:, i], A_COLS)], axis=0))
    return jnp.stack(packs)


def attention_gains(pack):
    gains = pack[:, SLICE : SLICE + 3, LAT:].astype(F32)
    return dict(
        attn=gains[:, 0, :SLICE].reshape(1, D),
        ffn=gains[:, 1, :SLICE].reshape(1, D),
        q=gains[:, 2, : QR // N_DP].reshape(1, QR),
        kv=gains[:, 2, QR // N_DP : QR // N_DP + KVR // N_DP].reshape(1, KVR),
    )


def head_tables(seq_lengths):
    core, t = lax.axis_index("section"), lax.axis_index("tensor")
    at = jnp.arange(ROWS, dtype=jnp.int32)
    pack = (core + at // PACK) % 2
    row = (t + at % PACK // SHARD) % N_Z * SHARD + at % SHARD
    lengths = jnp.where(pack[:, None] == 0, seq_lengths[:1], seq_lengths[1:])
    past_end = row[:, None] >= jnp.cumsum(lengths, axis=1)
    segment = jnp.sum(past_end.astype(jnp.int32), axis=1)
    position = (row - jnp.sum(jnp.where(past_end, lengths, 0), axis=1)).astype(F32)
    frequency = 10000.0 ** (-2.0 * jnp.arange(ROPE // 2, dtype=F32) / ROPE)
    angles = position[:, None] * frequency[None, :]
    cosine, sine = jnp.cos(angles), jnp.sin(angles)
    sequence = pack * PACK + segment
    allowed = (sequence[:, None] == sequence[None, :]) & (row[None, :] <= row[:, None])

    def tile(*pieces):
        x = jnp.concatenate(pieces, axis=1)
        return jnp.pad(x, ((0, 0), (0, HEAD - x.shape[1])))

    ones, none = jnp.ones((ROWS, NOPE), F32), jnp.zeros((ROWS, NOPE), F32)
    bias = jnp.where(allowed, 0.0, -1.0).astype(F32)
    return jnp.stack(
        [tile(ones, cosine, cosine), tile(none, -sine), tile(none, jnp.zeros_like(sine), sine), bias]
    )


def ring_hop(x, by, cores=(0, 1)):
    pairs = [
        (c * N_Z + t, c * N_Z + (t + (by if c == 0 else -by)) % N_Z) for c in cores for t in range(N_Z)
    ]
    return lax.ppermute(x, ("section", "tensor"), pairs)


def ring_pieces(x):
    near = ring_hop(x, 1)
    return [x, near, ring_hop(x, -1), ring_hop(near, 1)]


def ring_sum(layer, pieces):
    def add(*terms):
        return sum(x.astype(F32) for x in terms).astype(BF16)

    pair = [(1 - layer, layer)]
    far, near, after, mine = (
        add(pieces[k], lax.ppermute(pieces[k], "section", pair)) for k in (3, 1, 2, 0)
    )
    cores = (layer,)
    near = add(near, ring_hop(far, -1, cores))
    return add(mine, ring_hop(near, -1, cores), ring_hop(after, 1, cores))


def layer_forward(own, rows, x_own, pack, gains, ffn_weights, tab):
    core = lax.axis_index("section").reshape(1)
    normed, latent = latents(rows, gains["attn"], pack)
    part, *saved, latent_own = attend(
        core, latent, to_core(latent), tab, gains["q"], gains["kv"], pack
    )
    middle = x_own + RES_SCALE * scatter_tokens(part)
    ffn_rows = gather_dp(norm(middle, gains["ffn"]).astype(BF16))
    part, gu, hidden = ffn_forward(own, ffn_rows, ffn_weights)
    return part, (x_own, middle, ffn_rows, gu, hidden, normed, latent_own, saved)


def layer_out_rows(part, saved):
    return (saved[1] + RES_SCALE * scatter_dp(part)).astype(BF16)


def layer_backward(own, grad_own, d_rows, saved, pack, gains, ffn_weights, tab, after_gather):
    core = lax.axis_index("section")
    t = lax.axis_index("tensor")
    x_own, middle, ffn_rows, gu, hidden, normed, latent_own, saved = saved
    part, ffn_grads = ffn_backward(own, d_rows, ffn_rows, gu, hidden, ffn_weights)
    d_normed_two = scatter_dp(part)
    d_middle, ffn_gain = norm_back(middle, gains["ffn"], d_normed_two)
    d_middle = d_middle + grad_own
    d_attended = gather_tokens((RES_SCALE * d_middle).astype(BF16))
    d_attended, after_gather = lax.optimization_barrier((d_attended, after_gather))
    part, early = attend_back(d_attended, tab, saved, pack)
    d_latent = scatter_tokens(part)
    d_q, q_gain = norm_back(latent_own[:, :QR], gains["q"], d_latent[:, :QR])
    d_c, kv_gain = norm_back(latent_own[:, QR:], gains["kv"], d_latent[:, QR : QR + KVR])
    d_rope = d_latent[:, QR + KVR + NOPE : QR + KVR + NOPE + ROPE]
    blank = jnp.zeros((SHARD, HEAD), F32)
    d_first = jnp.concatenate([d_q[:, :512], blank], axis=1).astype(BF16)
    d_second = jnp.concatenate([d_q[:, 512:], d_c, d_rope, blank[:, ROPE:]], axis=1).astype(BF16)
    mine = jnp.where(core == 0, d_first, d_second)
    other = to_core(jnp.where(core == 0, d_second, d_first))
    both = jnp.concatenate([mine, other], axis=0)
    part = normed_back(both, pack)
    d_normed = part[:SHARD] + to_core(part[SHARD:])
    d_block, attn_gain = norm_back(x_own, gains["attn"], d_normed)
    d_block = (d_block + d_middle).astype(BF16)
    columns = both.reshape(2 * SHARD, LAT // HEAD, HEAD).transpose(1, 0, 2)

    def piece(by):
        tile = lax.dynamic_index_in_dim(columns, (t + by) % N_Z, 0, keepdims=False)
        return jnp.concatenate([tile, columns[N_Z]], axis=1)

    rows = jnp.stack([piece(0), z_hop(piece(3), -1), z_hop(piece(2), 2), z_hop(piece(1), 1)])
    rows = rows.reshape(N_Z, 2, SHARD, 2 * HEAD).transpose(1, 0, 2, 3).reshape(ROWS, 2 * HEAD)
    down_grad = dot_tn(normed, rows).astype(BF16).reshape(N_DP, SLICE, 2 * HEAD)
    return d_block, ffn_grads, early, down_grad, (attn_gain, ffn_gain, q_gain, kv_gain), after_gather


def scatter_sum(x):
    return jnp.sum(lax.all_to_all(x, "dp", 0, 0).astype(F32), axis=0)


def late_pack(down_grad, gains):
    attn, ffn, q, kv = (g.reshape(N_DP, -1) for g in gains)
    wide = ((0, 0), (0, 2 * HEAD - SLICE))
    row = jnp.concatenate([jnp.pad(attn, wide), jnp.pad(ffn, wide), q, kv], axis=1)
    row = jnp.pad(row, ((0, 0), (0, 16 * HEAD - row.shape[1]))).reshape(N_DP, 16, HEAD)
    row = jnp.pad(row, ((0, 0), (0, 0), (0, HEAD))).astype(BF16)
    return jnp.concatenate([down_grad, row], axis=1)


def body(
    layer_input,
    cotangent,
    seq_lengths,
    g_attn,
    w_qa,
    g_q,
    w_qb,
    w_kva,
    g_kv,
    w_kvb,
    w_o,
    g_ffn,
    w_gate,
    w_up,
    w_down,
):
    core = lax.axis_index("section")
    gains = jnp.stack(
        [
            jnp.pad(g, (0, A_COLS - LAT - g.shape[0]))
            for g in (g_attn[0], g_ffn[0], jnp.concatenate([g_q[0], g_kv[0]]))
        ]
    )
    gains = jnp.pad(gains, ((0, QR // N_DP - 3), (0, 0)))
    packs = attention_packs(w_qa[0], w_qb[0], w_kva[0], w_kvb[0], w_o[0], gains)
    keep = lax.dynamic_index_in_dim(packs, core, 0, keepdims=False)
    give = lax.dynamic_index_in_dim(packs, 1 - core, 0, keepdims=False)
    attn_one, attn_two = by_core(core, keep, to_core(give))
    attn_one = lax.all_gather(attn_one, "dp")
    attn_two = lax.all_gather(attn_two, "dp")

    blocks = lax.all_to_all(ffn_pack(w_gate[0], w_up[0], w_down[0]), "dp", 0, 0)
    tab = head_tables(seq_lengths)
    blocks, cotangent, layer_input = lax.optimization_barrier((blocks, cotangent, layer_input))
    mine = ring_pieces(blocks.reshape(D, MATS))
    ffn_weights = mine + [to_core(piece) for piece in mine]

    def token_rows(x):
        packs = x.reshape(2, N_Z, SHARD, D)
        first, second = by_core(core, packs[0], packs[1])
        return from_here(first).reshape(PACK, D), from_here(second).reshape(PACK, D)

    def d_mlp_rows(grad):
        return gather_dp((RES_SCALE * grad).astype(BF16))

    cot_own = token_rows(cotangent)[0][:SHARD].astype(F32)
    d_rows_two = d_mlp_rows(cot_own)
    attn_one, d_rows_two, tab = lax.optimization_barrier((attn_one, d_rows_two, tab))
    gains_one, gains_two = attention_gains(attn_one), attention_gains(attn_two)
    own_one = (core == 0).astype(jnp.int32).reshape(1)
    own_two = 1 - own_one

    rows = token_rows(layer_input)
    x_own = rows[0][:SHARD].astype(F32)
    part, saved_one = layer_forward(own_one, rows, x_own, attn_one, gains_one, ffn_weights, tab)
    out_one = layer_out_rows(part, saved_one)
    rows_one = gather_tokens(out_one)
    part_two, saved_two = layer_forward(
        own_two, rows_one, out_one.astype(F32), attn_two, gains_two, ffn_weights, tab
    )
    in_grad_two, ffn_grads_two, early_two, down_two, dg_two, part_two = layer_backward(
        own_two, cot_own, d_rows_two, saved_two, attn_two, gains_two, ffn_weights, tab, part_two
    )
    rows_two = gather_tokens(layer_out_rows(part_two, saved_two))
    early_two = lax.psum_scatter(
        early_two.reshape(N_DP * E_ROWS, WO), "dp", scatter_dimension=0, tiled=True
    )
    grad_one = in_grad_two.astype(F32)
    d_rows_one = d_mlp_rows(grad_one)
    d_rows_one, ffn_grads_two = lax.optimization_barrier((d_rows_one, ffn_grads_two))
    in_grad_one, ffn_grads_one, early_one, down_one, dg_one, _ = layer_backward(
        own_one, grad_one, d_rows_one, saved_one, attn_one, gains_one, ffn_weights, tab, ()
    )
    early_one = lax.psum_scatter(
        early_one.reshape(N_DP * E_ROWS, WO), "dp", scatter_dimension=0, tiled=True
    )

    totals = [ring_sum(0, ffn_grads_one), ring_sum(1, ffn_grads_two)]
    total = jnp.where(core == 0, totals[0], totals[1]).reshape(N_DP, SLICE, MATS)
    gate_grad, up_grad, down_grad = ffn_unpack(lax.all_to_all(total, "dp", 0, 0))

    late = jnp.concatenate([late_pack(down_one, dg_one), late_pack(down_two, dg_two)], axis=1)
    late = scatter_sum(late)
    tiles = from_zero(jnp.stack(gather_z(late[:, :HEAD].astype(BF16)))).astype(F32)
    late = late.reshape(2, SLICE + 16, 2 * HEAD)
    tiles = tiles.reshape(N_Z, 2, SLICE + 16, HEAD)
    sums = []
    for layer, early in enumerate((early_one, early_two)):
        lat = tiles[:, layer, :SLICE].transpose(1, 0, 2).reshape(SLICE, N_Z * HEAD)
        early = early.astype(F32)
        wide = jnp.concatenate([lat, late[layer, :SLICE, HEAD:], early[:SLICE]], axis=1)
        low = jnp.concatenate([early[SLICE:A_ROWS], early[A_ROWS:, : LAT - WO]], axis=1)
        sums.append((wide, low, jnp.sum(tiles[:, layer, SLICE:], axis=0)))
    home = []
    for one, two in zip(*sums):
        keep = jnp.where(core == 0, one, two)
        give = jnp.where(core == 0, two, one)
        home.append(by_core(core, keep, to_core(give)))
    (wide_low, wide_high), (low_low, low_high), (dg_low, dg_high) = home
    qa_grad = jnp.concatenate([wide_low[:, :512], wide_high[:, :256]], axis=1)
    kva_grad = wide_high[:, 256 : 256 + KVR + ROPE]
    at = LAT + WO - HEADS * VD
    wo_grad = jnp.concatenate([wide_low[:, at:], wide_high[:, at:]], axis=1).T
    qb_rows, kvb_rows = slice(0, QR // N_DP), slice(QR // N_DP, A_ROWS - SLICE)
    heads = jnp.concatenate([low_low[qb_rows], low_high[qb_rows]], axis=1)
    heads = heads.reshape(QR // N_DP, 2 * HEADS, HEAD)[:, :, : NOPE + ROPE]
    qb_grad = heads.reshape(QR // N_DP, 2 * HEADS * (NOPE + ROPE))
    kvb_grad = jnp.concatenate([low_low[kvb_rows], low_high[kvb_rows]], axis=1)
    gains = (dg_low + dg_high).reshape(-1)

    def gain_part(at, width):
        return gains[at : at + width][None]

    layer_out = in_order(*(jnp.where(core == 0, one, two) for one, two in zip(rows_one, rows_two)))[None]
    give = jnp.where(core == 0, in_grad_two, in_grad_one)
    mine = jnp.where(core == 0, in_grad_one, in_grad_two)
    both = jnp.concatenate([mine, to_core(give)], axis=1)
    both = jnp.concatenate(gather_z(both), axis=0)
    input_grad = in_order(both[:, :D], both[:, D:])[None]
    return (
        layer_out,
        input_grad,
        gain_part(0, SLICE),
        qa_grad[None],
        gain_part(4 * HEAD, QR // N_DP),
        qb_grad[None],
        kva_grad[None],
        gain_part(4 * HEAD + QR // N_DP, KVR // N_DP),
        kvb_grad[None],
        wo_grad[None],
        gain_part(2 * HEAD, SLICE),
        gate_grad[None],
        up_grad[None],
        down_grad[None],
    )


def solution(mesh):
    in_specs = (
        P("dp", None),
        P("dp", None),
        P("dp", None),
        P("section", "dp"),
        P("section", "dp", None),
        P("section", "dp"),
        P("section", "dp", "tensor"),
        P("section", "dp", None),
        P("section", "dp"),
        P("section", "dp", "tensor"),
        P("section", "tensor", "dp"),
        P("section", "dp"),
        P("section", "dp", "tensor"),
        P("section", "dp", "tensor"),
        P("section", "tensor", "dp"),
    )
    out_specs = (
        P("section", "dp", None),
        P("section", "dp", None),
        P("section", "dp"),
        P("section", "dp", None),
        P("section", "dp"),
        P("section", "dp", "tensor"),
        P("section", "dp", None),
        P("section", "dp"),
        P("section", "dp", "tensor"),
        P("section", "tensor", "dp"),
        P("section", "dp"),
        P("section", "dp", "tensor"),
        P("section", "dp", "tensor"),
        P("section", "tensor", "dp"),
    )
    return jax.shard_map(body, mesh=mesh, in_specs=in_specs, out_specs=out_specs, check_vma=False)
```

```python
import math

import jax
import jax.numpy as jnp
from jax import lax
from jax.experimental import pallas as pl
from jax.experimental.pallas import tpu as pltpu
from jax.sharding import PartitionSpec as P

D = 2560
NOPE = 64
ROPE = 32
VD = 64
QR = 768
KVR = 256
PACK = 64
MB = 2
N_DP = 16
N_Z = 4
HEADS = 5
SLICE = D // N_DP
FF_PART = 100
LANES = 128
SHARD = 16
RES_SCALE = 1.4 / math.sqrt(62.0)
EPSILON = 1e-05
SCORE_SCALE = (NOPE + ROPE) ** (-0.5)
BF16 = jnp.bfloat16
F32 = jnp.float32


def dot(a, b):
    return jnp.dot(a, b, preferred_element_type=F32)


def dot_tn(a, b):
    return lax.dot_general(a, b, (((0,), (0,)), ((), ())), preferred_element_type=F32)


def dot_nt(a, b):
    return lax.dot_general(a, b, (((1,), (1,)), ((), ())), preferred_element_type=F32)


def to_core(x):
    return lax.ppermute(x, "section", [(0, 1), (1, 0)])


def z_hop(x, by):
    return lax.ppermute(x, "tensor", [(i, (i + by) % N_Z) for i in range(N_Z)])


def by_core(core, mine, other):
    return jnp.where(core == 0, mine, other), jnp.where(core == 0, other, mine)


def from_here(x):
    return lax.dynamic_slice_in_dim(jnp.concatenate([x, x]), lax.axis_index("tensor"), N_Z, 0)


def from_zero(x):
    at = (N_Z - lax.axis_index("tensor")) % N_Z
    return lax.dynamic_slice_in_dim(jnp.concatenate([x, x]), at, N_Z, 0)


def gather_z(x):
    return [x, z_hop(x, -1), z_hop(x, 2), z_hop(x, 1)]


def gather_tokens(x):
    mine = jnp.concatenate(gather_z(x), axis=0)
    return mine, to_core(mine)


def in_order(mine, other):
    core = lax.axis_index("section")
    shape = (N_Z, SHARD, mine.shape[-1])
    mine, other = from_zero(mine.reshape(shape)), from_zero(other.reshape(shape))
    return jnp.concatenate(by_core(core, mine, other), axis=0).reshape(-1, shape[-1])


def scatter_tokens(part):
    half = part[:PACK].astype(F32) + to_core(part[PACK:]).astype(F32)
    sent = half.astype(BF16)
    total = half[:SHARD]
    for by in (2, 1, 3):
        total = total + z_hop(sent[SHARD * by : SHARD * (by + 1)], by).astype(F32)
    return total


def gather_dp(x):
    copies = jnp.broadcast_to(x[None], (N_DP,) + x.shape)
    return lax.all_to_all(copies, "dp", 0, 0).reshape(N_DP * x.shape[0], x.shape[1])


def scatter_dp(part):
    pieces = lax.all_to_all(part.reshape(N_DP, SHARD, D), "dp", 0, 0)
    return jnp.sum(pieces.astype(F32), axis=0)


def norm_scale(x):
    return lax.rsqrt(jnp.mean(x * x, axis=-1, keepdims=True) + EPSILON)


def norm(x, gain):
    return x * norm_scale(x) * gain


def norm_back(x, gain, d):
    q = norm_scale(x)
    along = jnp.mean(gain * d * x, axis=-1, keepdims=True)
    return q * gain * d - x * (q * q * q) * along, jnp.sum(d * x * q, axis=0)


MATS = 3 * LANES
TOKENS = N_DP * SHARD
FF_VMEM = 56 * 1024 * 1024
FF_SCRATCH = [pltpu.VMEM((N_Z, D, MATS), BF16), pltpu.SemaphoreType.DMA((N_Z,))]


def ffn_copies(own_ref, mine, other, w_ref, sems):
    copies = [pltpu.make_async_copy(mine[z], w_ref.at[z], sems.at[z]) for z in range(N_Z)]
    others = [pltpu.make_async_copy(other[z], w_ref.at[z], sems.at[z]) for z in range(N_Z)]

    @pl.when(own_ref[0] == 1)
    def _():
        for copy in copies:
            copy.start()

    @pl.when(own_ref[0] != 1)
    def _():
        for copy in others:
            copy.start()

    return copies


def down_pair(w_ref, z):
    return jnp.concatenate([w_ref[z, :, 2 * LANES :], w_ref[z + 1, :, 2 * LANES :]], axis=1)


def ffn_forward_kernel(own_ref, n_ref, *refs):
    mine, other = refs[:N_Z], refs[N_Z : 2 * N_Z]
    part_ref, gu_ref, hid_ref, w_ref, sems = refs[2 * N_Z :]
    copies = ffn_copies(own_ref, mine, other, w_ref, sems)
    for z in range(N_Z):
        copies[z].wait()
        gu = dot(n_ref[...], w_ref[z, :, : 2 * LANES])
        gu_ref[:, 2 * LANES * z : 2 * LANES * (z + 1)] = gu
        gate, up = gu[:, :LANES], gu[:, LANES:]
        hid_ref[:, LANES * z : LANES * (z + 1)] = (gate * jax.nn.sigmoid(gate) * up).astype(BF16)
    out = dot_nt(hid_ref[:, : 2 * LANES], down_pair(w_ref, 0))
    part_ref[...] = (out + dot_nt(hid_ref[:, 2 * LANES :], down_pair(w_ref, 2))).astype(BF16)


def ffn_specs(arrays):
    vmem = pl.BlockSpec(memory_space=pltpu.VMEM)
    smem = pl.BlockSpec(memory_space=pltpu.SMEM)
    return [smem] + [vmem] * arrays + [pl.BlockSpec(memory_space=pl.ANY)] * (2 * N_Z)


def ffn_forward(own, rows, weights):
    return pl.pallas_call(
        ffn_forward_kernel,
        out_shape=(
            jax.ShapeDtypeStruct((TOKENS, D), BF16),
            jax.ShapeDtypeStruct((TOKENS, 2 * LANES * N_Z), F32),
            jax.ShapeDtypeStruct((TOKENS, LANES * N_Z), BF16),
        ),
        in_specs=ffn_specs(1),
        out_specs=(pl.BlockSpec(memory_space=pltpu.VMEM),) * 3,
        scratch_shapes=FF_SCRATCH,
        compiler_params=pltpu.CompilerParams(vmem_limit_bytes=FF_VMEM),
        name="ffn_forward",
    )(own, rows, *weights)


HALF_ROWS = SLICE // 2


def ffn_backward_kernel(own_ref, dm_ref, gu_ref, *refs):
    mine, other = refs[:N_Z], refs[N_Z : 2 * N_Z]
    part_ref, dgu_ref, w_ref, sems = refs[2 * N_Z :]
    copies = ffn_copies(own_ref, mine, other, w_ref, sems)
    out = None
    for z in range(0, N_Z, 2):
        copies[z].wait()
        copies[z + 1].wait()
        d_hidden = dot(dm_ref[...], down_pair(w_ref, z))
        for k in range(2):
            columns = slice(2 * LANES * (z + k), 2 * LANES * (z + k) + LANES)
            more = slice(columns.stop, columns.stop + LANES)
            gate, up = gu_ref[:, columns], gu_ref[:, more]
            d_h = d_hidden[:, LANES * k : LANES * (k + 1)]
            s = jax.nn.sigmoid(gate)
            dgu_ref[:, columns] = (d_h * up * (s + gate * s * (1.0 - s))).astype(BF16)
            dgu_ref[:, more] = (d_h * (gate * s)).astype(BF16)
    for z in range(N_Z):
        term = dot_nt(dgu_ref[:, 2 * LANES * z : 2 * LANES * (z + 1)], w_ref[z, :, : 2 * LANES])
        out = term if z == 0 else out + term
    part_ref[...] = out.astype(BF16)


def ffn_backward(own, d_rows, gu, weights):
    return pl.pallas_call(
        ffn_backward_kernel,
        out_shape=(
            jax.ShapeDtypeStruct((TOKENS, D), BF16),
            jax.ShapeDtypeStruct((TOKENS, 2 * LANES * N_Z), BF16),
        ),
        in_specs=ffn_specs(2),
        out_specs=(pl.BlockSpec(memory_space=pltpu.VMEM),) * 2,
        scratch_shapes=FF_SCRATCH,
        compiler_params=pltpu.CompilerParams(vmem_limit_bytes=FF_VMEM),
        name="ffn_backward",
    )(own, d_rows, gu, *weights)


HALF_ROWS = SLICE // 2


def ffn_gradients_kernel(own_ref, dm_ref, n_ref, dgu_ref, hid_ref, *refs):
    outs, grad_ref, out_sems = refs[: 2 * N_Z], refs[2 * N_Z], refs[2 * N_Z + 1]
    core = own_ref[1]

    def store(z, columns, grad):
        grad_ref[z, :, :, :, columns] = grad.reshape(N_DP, 2, HALF_ROWS, grad.shape[1])

    def send(z, keep_at, give_at):
        return [
            pltpu.make_async_copy(grad_ref.at[z, :, core], outs[keep_at], out_sems.at[keep_at]),
            pltpu.make_async_copy(
                grad_ref.at[z, :, 1 - core], outs[N_Z + give_at], out_sems.at[N_Z + give_at]
            ),
        ]

    for z in (2, 0):
        hidden = hid_ref[:, LANES * z : LANES * (z + 2)]
        grad = dot_tn(dm_ref[...], hidden).astype(BF16)
        store(z, slice(2 * LANES, MATS), grad[:, :LANES])
        store(z + 1, slice(2 * LANES, MATS), grad[:, LANES:])
        for k in range(2):
            d_gu = dgu_ref[:, 2 * LANES * (z + k) : 2 * LANES * (z + k + 1)]
            store(z + k, slice(0, 2 * LANES), dot_tn(n_ref[...], d_gu).astype(BF16))
            if z + k in (0, N_Z - 1):
                for copy in send(z + k, z + k, z + k):
                    copy.start()
            else:
                for owner in (1, 0):
                    keep_at = z + k if owner == 1 else 3 - z - k

                    @pl.when(own_ref[0] == owner)
                    def _(at=z + k, keep_at=keep_at):
                        for copy in send(at, keep_at, 3 - keep_at):
                            copy.start()

    for z in range(N_Z):
        for copy in send(z, z, z):
            copy.wait()


def ffn_gradients(own, d_rows, rows, d_gu, hidden):
    vmem = pl.BlockSpec(memory_space=pltpu.VMEM)
    return pl.pallas_call(
        ffn_gradients_kernel,
        out_shape=tuple(jax.ShapeDtypeStruct((N_DP, HALF_ROWS, MATS), BF16) for _ in range(2 * N_Z)),
        in_specs=[pl.BlockSpec(memory_space=pltpu.SMEM)] + [vmem] * 4,
        out_specs=(pl.BlockSpec(memory_space=pl.ANY),) * (2 * N_Z),
        scratch_shapes=[
            pltpu.VMEM((N_Z, N_DP, 2, HALF_ROWS, MATS), BF16),
            pltpu.SemaphoreType.DMA((2 * N_Z,)),
        ],
        compiler_params=pltpu.CompilerParams(vmem_limit_bytes=FF_VMEM),
        cost_estimate=pl.CostEstimate(flops=2 * TOKENS * D * MATS * N_Z, bytes_accessed=1 << 24, transcendentals=0),
        name="ffn_gradients",
    )(own, d_rows, rows, d_gu, hidden)


FF = N_DP * FF_PART
WINDOW = 2 * LANES
FF_PADDED = (FF - FF_PART) // LANES * LANES + WINDOW


def ffn_pack_kernel(gate_ref, up_ref, down_ref, out_ref, wide_ref):
    wide_ref[0, :, :FF] = gate_ref[...].astype(F32)
    wide_ref[1, :, :FF] = up_ref[...].astype(F32)
    wide_ref[2, :, :FF] = down_ref[...].astype(F32)
    valid = lax.broadcasted_iota(jnp.int32, (SLICE, LANES), 1) < FF_PART
    for p in range(N_DP):
        at = FF_PART * p // LANES * LANES
        by = FF_PART * p - at
        for m in range(3):
            window = wide_ref[m, :, at : at + WINDOW]
            if by > 0:
                window = pltpu.roll(window, WINDOW - by, 1)
            block = jnp.where(valid, window[:, :LANES], 0.0)
            out_ref[p, :, LANES * m : LANES * (m + 1)] = block.astype(BF16)


def ffn_pack(w_gate, w_up, w_down):
    return pl.pallas_call(
        ffn_pack_kernel,
        out_shape=jax.ShapeDtypeStruct((N_DP, SLICE, MATS), BF16),
        scratch_shapes=[pltpu.VMEM((3, SLICE, FF_PADDED), F32)],
        compiler_params=pltpu.CompilerParams(vmem_limit_bytes=FF_VMEM),
        name="ffn_pack",
    )(w_gate, w_up, w_down)


def ffn_unpack_kernel(core_ref, one, one_got, two, two_got, gate_ref, up_ref, down_ref, wide_ref):
    first = core_ref[0] == 0
    wide_ref[...] = jnp.zeros(wide_ref.shape, F32)
    valid = lax.broadcasted_iota(jnp.int32, (HALF_ROWS, LANES), 1) < FF_PART
    for p in range(N_DP):
        at = FF_PART * p // LANES * LANES
        by = FF_PART * p - at
        for m in range(3):
            columns = slice(LANES * m, LANES * (m + 1))
            low = jnp.where(first, one[p, :, columns].astype(F32), two_got[p, :, columns].astype(F32))
            high = jnp.where(first, one_got[p, :, columns].astype(F32), two[p, :, columns].astype(F32))
            for half, block in enumerate((low, high)):
                block = jnp.where(valid, block, 0.0)
                window = jnp.concatenate([block, jnp.zeros_like(block)], axis=1)
                if by > 0:
                    window = pltpu.roll(window, by, 1)
                wide_ref[m, HALF_ROWS * half : HALF_ROWS * (half + 1), at : at + WINDOW] += window
    gate_ref[...] = wide_ref[0, :, :FF]
    up_ref[...] = wide_ref[1, :, :FF]
    down_ref[...] = wide_ref[2, :, :FF]


def ffn_unpack(core, *blocks):
    vmem = pl.BlockSpec(memory_space=pltpu.VMEM)
    return pl.pallas_call(
        ffn_unpack_kernel,
        out_shape=(
            jax.ShapeDtypeStruct((SLICE, FF), F32),
            jax.ShapeDtypeStruct((SLICE, FF), F32),
            jax.ShapeDtypeStruct((SLICE, FF), F32),
        ),
        in_specs=[pl.BlockSpec(memory_space=pltpu.SMEM)] + [vmem] * 4,
        out_specs=(vmem,) * 3,
        scratch_shapes=[pltpu.VMEM((3, SLICE, FF_PADDED), F32)],
        compiler_params=pltpu.CompilerParams(vmem_limit_bytes=FF_VMEM),
        name="ffn_unpack",
    )(core, *blocks)


A_ROWS = SLICE + QR // N_DP + KVR // N_DP
A_COLS = 896
LAT = 640
WO_AT = 512
WO = 384
HEAD = 128
ROWS = MB * PACK
QB_ROWS = slice(SLICE, SLICE + QR // N_DP)
KVB_ROWS = slice(SLICE + QR // N_DP, A_ROWS)
E_ROWS = 2 * A_ROWS - SLICE
ATT_VMEM = 48 * 1024 * 1024


def latent_kernel(mine_ref, other_ref, gain_ref, pack_ref, normed_ref, lat_ref, w_ref, sem):
    copy = pltpu.make_async_copy(pack_ref.at[:, 0:SLICE, 0:LAT], w_ref, sem)
    copy.start()
    normed_ref[:PACK] = norm(mine_ref[...].astype(F32), gain_ref[...]).astype(BF16)
    normed_ref[PACK:] = norm(other_ref[...].astype(F32), gain_ref[...]).astype(BF16)
    copy.wait()
    lat_ref[...] = dot(normed_ref[...], w_ref[...].reshape(D, LAT))


def latents(rows, gain, pack):
    vmem = pl.BlockSpec(memory_space=pltpu.VMEM)
    return pl.pallas_call(
        latent_kernel,
        out_shape=(
            jax.ShapeDtypeStruct((ROWS, D), BF16),
            jax.ShapeDtypeStruct((ROWS, LAT), F32),
        ),
        in_specs=[vmem, vmem, vmem, pl.BlockSpec(memory_space=pl.ANY)],
        out_specs=(vmem, vmem),
        scratch_shapes=[pltpu.VMEM((N_DP, SLICE, LAT), BF16), pltpu.SemaphoreType.DMA],
        compiler_params=pltpu.CompilerParams(vmem_limit_bytes=ATT_VMEM),
        name="latents",
    )(*rows, gain, pack)


def weight_copies(pack_ref, qb_ref, kvb_ref, wo_ref, sems):
    sources = (
        pack_ref.at[:, QB_ROWS, 0:LAT],
        pack_ref.at[:, KVB_ROWS, 0:LAT],
        pack_ref.at[:, 0:SLICE, WO_AT : WO_AT + WO],
    )
    targets = (qb_ref, kvb_ref, wo_ref)
    copies = [pltpu.make_async_copy(a, b, sems.at[i]) for i, (a, b) in enumerate(zip(sources, targets))]
    for copy in copies:
        copy.start()
    return copies


def weight_scratch():
    return [
        pltpu.VMEM((N_DP, QR // N_DP, LAT), BF16),
        pltpu.VMEM((N_DP, KVR // N_DP, LAT), BF16),
        pltpu.VMEM((N_DP, SLICE, WO), BF16),
        pltpu.SemaphoreType.DMA((3,)),
    ]


def lanes_of(x):
    return lax.broadcasted_iota(jnp.int32, x.shape, 1)


def turn(x, tab_ref):
    return (
        x * tab_ref[0]
        + pltpu.roll(x, HEAD - ROPE // 2, 1) * tab_ref[1]
        + pltpu.roll(x, ROPE // 2, 1) * tab_ref[2]
    )


def turn_back(x, tab_ref):
    return (
        x * tab_ref[0]
        - pltpu.roll(x, HEAD - ROPE // 2, 1) * tab_ref[1]
        - pltpu.roll(x, ROPE // 2, 1) * tab_ref[2]
    )


def head_columns(h):
    return slice(HEAD * h, HEAD * (h + 1))


def probs_of(query, key, tab_ref):
    scores = jnp.where(tab_ref[3] < 0.0, -1e30, dot_nt(query, key) * SCORE_SCALE)
    weight = jnp.exp(scores - jnp.max(scores, axis=-1, keepdims=True))
    return weight / jnp.sum(weight, axis=-1, keepdims=True)


def attend_kernel(
    core_ref, mine_ref, other_ref, tab_ref, gq_ref, gkv_ref, pack_ref,
    part_ref, sq_ref, comp_ref, q_ref, kv_ref, kr_ref, mixed_ref, lat_ref,
    qb_ref, kvb_ref, wo_ref, sems,
):
    copies = weight_copies(pack_ref, qb_ref, kvb_ref, wo_ref, sems)
    zero = core_ref[0] == 0
    other = jnp.concatenate([other_ref[PACK:], other_ref[:PACK]], axis=0)
    second = jnp.where(zero, other, mine_ref[...])
    first = jnp.where(zero, mine_ref[:, :512], other[:, :512])
    latent_q = jnp.concatenate([first, second[:, :256]], axis=1)
    lat_ref[:, :QR] = latent_q[:SHARD]
    lat_ref[:, QR:] = second[:SHARD, 256:512]
    sq_ref[...] = norm(latent_q, gq_ref[...]).astype(BF16)
    comp_ref[...] = norm(second[:, 256:512], gkv_ref[...]).astype(BF16)
    rope = pltpu.roll(second[:, 512:640], NOPE, 1)
    rope = jnp.where(lanes_of(rope) < NOPE, 0.0, turn(rope, tab_ref)).astype(BF16)
    kr_ref[...] = rope
    copies[0].wait()
    query = dot(sq_ref[...], qb_ref[...].reshape(QR, LAT))
    for h in range(HEADS):
        q_ref[:, head_columns(h)] = turn(query[:, head_columns(h)], tab_ref).astype(BF16)
    copies[1].wait()
    kv_ref[...] = dot(comp_ref[...], kvb_ref[...].reshape(KVR, LAT)).astype(BF16)
    heads = []
    for h in range(HEADS):
        kv = kv_ref[:, head_columns(h)]
        key = jnp.where(lanes_of(kv) < NOPE, kv, rope)
        probs = probs_of(q_ref[:, head_columns(h)], key, tab_ref)
        heads.append(dot(probs.astype(BF16), kv))
    low = lanes_of(heads[0]) < NOPE
    tiles = [jnp.where(low, 0.0, heads[0])]
    tiles += [jnp.where(low, pltpu.roll(heads[i], NOPE, 1), heads[i + 1]) for i in (1, 3)]
    mixed_ref[...] = jnp.concatenate(tiles, axis=1).astype(BF16)
    copies[2].wait()
    part_ref[...] = dot_nt(mixed_ref[...], wo_ref[...].reshape(D, WO)).astype(BF16)


def attend(core, mine, other, tab, g_q, g_kv, pack):
    vmem = pl.BlockSpec(memory_space=pltpu.VMEM)
    widths = (D, QR, KVR, LAT, LAT, HEAD, WO)
    return pl.pallas_call(
        attend_kernel,
        out_shape=tuple(jax.ShapeDtypeStruct((ROWS, w), BF16) for w in widths)
        + (jax.ShapeDtypeStruct((SHARD, QR + KVR), F32),),
        in_specs=[pl.BlockSpec(memory_space=pltpu.SMEM)] + [vmem] * 5 + [pl.BlockSpec(memory_space=pl.ANY)],
        out_specs=(vmem,) * (len(widths) + 1),
        scratch_shapes=weight_scratch(),
        compiler_params=pltpu.CompilerParams(vmem_limit_bytes=ATT_VMEM),
        name="attend",
    )(core, mine, other, tab, g_q, g_kv, pack)


def attend_back_kernel(
    mine_ref, other_ref, tab_hbm, q_hbm, kv_hbm, kr_hbm, pack_ref,
    part_ref, dq_ref, dkv_ref,
    tab_ref, q_ref, kv_ref, kr_ref, in_sems, qb_ref, kvb_ref, wo_ref, sems,
):
    pairs = ((kv_hbm, kv_ref), (kr_hbm, kr_ref), (q_hbm, q_ref), (tab_hbm, tab_ref))
    inputs = [pltpu.make_async_copy(a, b, in_sems.at[i]) for i, (a, b) in enumerate(pairs)]
    for copy in inputs:
        copy.start()
    copies = weight_copies(pack_ref, qb_ref, kvb_ref, wo_ref, sems)
    d_att = jnp.concatenate([mine_ref[...], other_ref[...]], axis=0)
    copies[2].wait()
    d_mixed = dot(d_att, wo_ref[...].reshape(D, WO))
    for copy in inputs:
        copy.wait()
    rope = kr_ref[...]
    d_rope = jnp.zeros((ROWS, HEAD), F32)
    for h in range(HEADS):
        kv = kv_ref[:, head_columns(h)]
        low = lanes_of(kv) < NOPE
        key = jnp.where(low, kv, rope)
        query = q_ref[:, head_columns(h)]
        probs = probs_of(query, key, tab_ref)
        tile = d_mixed[:, head_columns((h + 1) // 2)]
        if h % 2 == 1:
            tile = pltpu.roll(tile, NOPE, 1)
        tile = jnp.where(low, 0.0, tile).astype(BF16)
        d_probs = dot_nt(tile, kv)
        d_scores = probs * (d_probs - jnp.sum(probs * d_probs, axis=-1, keepdims=True))
        d_scores = d_scores.astype(BF16)
        d_query = dot(d_scores, key) * SCORE_SCALE
        d_key = dot_tn(d_scores, query) * SCORE_SCALE
        d_value = dot_tn(probs.astype(BF16), tile)
        dq_ref[:, head_columns(h)] = turn_back(d_query, tab_ref).astype(BF16)
        dkv_ref[:, head_columns(h)] = jnp.where(low, d_key, d_value).astype(BF16)
        d_rope = d_rope + d_key
    d_rope = jnp.where(lanes_of(d_rope) < NOPE, 0.0, turn_back(jnp.where(lanes_of(d_rope) < NOPE, 0.0, d_rope), tab_ref))
    copies[0].wait()
    copies[1].wait()
    part_ref[:, :QR] = dot_nt(dq_ref[...], qb_ref[...].reshape(QR, LAT)).astype(BF16)
    part_ref[:, QR : QR + KVR] = dot_nt(dkv_ref[...], kvb_ref[...].reshape(KVR, LAT)).astype(BF16)
    part_ref[:, QR + KVR :] = d_rope.astype(BF16)


def attend_back(d_attended, tab, saved, pack):
    vmem = pl.BlockSpec(memory_space=pltpu.VMEM)
    return pl.pallas_call(
        attend_back_kernel,
        out_shape=(
            jax.ShapeDtypeStruct((ROWS, QR + KVR + HEAD), BF16),
            jax.ShapeDtypeStruct((ROWS, LAT), BF16),
            jax.ShapeDtypeStruct((ROWS, LAT), BF16),
        ),
        in_specs=[vmem] * 2 + [pl.BlockSpec(memory_space=pl.ANY)] * 5,
        out_specs=(vmem,) * 3,
        scratch_shapes=[
            pltpu.VMEM((4, ROWS, HEAD), F32),
            pltpu.VMEM((ROWS, LAT), BF16),
            pltpu.VMEM((ROWS, LAT), BF16),
            pltpu.VMEM((ROWS, HEAD), BF16),
            pltpu.SemaphoreType.DMA((4,)),
        ]
        + weight_scratch(),
        compiler_params=pltpu.CompilerParams(vmem_limit_bytes=ATT_VMEM),
        name="attend_back",
    )(*d_attended, tab, *saved[2:5], pack)


def attend_gradients_kernel(
    mine_ref, other_ref, dq_ref, dkv_ref, sq_hbm, comp_hbm, mixed_hbm,
    early_ref,
    sq_ref, comp_ref, mixed_ref, sems,
):
    pairs = ((mixed_hbm, mixed_ref), (sq_hbm, sq_ref), (comp_hbm, comp_ref))
    copies = [pltpu.make_async_copy(a, b, sems.at[i]) for i, (a, b) in enumerate(pairs)]
    for copy in copies:
        copy.start()
    d_att = jnp.concatenate([mine_ref[...], other_ref[...]], axis=0)
    copies[0].wait()
    wo_grad = dot_tn(d_att, mixed_ref[...]).astype(BF16)
    early_ref[:, :SLICE, :] = wo_grad.reshape(N_DP, SLICE, WO)
    copies[1].wait()
    qb_grad = dot_tn(sq_ref[...], dq_ref[...]).astype(BF16).reshape(N_DP, QR // N_DP, LAT)
    copies[2].wait()
    kvb_grad = dot_tn(comp_ref[...], dkv_ref[...]).astype(BF16).reshape(N_DP, KVR // N_DP, LAT)
    early_ref[:, QB_ROWS, :] = qb_grad[:, :, :WO]
    early_ref[:, KVB_ROWS, :] = kvb_grad[:, :, :WO]
    more = slice(A_ROWS, A_ROWS + QR // N_DP)
    early_ref[:, more, : LAT - WO] = qb_grad[:, :, WO:]
    early_ref[:, more.stop : E_ROWS, : LAT - WO] = kvb_grad[:, :, WO:]
    early_ref[:, A_ROWS:E_ROWS, LAT - WO :] = jnp.zeros((N_DP, E_ROWS - A_ROWS, 2 * WO - LAT), BF16)
    if early_ref.shape[1] > E_ROWS:
        rest = early_ref.shape[1] - E_ROWS
        early_ref[:, E_ROWS:, 2 * HEAD :] = jnp.zeros((N_DP, rest, WO - 2 * HEAD), BF16)
        early_ref[:, E_ROWS:, : 2 * HEAD] = jnp.zeros((N_DP, rest, 2 * HEAD), BF16)


def attend_gradients(d_attended, saved, d_query, d_key_value, rows):
    vmem = pl.BlockSpec(memory_space=pltpu.VMEM)
    return pl.pallas_call(
        attend_gradients_kernel,
        out_shape=jax.ShapeDtypeStruct((N_DP, rows, WO), BF16),
        in_specs=[vmem] * 4 + [pl.BlockSpec(memory_space=pl.ANY)] * 3,
        out_specs=vmem,
        scratch_shapes=[
            pltpu.VMEM((ROWS, QR), BF16),
            pltpu.VMEM((ROWS, KVR), BF16),
            pltpu.VMEM((ROWS, WO), BF16),
            pltpu.SemaphoreType.DMA((3,)),
        ],
        compiler_params=pltpu.CompilerParams(vmem_limit_bytes=ATT_VMEM),
        name="attend_gradients",
    )(*d_attended, d_query, d_key_value, saved[0], saved[1], saved[5])


L_ROWS = SLICE + 16


def late_kernel(rows_ref, gains_ref, normed_hbm, *refs):
    packs = len(refs) == 6
    out_ref, late_ref, normed_ref, sem, out_sem = refs[1:] if packs else (refs[0], refs[0], *refs[1:], None)
    copy = pltpu.make_async_copy(normed_hbm, normed_ref, sem)
    copy.start()
    late_ref[:, SLICE:, :HEAD] = gains_ref[...]
    late_ref[:, SLICE:, HEAD:] = jnp.zeros(gains_ref.shape, BF16)
    copy.wait()
    grad = dot_tn(normed_ref[...], rows_ref[...]).astype(BF16)
    late_ref[:, :SLICE, :] = grad.reshape(N_DP, SLICE, 2 * HEAD)
    if packs:
        copy = pltpu.make_async_copy(late_ref, out_ref.at[:, E_ROWS:, : 2 * HEAD], out_sem)
        copy.start()
        copy.wait()


def late_pack(normed, rows, gains, packs=None):
    attn, q, kv, ffn = (g.reshape(N_DP, -1) for g in gains)
    wide = ((0, 0), (0, 2 * HEAD - SLICE))
    row = jnp.concatenate([jnp.pad(attn, wide), jnp.pad(ffn, wide), q, kv], axis=1)
    row = jnp.pad(row, ((0, 0), (0, 16 * HEAD - row.shape[1]))).reshape(N_DP, 16, HEAD).astype(BF16)
    vmem = pl.BlockSpec(memory_space=pltpu.VMEM)
    hbm = pl.BlockSpec(memory_space=pl.ANY)
    shape = (N_DP, L_ROWS, 2 * HEAD)
    scratch = [pltpu.VMEM((ROWS, D), BF16), pltpu.SemaphoreType.DMA]
    params = pltpu.CompilerParams(vmem_limit_bytes=ATT_VMEM)
    if packs is None:
        return pl.pallas_call(
            late_kernel,
            out_shape=jax.ShapeDtypeStruct(shape, BF16),
            in_specs=[vmem, vmem, hbm],
            out_specs=vmem,
            scratch_shapes=scratch,
            compiler_params=params,
            name="late",
        )(rows, row, normed)
    return pl.pallas_call(
        late_kernel,
        out_shape=jax.ShapeDtypeStruct(packs.shape, BF16),
        in_specs=[vmem, vmem, hbm, hbm],
        out_specs=hbm,
        scratch_shapes=[pltpu.VMEM(shape, BF16)] + scratch + [pltpu.SemaphoreType.DMA],
        input_output_aliases={3: 0},
        compiler_params=params,
        name="late_in_packs",
    )(rows, row, normed, packs)


def normed_back_kernel(d_ref, pack_ref, out_ref, w_ref, sem):
    copy = pltpu.make_async_copy(pack_ref.at[:, 0:SLICE, 0:LAT], w_ref, sem)
    copy.start()
    copy.wait()
    out_ref[...] = dot_nt(d_ref[...], w_ref[...].reshape(D, LAT))


def normed_back(d_latent, pack):
    vmem = pl.BlockSpec(memory_space=pltpu.VMEM)
    return pl.pallas_call(
        normed_back_kernel,
        out_shape=jax.ShapeDtypeStruct((d_latent.shape[0], D), F32),
        in_specs=[vmem, pl.BlockSpec(memory_space=pl.ANY)],
        out_specs=vmem,
        scratch_shapes=[pltpu.VMEM((N_DP, SLICE, LAT), BF16), pltpu.SemaphoreType.DMA],
        compiler_params=pltpu.CompilerParams(vmem_limit_bytes=ATT_VMEM),
        name="normed_back",
    )(d_latent, pack)


def home_kernel(
    core_ref, tiles_ref, tiles_got_ref, rope_ref, rope_got_ref, early_ref, early_got_ref,
    qa_ref, kva_ref, qb_ref, kvb_ref, wo_ref, gain_ref, heads_ref,
):
    first = core_ref[0] == 0

    def halves(keep, got):
        keep, got = keep.astype(F32), got.astype(F32)
        return jnp.where(first, keep, got), jnp.where(first, got, keep)

    wide = slice(0, SLICE)
    gains = jnp.zeros(gain_ref.shape, F32)
    for z in range(N_Z):
        low, high = halves(tiles_ref[z], tiles_got_ref[z])
        gains = gains + low[SLICE:] + high[SLICE:]
        qa_ref[:, HEAD * z : HEAD * (z + 1)] = low[wide]
        if z < 2:
            qa_ref[:, HEAD * (z + 4) : HEAD * (z + 5)] = high[wide]
        else:
            kva_ref[:, HEAD * (z - 2) : HEAD * (z - 1)] = high[wide]
    gain_ref[...] = gains
    _, high = halves(rope_ref[...], rope_got_ref[...])
    kva_ref[:, KVR:] = high[:, :ROPE]
    low, high = halves(early_ref[wide], early_got_ref[wide])
    at = WO - HEADS * VD
    wo_ref[...] = jnp.concatenate([low[:, at:], high[:, at:]], axis=1)
    heads_ref[...] = jnp.zeros(heads_ref.shape, F32)
    valid = lax.broadcasted_iota(jnp.int32, (QR // N_DP, HEAD), 1) < NOPE + ROPE
    more = A_ROWS - SLICE
    for j in range(HEADS):
        rows = QB_ROWS if j < 3 else slice(QB_ROWS.start + more, QB_ROWS.stop + more)
        columns = slice(HEAD * (j % 3), HEAD * (j % 3 + 1))
        for k, tile in enumerate(halves(early_ref[rows, columns], early_got_ref[rows, columns])):
            start = (NOPE + ROPE) * (HEADS * k + j)
            at = start // HEAD * HEAD
            tile = jnp.where(valid, tile, 0.0)
            window = jnp.concatenate([tile, jnp.zeros_like(tile)], axis=1)
            if start > at:
                window = pltpu.roll(window, start - at, 1)
            heads_ref[:, at : at + 2 * HEAD] += window
        rows = KVB_ROWS if j < 3 else slice(KVB_ROWS.start + more, KVB_ROWS.stop + more)
        for k, tile in enumerate(halves(early_ref[rows, columns], early_got_ref[rows, columns])):
            kvb_ref[:, HEAD * (HEADS * k + j) : HEAD * (HEADS * k + j + 1)] = tile
    qb_ref[...] = heads_ref[:, : 2 * HEADS * (NOPE + ROPE)]


def home(core, *pieces):
    vmem = pl.BlockSpec(memory_space=pltpu.VMEM)
    shapes = (
        (SLICE, QR),
        (SLICE, KVR + ROPE),
        (QR // N_DP, 2 * HEADS * (NOPE + ROPE)),
        (KVR // N_DP, 2 * LAT),
        (SLICE, 2 * HEADS * VD),
        (16, HEAD),
    )
    return pl.pallas_call(
        home_kernel,
        out_shape=tuple(jax.ShapeDtypeStruct(x, F32) for x in shapes),
        in_specs=[pl.BlockSpec(memory_space=pltpu.SMEM)] + [vmem] * len(pieces),
        out_specs=(vmem,) * len(shapes),
        scratch_shapes=[pltpu.VMEM((QR // N_DP, 1152), F32)],
        compiler_params=pltpu.CompilerParams(vmem_limit_bytes=ATT_VMEM),
        name="home",
    )(core, *pieces)


def attention_pack_kernel(
    core_ref, qa_ref, qb_ref, kva_ref, kvb_ref, wo_ref, ga_ref, gf_ref, gq_ref, gk_ref,
    keep_ref, give_ref, heads_ref,
):
    half = HEADS * VD
    first = core_ref[0] == 0

    def put(rows, columns, zero, one):
        keep_ref[rows, columns] = jnp.where(first, zero, one).astype(BF16)
        give_ref[rows, columns] = jnp.where(first, one, zero).astype(BF16)

    def blank(rows, columns):
        zero = jnp.zeros((rows.stop - rows.start, columns.stop - columns.start), BF16)
        keep_ref[rows, columns] = zero
        give_ref[rows, columns] = zero

    wide = slice(0, SLICE)
    qa = qa_ref[...].astype(F32)
    put(wide, slice(0, 256), qa[:, :256], qa[:, 512:])
    put(wide, slice(256, 512), qa[:, 256:512], kva_ref[:, :256].astype(F32))
    wo_t = wo_ref[...].astype(F32)
    tail = jnp.zeros((SLICE, WO), F32)
    rope = jnp.concatenate([kva_ref[:, 256:].astype(F32), jnp.zeros((SLICE, WO - ROPE), F32)], axis=1)
    low = jnp.concatenate([tail[:, : WO - half], wo_t[:, :half]], axis=1)
    high = jnp.concatenate([tail[:, : WO - half], wo_t[:, half:]], axis=1)
    put(wide, slice(WO_AT, A_COLS), low, high + rope)
    heads_ref[:, : 2 * HEADS * (NOPE + ROPE)] = qb_ref[...].astype(F32)
    rows = QB_ROWS.stop - QB_ROWS.start
    valid = lax.broadcasted_iota(jnp.int32, (rows, HEAD), 1) < NOPE + ROPE
    tiles = []
    for j in range(2 * HEADS):
        at = (NOPE + ROPE) * j // HEAD * HEAD
        by = (NOPE + ROPE) * j - at
        window = heads_ref[:, at : at + 2 * HEAD]
        if by > 0:
            window = pltpu.roll(window, 2 * HEAD - by, 1)
        tiles.append(jnp.where(valid, window[:, :HEAD], 0.0))
    for j in range(HEADS):
        put(QB_ROWS, slice(HEAD * j, HEAD * (j + 1)), tiles[j], tiles[HEADS + j])
    gain_rows = [jnp.concatenate([g[...].astype(F32), jnp.zeros((1, 256 - SLICE), F32)], axis=1) for g in (ga_ref, gf_ref)]
    last = [gq_ref[...].astype(F32), gk_ref[...].astype(F32), jnp.zeros((1, 256 - 64), F32)]
    gain_rows.append(jnp.concatenate(last, axis=1))
    gains = jnp.concatenate(gain_rows + [jnp.zeros((rows - 3, 256), F32)], axis=0)
    put(QB_ROWS, slice(LAT, A_COLS), gains, gains)
    kvb = kvb_ref[...].astype(F32)
    put(KVB_ROWS, slice(0, LAT), kvb[:, :LAT], kvb[:, LAT:])
    blank(KVB_ROWS, slice(LAT, A_COLS))


def attention_packs(core, *weights):
    vmem = pl.BlockSpec(memory_space=pltpu.VMEM)
    return pl.pallas_call(
        attention_pack_kernel,
        out_shape=(jax.ShapeDtypeStruct((A_ROWS, A_COLS), BF16),) * 2,
        in_specs=[pl.BlockSpec(memory_space=pltpu.SMEM)] + [vmem] * len(weights),
        out_specs=(vmem, vmem),
        scratch_shapes=[pltpu.VMEM((QR // N_DP, 1152), F32)],
        compiler_params=pltpu.CompilerParams(vmem_limit_bytes=ATT_VMEM),
        name="attention_pack",
    )(core, *weights)


def attention_gains(pack):
    gains = pack[:, SLICE : SLICE + 3, LAT:].astype(F32)
    return dict(
        attn=gains[:, 0, :SLICE].reshape(1, D),
        ffn=gains[:, 1, :SLICE].reshape(1, D),
        q=gains[:, 2, : QR // N_DP].reshape(1, QR),
        kv=gains[:, 2, QR // N_DP : QR // N_DP + KVR // N_DP].reshape(1, KVR),
    )


def head_tables(seq_lengths):
    core, t = lax.axis_index("section"), lax.axis_index("tensor")
    at = jnp.arange(ROWS, dtype=jnp.int32)
    pack = (core + at // PACK) % 2
    row = (t + at % PACK // SHARD) % N_Z * SHARD + at % SHARD
    lengths = jnp.where(pack[:, None] == 0, seq_lengths[:1], seq_lengths[1:])
    past_end = row[:, None] >= jnp.cumsum(lengths, axis=1)
    segment = jnp.sum(past_end.astype(jnp.int32), axis=1)
    position = (row - jnp.sum(jnp.where(past_end, lengths, 0), axis=1)).astype(F32)
    frequency = 10000.0 ** (-2.0 * jnp.arange(ROPE // 2, dtype=F32) / ROPE)
    angles = position[:, None] * frequency[None, :]
    cosine, sine = jnp.cos(angles), jnp.sin(angles)
    sequence = pack * PACK + segment
    allowed = (sequence[:, None] == sequence[None, :]) & (row[None, :] <= row[:, None])

    def tile(*pieces):
        x = jnp.concatenate(pieces, axis=1)
        return jnp.pad(x, ((0, 0), (0, HEAD - x.shape[1])))

    ones, none = jnp.ones((ROWS, NOPE), F32), jnp.zeros((ROWS, NOPE), F32)
    bias = jnp.where(allowed, 0.0, -1.0).astype(F32)
    return jnp.stack(
        [tile(ones, cosine, cosine), tile(none, -sine), tile(none, jnp.zeros_like(sine), sine), bias]
    )


def ring_hop(x, by):
    pairs = [
        (c * N_Z + t, c * N_Z + (t + (by if c == 0 else -by)) % N_Z) for c in range(2) for t in range(N_Z)
    ]
    return lax.ppermute(x, ("section", "tensor"), pairs)


def add(*terms):
    return sum(x.astype(F32) for x in terms).astype(BF16)


def ring_pairs(pieces):
    got = [to_core(x) for x in pieces[N_Z:]]
    return add(pieces[3], got[3]), add(pieces[2], got[2]), (pieces[1], got[1]), (pieces[0], got[0])


def ring_first(pairs):
    far, after, near, mine = pairs
    return ring_hop(far, -1), ring_hop(after, 1), near, mine


def ring_last(first):
    far, after, near, mine = first
    return add(*mine, after, ring_hop(add(*near, far), -1))


tie = lax.optimization_barrier


def attention_forward(rows, x_own, pack, gains, tab, other=()):
    core = lax.axis_index("section").reshape(1)
    normed, latent = latents(rows, gains["attn"], pack)
    latent, other = tie((latent, other))
    part, *saved, latent_own = attend(
        core, latent, to_core(latent), tab, gains["q"], gains["kv"], pack
    )
    middle = x_own + RES_SCALE * scatter_tokens(part)
    return middle, (normed, latent_own, saved), other


def layer_forward(own, x_own, middle, saved, gains, ffn_weights, far=None):
    ffn_rows = gather_dp(norm(middle, gains["ffn"]).astype(BF16))
    if far is not None:
        ffn_rows, far = tie((ffn_rows, far))
        ffn_weights = ffn_weights[:3] + [far] + ffn_weights[3:] + [to_core(far)]
    part, gu, hidden = ffn_forward(own, ffn_rows, ffn_weights)
    return part, (x_own, middle, ffn_rows, gu, hidden) + saved, ffn_weights


def layer_out_rows(part, saved):
    return (saved[1] + RES_SCALE * part).astype(BF16)


def middle_backward(grad_own, d_normed_two, saved, gains):
    d_middle, ffn_gain = norm_back(saved[1], gains["ffn"], d_normed_two)
    return d_middle + grad_own, ffn_gain


def attention_backward(part, d_middle, saved, pack, gains, also=()):
    core = lax.axis_index("section")
    t = lax.axis_index("tensor")
    x_own, _, _, _, _, _, latent_own, _ = saved
    d_latent, also = tie((scatter_tokens(part), also))
    d_q, q_gain = norm_back(latent_own[:, :QR], gains["q"], d_latent[:, :QR])
    d_c, kv_gain = norm_back(latent_own[:, QR:], gains["kv"], d_latent[:, QR : QR + KVR])
    d_rope = d_latent[:, QR + KVR + NOPE : QR + KVR + NOPE + ROPE]
    blank = jnp.zeros((SHARD, HEAD), F32)
    d_first = jnp.concatenate([d_q[:, :512], blank], axis=1).astype(BF16)
    d_second = jnp.concatenate([d_q[:, 512:], d_c, d_rope, blank[:, ROPE:]], axis=1).astype(BF16)
    mine = jnp.where(core == 0, d_first, d_second)
    other = to_core(jnp.where(core == 0, d_second, d_first))
    both = jnp.concatenate([mine, other], axis=0)
    part = normed_back(both, pack)
    d_normed = part[:SHARD] + to_core(part[SHARD:])
    d_block, attn_gain = norm_back(x_own, gains["attn"], d_normed)
    d_block = (d_block + d_middle).astype(BF16)
    columns = both.reshape(2 * SHARD, LAT // HEAD, HEAD).transpose(1, 0, 2)

    def piece(by):
        tile = lax.dynamic_index_in_dim(columns, (t + by) % N_Z, 0, keepdims=False)
        return jnp.concatenate([tile, columns[N_Z]], axis=1)

    rows = jnp.stack([piece(0), z_hop(piece(3), -1), z_hop(piece(2), 2), z_hop(piece(1), 1)])
    rows = rows.reshape(N_Z, 2, SHARD, 2 * HEAD).transpose(1, 0, 2, 3).reshape(ROWS, 2 * HEAD)
    return d_block, rows, (attn_gain, q_gain, kv_gain), also


def scatter_sum(x):
    return jnp.sum(lax.all_to_all(x, "dp", 0, 0).astype(F32), axis=0)


def body(
    layer_input,
    cotangent,
    seq_lengths,
    g_attn,
    w_qa,
    g_q,
    w_qb,
    w_kva,
    g_kv,
    w_kvb,
    w_o,
    g_ffn,
    w_gate,
    w_up,
    w_down,
):
    core = lax.axis_index("section")
    keep, give = attention_packs(
        core.reshape(1), w_qa[0], w_qb[0], w_kva[0], w_kvb[0], w_o[0].T, g_attn, g_ffn, g_q, g_kv
    )
    attn_one, attn_two = by_core(core, keep, to_core(give))
    attn_one = lax.all_gather(attn_one, "dp")
    attn_two = lax.all_gather(attn_two, "dp")

    blocks = lax.all_to_all(ffn_pack(w_gate[0], w_up[0], w_down[0].T), "dp", 0, 0)
    tab = head_tables(seq_lengths)
    blocks, cotangent, layer_input = lax.optimization_barrier((blocks, cotangent, layer_input))
    weights = blocks.reshape(D, MATS)
    near, after = ring_hop(weights, 1), ring_hop(weights, -1)

    def token_rows(x):
        packs = x.reshape(2, N_Z, SHARD, D)
        first, second = by_core(core, packs[0], packs[1])
        return from_here(first).reshape(PACK, D), from_here(second).reshape(PACK, D)

    def d_mlp_rows(grad):
        return gather_dp((RES_SCALE * grad).astype(BF16))

    def d_attended_rows(d_middle):
        return gather_tokens((RES_SCALE * d_middle).astype(BF16))

    cot_own = token_rows(cotangent)[0][:SHARD].astype(F32)
    attn_one, tab = tie((attn_one, tab))
    gains_one, gains_two = attention_gains(attn_one), attention_gains(attn_two)
    own_one = jnp.stack([(core == 0).astype(jnp.int32), core])
    own_two = jnp.stack([(core == 1).astype(jnp.int32), core])

    rows = token_rows(layer_input)
    x_own = rows[0][:SHARD].astype(F32)
    middle, saved, (near, after) = attention_forward(
        rows, x_own, attn_one, gains_one, tab, (near, after)
    )
    mine = [weights, near, after]
    ffn_weights = mine + [to_core(piece) for piece in mine]
    middle, near, cot_rows = tie((middle, near, (RES_SCALE * cot_own).astype(BF16)))
    d_rows_two = lax.all_gather(cot_rows, "dp").reshape(TOKENS, D)
    part, saved_one, ffn_weights = layer_forward(
        own_one, x_own, middle, saved, gains_one, ffn_weights, ring_hop(near, 1)
    )
    out_one = layer_out_rows(scatter_dp(part), saved_one)
    rows_one = gather_tokens(out_one)
    x_own = out_one.astype(F32)
    middle, saved, _ = attention_forward(rows_one, x_own, attn_two, gains_two, tab)
    part_two, saved_two, _ = layer_forward(own_two, x_own, middle, saved, gains_two, ffn_weights)

    ffn_rows, gu, hidden = saved_two[2:5]
    part, d_gu = ffn_backward(own_two, d_rows_two, gu, ffn_weights)
    grads_two = ffn_gradients(own_two, d_rows_two, ffn_rows, d_gu, hidden)
    d_normed_two = scatter_dp(part)
    ring_two = ring_pairs(grads_two)
    d_middle, ffn_gain_two = middle_backward(cot_own, d_normed_two, saved_two, gains_two)
    d_attended = d_attended_rows(d_middle)
    part, d_query, d_key_value = attend_back(d_attended, tab, saved_two[-1], attn_two)
    packs_two = attend_gradients(d_attended, saved_two[-1], d_query, d_key_value, E_ROWS + L_ROWS)
    in_grad_two, rows, dg_two, part_two = attention_backward(
        part, d_middle, saved_two, attn_two, gains_two, scatter_dp(part_two)
    )
    packs_two = late_pack(saved_two[5], rows, (*dg_two, ffn_gain_two), packs_two).reshape(-1, WO)
    in_grad_two, ring_two = tie((in_grad_two, ring_two))
    ring_two = ring_first(ring_two)

    grad_one = in_grad_two.astype(F32)
    d_rows, packs_two = tie((d_mlp_rows(grad_one), packs_two))
    packs_two = lax.psum_scatter(packs_two, "dp", scatter_dimension=0, tiled=True)
    ffn_rows, gu, hidden = saved_one[2:5]
    part, d_gu = ffn_backward(own_one, d_rows, gu, ffn_weights)
    grads_one = ffn_gradients(own_one, d_rows, ffn_rows, d_gu, hidden)
    d_normed_two = scatter_dp(part)
    total_two = ring_last(ring_two)
    d_normed_two, total_two = tie((d_normed_two, total_two))
    d_middle, ffn_gain_one = middle_backward(grad_one, d_normed_two, saved_one, gains_one)
    d_attended = d_attended_rows(d_middle)
    part, d_query, d_key_value = attend_back(d_attended, tab, saved_one[-1], attn_one)
    early_one = attend_gradients(d_attended, saved_one[-1], d_query, d_key_value, E_ROWS)
    part, early_one = tie((part, early_one))
    early_one = scatter_sum(early_one)
    home_two = lax.all_to_all(total_two, "dp", 0, 0)
    part, home_two = tie((part, home_two))
    in_grad_one, rows, dg_one, grads_one = attention_backward(
        part, d_middle, saved_one, attn_one, gains_one, grads_one
    )
    rows, pairs = tie((rows, ring_pairs(grads_one)))
    total_one = ring_last(ring_first(pairs))
    in_grad_one, dg_one, early_one, part_two, packs_two = tie(
        (in_grad_one, dg_one, early_one, part_two, packs_two)
    )
    rows_two = gather_tokens(layer_out_rows(part_two, saved_two))
    late_one = scatter_sum(late_pack(saved_one[5], rows, (*dg_one, ffn_gain_one)))

    total_one, late_one = tie((total_one, late_one))
    home_one = lax.all_to_all(total_one, "dp", 0, 0)
    got_one = lax.ppermute(home_one, "section", [(1, 0)])
    got_two = lax.ppermute(home_two, "section", [(0, 1)])
    gate_grad, up_grad, down_grad = ffn_unpack(core.reshape(1), home_one, got_one, home_two, got_two)

    packs_two = packs_two.astype(F32)
    early_two, late_two = packs_two[:E_ROWS], packs_two[E_ROWS:, : 2 * HEAD]

    def homeward(one, two):
        give = jnp.where(core == 0, two, one)
        return jnp.where(core == 0, one, two), to_core(give)

    tiles = jnp.concatenate([late_one[:, :HEAD], late_two[:, :HEAD]], axis=0).astype(BF16)
    tiles = from_zero(jnp.stack(gather_z(tiles))).reshape(N_Z, 2, SLICE + 16, HEAD)
    qa_grad, kva_grad, qb_grad, kvb_grad, wo_grad, gains = home(
        core.reshape(1),
        *homeward(tiles[:, 0], tiles[:, 1]),
        *homeward(late_one[:SLICE, HEAD:], late_two[:SLICE, HEAD:]),
        *homeward(early_one, early_two),
    )
    gains = gains.reshape(-1)

    def gain_part(at, width):
        return gains[at : at + width][None]

    layer_out = in_order(*(jnp.where(core == 0, one, two) for one, two in zip(rows_one, rows_two)))[None]
    give = jnp.where(core == 0, in_grad_two, in_grad_one)
    mine = jnp.where(core == 0, in_grad_one, in_grad_two)
    both = jnp.concatenate([mine, to_core(give)], axis=1)
    both = jnp.concatenate(gather_z(both), axis=0)
    input_grad = in_order(both[:, :D], both[:, D:])[None]
    return (
        layer_out,
        input_grad,
        gain_part(0, SLICE),
        qa_grad[None],
        gain_part(4 * HEAD, QR // N_DP),
        qb_grad[None],
        kva_grad[None],
        gain_part(4 * HEAD + QR // N_DP, KVR // N_DP),
        kvb_grad[None],
        wo_grad.T[None],
        gain_part(2 * HEAD, SLICE),
        gate_grad[None],
        up_grad[None],
        down_grad.T[None],
    )


def solution(mesh):
    in_specs = (
        P("dp", None),
        P("dp", None),
        P("dp", None),
        P("section", "dp"),
        P("section", "dp", None),
        P("section", "dp"),
        P("section", "dp", "tensor"),
        P("section", "dp", None),
        P("section", "dp"),
        P("section", "dp", "tensor"),
        P("section", "tensor", "dp"),
        P("section", "dp"),
        P("section", "dp", "tensor"),
        P("section", "dp", "tensor"),
        P("section", "tensor", "dp"),
    )
    out_specs = (
        P("section", "dp", None),
        P("section", "dp", None),
        P("section", "dp"),
        P("section", "dp", None),
        P("section", "dp"),
        P("section", "dp", "tensor"),
        P("section", "dp", None),
        P("section", "dp"),
        P("section", "dp", "tensor"),
        P("section", "tensor", "dp"),
        P("section", "dp"),
        P("section", "dp", "tensor"),
        P("section", "dp", "tensor"),
        P("section", "tensor", "dp"),
    )
    return jax.shard_map(body, mesh=mesh, in_specs=in_specs, out_specs=out_specs, check_vma=False)
```

```python
import math

import jax
import jax.numpy as jnp
from jax import lax
from jax.experimental import pallas as pl
from jax.experimental.pallas import tpu as pltpu
from jax.sharding import PartitionSpec as P

D = 2560
NOPE = 64
ROPE = 32
VD = 64
QR = 768
KVR = 256
PACK = 64
MB = 2
N_DP = 16
N_Z = 4
HEADS = 5
SLICE = D // N_DP
FF_PART = 100
LANES = 128
SHARD = 16
RES_SCALE = 1.4 / math.sqrt(62.0)
EPSILON = 1e-05
SCORE_SCALE = (NOPE + ROPE) ** (-0.5)
BF16 = jnp.bfloat16
F32 = jnp.float32


def dot(a, b):
    return jnp.dot(a, b, preferred_element_type=F32)


def dot_tn(a, b):
    return lax.dot_general(a, b, (((0,), (0,)), ((), ())), preferred_element_type=F32)


def dot_nt(a, b):
    return lax.dot_general(a, b, (((1,), (1,)), ((), ())), preferred_element_type=F32)


def to_core(x):
    return lax.ppermute(x, "section", [(0, 1), (1, 0)])


def z_hop(x, by):
    return lax.ppermute(x, "tensor", [(i, (i + by) % N_Z) for i in range(N_Z)])


def by_core(core, mine, other):
    return jnp.where(core == 0, mine, other), jnp.where(core == 0, other, mine)


def from_here(x):
    return lax.dynamic_slice_in_dim(jnp.concatenate([x, x]), lax.axis_index("tensor"), N_Z, 0)


def from_zero(x):
    at = (N_Z - lax.axis_index("tensor")) % N_Z
    return lax.dynamic_slice_in_dim(jnp.concatenate([x, x]), at, N_Z, 0)


def gather_z(x):
    return [x, z_hop(x, -1), z_hop(x, 2), z_hop(x, 1)]


def gather_tokens(x):
    mine = jnp.concatenate(gather_z(x), axis=0)
    return mine, to_core(mine)


def in_order(mine, other):
    core = lax.axis_index("section")
    shape = (N_Z, SHARD, mine.shape[-1])
    mine, other = from_zero(mine.reshape(shape)), from_zero(other.reshape(shape))
    return jnp.concatenate(by_core(core, mine, other), axis=0).reshape(-1, shape[-1])


def scatter_tokens(part):
    half = part[:PACK].astype(F32) + to_core(part[PACK:]).astype(F32)
    sent = half.astype(BF16)
    total = half[:SHARD]
    for by in (2, 1, 3):
        total = total + z_hop(sent[SHARD * by : SHARD * (by + 1)], by).astype(F32)
    return total


def gather_dp(x):
    copies = jnp.broadcast_to(x[None], (N_DP,) + x.shape)
    return lax.all_to_all(copies, "dp", 0, 0).reshape(N_DP * x.shape[0], x.shape[1])


def scatter_dp(part):
    pieces = lax.all_to_all(part.reshape(N_DP, SHARD, D), "dp", 0, 0)
    return jnp.sum(pieces.astype(F32), axis=0)


def norm_scale(x):
    return lax.rsqrt(jnp.mean(x * x, axis=-1, keepdims=True) + EPSILON)


def norm(x, gain):
    return x * norm_scale(x) * gain


def norm_back(x, gain, d):
    q = norm_scale(x)
    along = jnp.mean(gain * d * x, axis=-1, keepdims=True)
    return q * gain * d - x * (q * q * q) * along, jnp.sum(d * x * q, axis=0)


MATS = 3 * LANES
TOKENS = N_DP * SHARD
FF_VMEM = 56 * 1024 * 1024
FF_SCRATCH = [pltpu.VMEM((N_Z, D, MATS), BF16), pltpu.SemaphoreType.DMA((N_Z,))]


def ffn_copies(own_ref, mine, other, w_ref, sems):
    copies = [pltpu.make_async_copy(mine[z], w_ref.at[z], sems.at[z]) for z in range(N_Z)]
    others = [pltpu.make_async_copy(other[z], w_ref.at[z], sems.at[z]) for z in range(N_Z)]

    @pl.when(own_ref[0] == 1)
    def _():
        for copy in copies:
            copy.start()

    @pl.when(own_ref[0] != 1)
    def _():
        for copy in others:
            copy.start()

    return copies


def down_pair(w_ref, z):
    return jnp.concatenate([w_ref[z, :, 2 * LANES :], w_ref[z + 1, :, 2 * LANES :]], axis=1)


def ffn_forward_kernel(own_ref, n_ref, *refs):
    mine, other = refs[:N_Z], refs[N_Z : 2 * N_Z]
    part_ref, gu_ref, hid_ref, w_ref, sems = refs[2 * N_Z :]
    copies = ffn_copies(own_ref, mine, other, w_ref, sems)
    for z in range(N_Z):
        copies[z].wait()
        gu = dot(n_ref[...], w_ref[z, :, : 2 * LANES])
        gu_ref[:, 2 * LANES * z : 2 * LANES * (z + 1)] = gu
        gate, up = gu[:, :LANES], gu[:, LANES:]
        hid_ref[:, LANES * z : LANES * (z + 1)] = (gate * jax.nn.sigmoid(gate) * up).astype(BF16)
    out = dot_nt(hid_ref[:, : 2 * LANES], down_pair(w_ref, 0))
    part_ref[...] = (out + dot_nt(hid_ref[:, 2 * LANES :], down_pair(w_ref, 2))).astype(BF16)


def ffn_specs(arrays):
    vmem = pl.BlockSpec(memory_space=pltpu.VMEM)
    smem = pl.BlockSpec(memory_space=pltpu.SMEM)
    return [smem] + [vmem] * arrays + [pl.BlockSpec(memory_space=pl.ANY)] * (2 * N_Z)


def ffn_forward(own, rows, weights):
    return pl.pallas_call(
        ffn_forward_kernel,
        out_shape=(
            jax.ShapeDtypeStruct((TOKENS, D), BF16),
            jax.ShapeDtypeStruct((TOKENS, 2 * LANES * N_Z), F32),
            jax.ShapeDtypeStruct((TOKENS, LANES * N_Z), BF16),
        ),
        in_specs=ffn_specs(1),
        out_specs=(pl.BlockSpec(memory_space=pltpu.VMEM),) * 3,
        scratch_shapes=FF_SCRATCH,
        compiler_params=pltpu.CompilerParams(vmem_limit_bytes=FF_VMEM),
        name="ffn_forward",
    )(own, rows, *weights)


HALF_ROWS = SLICE // 2


def ffn_backward_kernel(own_ref, dm_ref, gu_ref, *refs):
    mine, other = refs[:N_Z], refs[N_Z : 2 * N_Z]
    part_ref, dgu_ref, w_ref, sems = refs[2 * N_Z :]
    copies = ffn_copies(own_ref, mine, other, w_ref, sems)
    out = None
    for z in range(0, N_Z, 2):
        copies[z].wait()
        copies[z + 1].wait()
        d_hidden = dot(dm_ref[...], down_pair(w_ref, z))
        for k in range(2):
            columns = slice(2 * LANES * (z + k), 2 * LANES * (z + k) + LANES)
            more = slice(columns.stop, columns.stop + LANES)
            gate, up = gu_ref[:, columns], gu_ref[:, more]
            d_h = d_hidden[:, LANES * k : LANES * (k + 1)]
            s = jax.nn.sigmoid(gate)
            dgu_ref[:, columns] = (d_h * up * (s + gate * s * (1.0 - s))).astype(BF16)
            dgu_ref[:, more] = (d_h * (gate * s)).astype(BF16)
    for z in range(N_Z):
        term = dot_nt(dgu_ref[:, 2 * LANES * z : 2 * LANES * (z + 1)], w_ref[z, :, : 2 * LANES])
        out = term if z == 0 else out + term
    part_ref[...] = out.astype(BF16)


def ffn_backward(own, d_rows, gu, weights):
    return pl.pallas_call(
        ffn_backward_kernel,
        out_shape=(
            jax.ShapeDtypeStruct((TOKENS, D), BF16),
            jax.ShapeDtypeStruct((TOKENS, 2 * LANES * N_Z), BF16),
        ),
        in_specs=ffn_specs(2),
        out_specs=(pl.BlockSpec(memory_space=pltpu.VMEM),) * 2,
        scratch_shapes=FF_SCRATCH,
        compiler_params=pltpu.CompilerParams(vmem_limit_bytes=FF_VMEM),
        name="ffn_backward",
    )(own, d_rows, gu, *weights)


HALF_ROWS = SLICE // 2


def ffn_gradients_kernel(own_ref, dm_ref, n_ref, dgu_ref, hid_ref, *refs):
    outs, grad_ref, out_sems = refs[: 2 * N_Z], refs[2 * N_Z], refs[2 * N_Z + 1]
    core = own_ref[1]

    def store(z, columns, grad):
        grad_ref[z, :, :, :, columns] = grad.reshape(N_DP, 2, HALF_ROWS, grad.shape[1])

    def send(z, keep_at, give_at):
        return [
            pltpu.make_async_copy(grad_ref.at[z, :, core], outs[keep_at], out_sems.at[keep_at]),
            pltpu.make_async_copy(
                grad_ref.at[z, :, 1 - core], outs[N_Z + give_at], out_sems.at[N_Z + give_at]
            ),
        ]

    for z in (2, 0):
        hidden = hid_ref[:, LANES * z : LANES * (z + 2)]
        grad = dot_tn(dm_ref[...], hidden).astype(BF16)
        store(z, slice(2 * LANES, MATS), grad[:, :LANES])
        store(z + 1, slice(2 * LANES, MATS), grad[:, LANES:])
        for k in range(2):
            d_gu = dgu_ref[:, 2 * LANES * (z + k) : 2 * LANES * (z + k + 1)]
            store(z + k, slice(0, 2 * LANES), dot_tn(n_ref[...], d_gu).astype(BF16))
            if z + k in (0, N_Z - 1):
                for copy in send(z + k, z + k, z + k):
                    copy.start()
            else:
                for owner in (1, 0):
                    keep_at = z + k if owner == 1 else 3 - z - k

                    @pl.when(own_ref[0] == owner)
                    def _(at=z + k, keep_at=keep_at):
                        for copy in send(at, keep_at, 3 - keep_at):
                            copy.start()

    for z in range(N_Z):
        for copy in send(z, z, z):
            copy.wait()


def ffn_gradients(own, d_rows, rows, d_gu, hidden):
    vmem = pl.BlockSpec(memory_space=pltpu.VMEM)
    return pl.pallas_call(
        ffn_gradients_kernel,
        out_shape=tuple(jax.ShapeDtypeStruct((N_DP, HALF_ROWS, MATS), BF16) for _ in range(2 * N_Z)),
        in_specs=[pl.BlockSpec(memory_space=pltpu.SMEM)] + [vmem] * 4,
        out_specs=(pl.BlockSpec(memory_space=pl.ANY),) * (2 * N_Z),
        scratch_shapes=[
            pltpu.VMEM((N_Z, N_DP, 2, HALF_ROWS, MATS), BF16),
            pltpu.SemaphoreType.DMA((2 * N_Z,)),
        ],
        compiler_params=pltpu.CompilerParams(vmem_limit_bytes=FF_VMEM),
        cost_estimate=pl.CostEstimate(flops=2 * TOKENS * D * MATS * N_Z, bytes_accessed=1 << 24, transcendentals=0),
        name="ffn_gradients",
    )(own, d_rows, rows, d_gu, hidden)


FF = N_DP * FF_PART
WINDOW = 2 * LANES
FF_PADDED = (FF - FF_PART) // LANES * LANES + WINDOW


def ffn_pack_kernel(gate_ref, up_ref, down_ref, out_ref, wide_ref):
    wide_ref[0, :, :FF] = gate_ref[...].astype(F32)
    wide_ref[1, :, :FF] = up_ref[...].astype(F32)
    wide_ref[2, :, :FF] = down_ref[...].astype(F32)
    valid = lax.broadcasted_iota(jnp.int32, (SLICE, LANES), 1) < FF_PART
    for p in range(N_DP):
        at = FF_PART * p // LANES * LANES
        by = FF_PART * p - at
        for m in range(3):
            window = wide_ref[m, :, at : at + WINDOW]
            if by > 0:
                window = pltpu.roll(window, WINDOW - by, 1)
            block = jnp.where(valid, window[:, :LANES], 0.0)
            out_ref[p, :, LANES * m : LANES * (m + 1)] = block.astype(BF16)


def ffn_pack(w_gate, w_up, w_down):
    return pl.pallas_call(
        ffn_pack_kernel,
        out_shape=jax.ShapeDtypeStruct((N_DP, SLICE, MATS), BF16),
        scratch_shapes=[pltpu.VMEM((3, SLICE, FF_PADDED), F32)],
        compiler_params=pltpu.CompilerParams(vmem_limit_bytes=FF_VMEM),
        name="ffn_pack",
    )(w_gate, w_up, w_down)


def ffn_unpack_kernel(core_ref, one, one_got, two, two_got, gate_ref, up_ref, down_ref, wide_ref):
    first = core_ref[0] == 0
    rows = slice(0, HALF_ROWS)
    wide_ref[...] = jnp.zeros(wide_ref.shape, F32)
    valid = lax.broadcasted_iota(jnp.int32, (HALF_ROWS, LANES), 1) < FF_PART
    for p in range(N_DP):
        at = FF_PART * p // LANES * LANES
        by = FF_PART * p - at
        for m in range(3):
            columns = slice(LANES * m, LANES * (m + 1))
            low = jnp.where(first, one[p, rows, columns].astype(F32), two_got[p, :, columns].astype(F32))
            high = jnp.where(first, one_got[p, rows, columns].astype(F32), two[p, :, columns].astype(F32))
            for half, block in enumerate((low, high)):
                block = jnp.where(valid, block, 0.0)
                window = jnp.concatenate([block, jnp.zeros_like(block)], axis=1)
                if by > 0:
                    window = pltpu.roll(window, by, 1)
                wide_ref[m, HALF_ROWS * half : HALF_ROWS * (half + 1), at : at + WINDOW] += window
    gate_ref[...] = wide_ref[0, :, :FF]
    up_ref[...] = wide_ref[1, :, :FF]
    down_ref[...] = wide_ref[2, :, :FF]


def ffn_unpack(core, *blocks):
    vmem = pl.BlockSpec(memory_space=pltpu.VMEM)
    return pl.pallas_call(
        ffn_unpack_kernel,
        out_shape=(
            jax.ShapeDtypeStruct((SLICE, FF), F32),
            jax.ShapeDtypeStruct((SLICE, FF), F32),
            jax.ShapeDtypeStruct((SLICE, FF), F32),
        ),
        in_specs=[pl.BlockSpec(memory_space=pltpu.SMEM)] + [vmem] * 4,
        out_specs=(vmem,) * 3,
        scratch_shapes=[pltpu.VMEM((3, SLICE, FF_PADDED), F32)],
        compiler_params=pltpu.CompilerParams(vmem_limit_bytes=FF_VMEM),
        name="ffn_unpack",
    )(core, *blocks)


A_ROWS = SLICE + QR // N_DP + KVR // N_DP
A_COLS = 896
LAT = 640
WO_AT = 512
WO = 384
HEAD = 128
ROWS = MB * PACK
QB_ROWS = slice(SLICE, SLICE + QR // N_DP)
KVB_ROWS = slice(SLICE + QR // N_DP, A_ROWS)
E_ROWS = 2 * A_ROWS - SLICE
ATT_VMEM = 48 * 1024 * 1024


def latent_kernel(mine_ref, other_ref, gain_ref, pack_ref, normed_ref, lat_ref, w_ref, sem):
    copy = pltpu.make_async_copy(pack_ref.at[:, 0:SLICE, 0:LAT], w_ref, sem)
    copy.start()
    normed_ref[:PACK] = norm(mine_ref[...].astype(F32), gain_ref[...]).astype(BF16)
    normed_ref[PACK:] = norm(other_ref[...].astype(F32), gain_ref[...]).astype(BF16)
    copy.wait()
    lat_ref[...] = dot(normed_ref[...], w_ref[...].reshape(D, LAT))


def latents(rows, gain, pack):
    vmem = pl.BlockSpec(memory_space=pltpu.VMEM)
    return pl.pallas_call(
        latent_kernel,
        out_shape=(
            jax.ShapeDtypeStruct((ROWS, D), BF16),
            jax.ShapeDtypeStruct((ROWS, LAT), F32),
        ),
        in_specs=[vmem, vmem, vmem, pl.BlockSpec(memory_space=pl.ANY)],
        out_specs=(vmem, vmem),
        scratch_shapes=[pltpu.VMEM((N_DP, SLICE, LAT), BF16), pltpu.SemaphoreType.DMA],
        compiler_params=pltpu.CompilerParams(vmem_limit_bytes=ATT_VMEM),
        name="latents",
    )(*rows, gain, pack)


def weight_copies(pack_ref, qb_ref, kvb_ref, wo_ref, sems):
    sources = (
        pack_ref.at[:, QB_ROWS, 0:LAT],
        pack_ref.at[:, KVB_ROWS, 0:LAT],
        pack_ref.at[:, 0:SLICE, WO_AT : WO_AT + WO],
    )
    targets = (qb_ref, kvb_ref, wo_ref)
    copies = [pltpu.make_async_copy(a, b, sems.at[i]) for i, (a, b) in enumerate(zip(sources, targets))]
    for copy in copies:
        copy.start()
    return copies


def weight_scratch():
    return [
        pltpu.VMEM((N_DP, QR // N_DP, LAT), BF16),
        pltpu.VMEM((N_DP, KVR // N_DP, LAT), BF16),
        pltpu.VMEM((N_DP, SLICE, WO), BF16),
        pltpu.SemaphoreType.DMA((3,)),
    ]


def lanes_of(x):
    return lax.broadcasted_iota(jnp.int32, x.shape, 1)


def turn(x, tab_ref):
    return (
        x * tab_ref[0]
        + pltpu.roll(x, HEAD - ROPE // 2, 1) * tab_ref[1]
        + pltpu.roll(x, ROPE // 2, 1) * tab_ref[2]
    )


def turn_back(x, tab_ref):
    return (
        x * tab_ref[0]
        - pltpu.roll(x, HEAD - ROPE // 2, 1) * tab_ref[1]
        - pltpu.roll(x, ROPE // 2, 1) * tab_ref[2]
    )


def head_columns(h):
    return slice(HEAD * h, HEAD * (h + 1))


def probs_of(query, key, tab_ref):
    scores = jnp.where(tab_ref[3] < 0.0, -1e30, dot_nt(query, key) * SCORE_SCALE)
    weight = jnp.exp(scores - jnp.max(scores, axis=-1, keepdims=True))
    return weight / jnp.sum(weight, axis=-1, keepdims=True)


def attend_kernel(
    core_ref, mine_ref, other_ref, tab_ref, gq_ref, gkv_ref, pack_ref,
    part_ref, sq_ref, comp_ref, q_ref, kv_ref, kr_ref, mixed_ref, lat_ref,
    qb_ref, kvb_ref, wo_ref, sems,
):
    copies = weight_copies(pack_ref, qb_ref, kvb_ref, wo_ref, sems)
    zero = core_ref[0] == 0
    other = jnp.concatenate([other_ref[PACK:], other_ref[:PACK]], axis=0)
    second = jnp.where(zero, other, mine_ref[...])
    first = jnp.where(zero, mine_ref[:, :512], other[:, :512])
    latent_q = jnp.concatenate([first, second[:, :256]], axis=1)
    lat_ref[:, :QR] = latent_q[:SHARD]
    lat_ref[:, QR:] = second[:SHARD, 256:512]
    sq_ref[...] = norm(latent_q, gq_ref[...]).astype(BF16)
    comp_ref[...] = norm(second[:, 256:512], gkv_ref[...]).astype(BF16)
    rope = pltpu.roll(second[:, 512:640], NOPE, 1)
    rope = jnp.where(lanes_of(rope) < NOPE, 0.0, turn(rope, tab_ref)).astype(BF16)
    kr_ref[...] = rope
    copies[0].wait()
    query = dot(sq_ref[...], qb_ref[...].reshape(QR, LAT))
    for h in range(HEADS):
        q_ref[:, head_columns(h)] = turn(query[:, head_columns(h)], tab_ref).astype(BF16)
    copies[1].wait()
    kv_ref[...] = dot(comp_ref[...], kvb_ref[...].reshape(KVR, LAT)).astype(BF16)
    heads = []
    for h in range(HEADS):
        kv = kv_ref[:, head_columns(h)]
        key = jnp.where(lanes_of(kv) < NOPE, kv, rope)
        probs = probs_of(q_ref[:, head_columns(h)], key, tab_ref)
        heads.append(dot(probs.astype(BF16), kv))
    low = lanes_of(heads[0]) < NOPE
    tiles = [jnp.where(low, 0.0, heads[0])]
    tiles += [jnp.where(low, pltpu.roll(heads[i], NOPE, 1), heads[i + 1]) for i in (1, 3)]
    mixed_ref[...] = jnp.concatenate(tiles, axis=1).astype(BF16)
    copies[2].wait()
    part_ref[...] = dot_nt(mixed_ref[...], wo_ref[...].reshape(D, WO)).astype(BF16)


def attend(core, mine, other, tab, g_q, g_kv, pack):
    vmem = pl.BlockSpec(memory_space=pltpu.VMEM)
    widths = (D, QR, KVR, LAT, LAT, HEAD, WO)
    return pl.pallas_call(
        attend_kernel,
        out_shape=tuple(jax.ShapeDtypeStruct((ROWS, w), BF16) for w in widths)
        + (jax.ShapeDtypeStruct((SHARD, QR + KVR), F32),),
        in_specs=[pl.BlockSpec(memory_space=pltpu.SMEM)] + [vmem] * 5 + [pl.BlockSpec(memory_space=pl.ANY)],
        out_specs=(vmem,) * (len(widths) + 1),
        scratch_shapes=weight_scratch(),
        compiler_params=pltpu.CompilerParams(vmem_limit_bytes=ATT_VMEM),
        name="attend",
    )(core, mine, other, tab, g_q, g_kv, pack)


def attend_back_kernel(
    mine_ref, other_ref, tab_hbm, q_hbm, kv_hbm, kr_hbm, pack_ref,
    part_ref, dq_ref, dkv_ref,
    tab_ref, q_ref, kv_ref, kr_ref, in_sems, qb_ref, kvb_ref, wo_ref, sems,
):
    pairs = ((kv_hbm, kv_ref), (kr_hbm, kr_ref), (q_hbm, q_ref), (tab_hbm, tab_ref))
    inputs = [pltpu.make_async_copy(a, b, in_sems.at[i]) for i, (a, b) in enumerate(pairs)]
    for copy in inputs:
        copy.start()
    copies = weight_copies(pack_ref, qb_ref, kvb_ref, wo_ref, sems)
    d_att = jnp.concatenate([mine_ref[...], other_ref[...]], axis=0)
    copies[2].wait()
    d_mixed = dot(d_att, wo_ref[...].reshape(D, WO))
    for copy in inputs:
        copy.wait()
    rope = kr_ref[...]
    d_rope = jnp.zeros((ROWS, HEAD), F32)
    for h in range(HEADS):
        kv = kv_ref[:, head_columns(h)]
        low = lanes_of(kv) < NOPE
        key = jnp.where(low, kv, rope)
        query = q_ref[:, head_columns(h)]
        probs = probs_of(query, key, tab_ref)
        tile = d_mixed[:, head_columns((h + 1) // 2)]
        if h % 2 == 1:
            tile = pltpu.roll(tile, NOPE, 1)
        tile = jnp.where(low, 0.0, tile).astype(BF16)
        d_probs = dot_nt(tile, kv)
        d_scores = probs * (d_probs - jnp.sum(probs * d_probs, axis=-1, keepdims=True))
        d_scores = d_scores.astype(BF16)
        d_query = dot(d_scores, key) * SCORE_SCALE
        d_key = dot_tn(d_scores, query) * SCORE_SCALE
        d_value = dot_tn(probs.astype(BF16), tile)
        dq_ref[:, head_columns(h)] = turn_back(d_query, tab_ref).astype(BF16)
        dkv_ref[:, head_columns(h)] = jnp.where(low, d_key, d_value).astype(BF16)
        d_rope = d_rope + d_key
    d_rope = jnp.where(lanes_of(d_rope) < NOPE, 0.0, turn_back(jnp.where(lanes_of(d_rope) < NOPE, 0.0, d_rope), tab_ref))
    copies[0].wait()
    copies[1].wait()
    part_ref[:, :QR] = dot_nt(dq_ref[...], qb_ref[...].reshape(QR, LAT)).astype(BF16)
    part_ref[:, QR : QR + KVR] = dot_nt(dkv_ref[...], kvb_ref[...].reshape(KVR, LAT)).astype(BF16)
    part_ref[:, QR + KVR :] = d_rope.astype(BF16)


def attend_back(d_attended, tab, saved, pack):
    vmem = pl.BlockSpec(memory_space=pltpu.VMEM)
    return pl.pallas_call(
        attend_back_kernel,
        out_shape=(
            jax.ShapeDtypeStruct((ROWS, QR + KVR + HEAD), BF16),
            jax.ShapeDtypeStruct((ROWS, LAT), BF16),
            jax.ShapeDtypeStruct((ROWS, LAT), BF16),
        ),
        in_specs=[vmem] * 2 + [pl.BlockSpec(memory_space=pl.ANY)] * 5,
        out_specs=(vmem,) * 3,
        scratch_shapes=[
            pltpu.VMEM((4, ROWS, HEAD), F32),
            pltpu.VMEM((ROWS, LAT), BF16),
            pltpu.VMEM((ROWS, LAT), BF16),
            pltpu.VMEM((ROWS, HEAD), BF16),
            pltpu.SemaphoreType.DMA((4,)),
        ]
        + weight_scratch(),
        compiler_params=pltpu.CompilerParams(vmem_limit_bytes=ATT_VMEM),
        name="attend_back",
    )(*d_attended, tab, *saved[2:5], pack)


def attend_gradients_kernel(
    mine_ref, other_ref, dq_ref, dkv_ref, sq_hbm, comp_hbm, mixed_hbm,
    out_ref,
    early_ref, sq_ref, comp_ref, mixed_ref, sems,
):
    pairs = ((mixed_hbm, mixed_ref), (sq_hbm, sq_ref), (comp_hbm, comp_ref))
    copies = [pltpu.make_async_copy(a, b, sems.at[i]) for i, (a, b) in enumerate(pairs)]
    for copy in copies:
        copy.start()
    d_att = jnp.concatenate([mine_ref[...], other_ref[...]], axis=0)
    copies[0].wait()
    wo_grad = dot_tn(d_att, mixed_ref[...]).astype(BF16)
    early_ref[:, :SLICE, :] = wo_grad.reshape(N_DP, SLICE, WO)
    copies[1].wait()
    qb_grad = dot_tn(sq_ref[...], dq_ref[...]).astype(BF16).reshape(N_DP, QR // N_DP, LAT)
    copies[2].wait()
    kvb_grad = dot_tn(comp_ref[...], dkv_ref[...]).astype(BF16).reshape(N_DP, KVR // N_DP, LAT)
    early_ref[:, QB_ROWS, :] = qb_grad[:, :, :WO]
    early_ref[:, KVB_ROWS, :] = kvb_grad[:, :, :WO]
    more = slice(A_ROWS, A_ROWS + QR // N_DP)
    early_ref[:, more, : LAT - WO] = qb_grad[:, :, WO:]
    early_ref[:, more.stop :, : LAT - WO] = kvb_grad[:, :, WO:]
    early_ref[:, A_ROWS:, LAT - WO :] = jnp.zeros((N_DP, E_ROWS - A_ROWS, 2 * WO - LAT), BF16)
    copy = pltpu.make_async_copy(early_ref, out_ref.at[:, :E_ROWS], sems.at[3])
    copy.start()
    copy.wait()


def attend_gradients(d_attended, saved, d_query, d_key_value):
    vmem = pl.BlockSpec(memory_space=pltpu.VMEM)
    hbm = pl.BlockSpec(memory_space=pl.ANY)
    return pl.pallas_call(
        attend_gradients_kernel,
        out_shape=jax.ShapeDtypeStruct((N_DP, E_ROWS + L_ROWS, WO), BF16),
        in_specs=[vmem] * 4 + [hbm] * 3,
        out_specs=hbm,
        scratch_shapes=[
            pltpu.VMEM((N_DP, E_ROWS, WO), BF16),
            pltpu.VMEM((ROWS, QR), BF16),
            pltpu.VMEM((ROWS, KVR), BF16),
            pltpu.VMEM((ROWS, WO), BF16),
            pltpu.SemaphoreType.DMA((4,)),
        ],
        compiler_params=pltpu.CompilerParams(vmem_limit_bytes=ATT_VMEM),
        name="attend_gradients",
    )(*d_attended, d_query, d_key_value, saved[0], saved[1], saved[5])


def low_gradients_kernel(
    dq_ref, dkv_ref, columns_ref, sq_hbm, comp_hbm, out_ref, sq_ref, comp_ref, sems
):
    copies = [
        pltpu.make_async_copy(sq_hbm, sq_ref, sems.at[0]),
        pltpu.make_async_copy(comp_hbm, comp_ref, sems.at[1]),
    ]
    for copy in copies:
        copy.start()
    copies[0].wait()
    grad = dot_tn(sq_ref[...], dq_ref[...]).astype(BF16)
    out_ref[:, : QR // N_DP, :] = grad.reshape(N_DP, QR // N_DP, LAT)
    copies[1].wait()
    grad = dot_tn(comp_ref[...], dkv_ref[...]).astype(BF16)
    out_ref[:, QR // N_DP : LOW_ROWS, :] = grad.reshape(N_DP, KVR // N_DP, LAT)
    out_ref[:, LOW_ROWS:, :SLICE] = columns_ref[...]
    out_ref[:, LOW_ROWS:, SLICE:] = jnp.zeros((N_DP, SHARD, LAT - SLICE), BF16)


LOW_ROWS = A_ROWS - SLICE


def low_gradients(saved, d_query, d_key_value, columns):
    vmem = pl.BlockSpec(memory_space=pltpu.VMEM)
    hbm = pl.BlockSpec(memory_space=pl.ANY)
    return pl.pallas_call(
        low_gradients_kernel,
        out_shape=jax.ShapeDtypeStruct((N_DP, LOW_ROWS + SHARD, LAT), BF16),
        in_specs=[vmem, vmem, vmem, hbm, hbm],
        out_specs=vmem,
        scratch_shapes=[
            pltpu.VMEM((ROWS, QR), BF16),
            pltpu.VMEM((ROWS, KVR), BF16),
            pltpu.SemaphoreType.DMA((2,)),
        ],
        compiler_params=pltpu.CompilerParams(vmem_limit_bytes=ATT_VMEM),
        name="low_gradients",
    )(d_query, d_key_value, columns, saved[0], saved[1])


def wo_gradient_kernel(mine_ref, other_ref, mixed_hbm, out_ref, mixed_ref, sem):
    copy = pltpu.make_async_copy(mixed_hbm, mixed_ref, sem)
    copy.start()
    copy.wait()
    total = None
    for i in range(2 * N_Z):
        d_ref = mine_ref if i < N_Z else other_ref
        d_att = d_ref[TOKENS * (i % N_Z) : TOKENS * (i % N_Z + 1)]
        mixed = mixed_ref[:, SHARD * i : SHARD * (i + 1), :].reshape(TOKENS, WO)
        term = dot_tn(d_att, mixed)
        total = term if total is None else total + term
    out_ref[...] = total


def wo_gradient(d_attended, mixed):
    vmem = pl.BlockSpec(memory_space=pltpu.VMEM)
    return pl.pallas_call(
        wo_gradient_kernel,
        out_shape=jax.ShapeDtypeStruct((SLICE, WO), F32),
        in_specs=[vmem, vmem, pl.BlockSpec(memory_space=pl.ANY)],
        out_specs=vmem,
        scratch_shapes=[pltpu.VMEM((N_DP, ROWS, WO), BF16), pltpu.SemaphoreType.DMA],
        compiler_params=pltpu.CompilerParams(vmem_limit_bytes=ATT_VMEM),
        name="wo_gradient",
    )(*d_attended, mixed)


LAT_ALL = QR + KVR + HEAD


def latent_gradient_kernel(rows_ref, normed_ref, out_ref):
    rows = rows_ref[...].reshape(TOKENS, LAT_ALL)
    out_ref[...] = dot_tn(normed_ref[...].reshape(TOKENS, SLICE), rows).astype(BF16)


def latent_gradient(rows, normed):
    return pl.pallas_call(
        latent_gradient_kernel,
        out_shape=jax.ShapeDtypeStruct((SLICE, LAT_ALL), BF16),
        compiler_params=pltpu.CompilerParams(vmem_limit_bytes=ATT_VMEM),
        name="latent_gradient",
    )(rows, normed)


L_ROWS = SLICE + 16


def late_kernel(rows_ref, gains_ref, normed_hbm, packs_ref, out_ref, late_ref, normed_ref, sem, out_sem):
    copy = pltpu.make_async_copy(normed_hbm, normed_ref, sem)
    copy.start()
    late_ref[:, SLICE:, :HEAD] = gains_ref[...]
    late_ref[:, SLICE:, HEAD : 2 * HEAD] = jnp.zeros(gains_ref.shape, BF16)
    late_ref[:, :, 2 * HEAD :] = jnp.zeros((N_DP, L_ROWS, WO - 2 * HEAD), BF16)
    copy.wait()
    grad = dot_tn(normed_ref[...], rows_ref[...]).astype(BF16)
    late_ref[:, :SLICE, : 2 * HEAD] = grad.reshape(N_DP, SLICE, 2 * HEAD)
    copy = pltpu.make_async_copy(late_ref, out_ref.at[:, E_ROWS:], out_sem)
    copy.start()
    copy.wait()


def late_pack(normed, rows, gains, packs):
    attn, q, kv, ffn = (g.reshape(N_DP, -1) for g in gains)
    wide = ((0, 0), (0, 2 * HEAD - SLICE))
    row = jnp.concatenate([jnp.pad(attn, wide), jnp.pad(ffn, wide), q, kv], axis=1)
    row = jnp.pad(row, ((0, 0), (0, 16 * HEAD - row.shape[1]))).reshape(N_DP, 16, HEAD).astype(BF16)
    vmem = pl.BlockSpec(memory_space=pltpu.VMEM)
    hbm = pl.BlockSpec(memory_space=pl.ANY)
    return pl.pallas_call(
        late_kernel,
        out_shape=jax.ShapeDtypeStruct(packs.shape, BF16),
        in_specs=[vmem, vmem, hbm, hbm],
        out_specs=hbm,
        scratch_shapes=[
            pltpu.VMEM((N_DP, L_ROWS, WO), BF16),
            pltpu.VMEM((ROWS, D), BF16),
            pltpu.SemaphoreType.DMA,
            pltpu.SemaphoreType.DMA,
        ],
        input_output_aliases={3: 0},
        compiler_params=pltpu.CompilerParams(vmem_limit_bytes=ATT_VMEM),
        name="late_in_packs",
    )(rows, row, normed, packs)


def normed_back_kernel(d_ref, pack_ref, out_ref, w_ref, sem):
    copy = pltpu.make_async_copy(pack_ref.at[:, 0:SLICE, 0:LAT], w_ref, sem)
    copy.start()
    copy.wait()
    out_ref[...] = dot_nt(d_ref[...], w_ref[...].reshape(D, LAT))


def normed_back(d_latent, pack):
    vmem = pl.BlockSpec(memory_space=pltpu.VMEM)
    return pl.pallas_call(
        normed_back_kernel,
        out_shape=jax.ShapeDtypeStruct((d_latent.shape[0], D), F32),
        in_specs=[vmem, pl.BlockSpec(memory_space=pl.ANY)],
        out_specs=vmem,
        scratch_shapes=[pltpu.VMEM((N_DP, SLICE, LAT), BF16), pltpu.SemaphoreType.DMA],
        compiler_params=pltpu.CompilerParams(vmem_limit_bytes=ATT_VMEM),
        name="normed_back",
    )(d_latent, pack)


def home_kernel(
    core_ref, lat_ref, wo1_ref, wo1_got_ref, low_ref, low_got_ref,
    tiles_ref, tiles_got_ref, packs_ref, packs_got_ref,
    qa_ref, kva_ref, qb_ref, kvb_ref, wo_ref, gain_ref, heads_ref,
):
    first = core_ref[0] == 0

    def pick(one, two):
        return jnp.where(first, one.astype(F32), two.astype(F32))

    wide = slice(0, SLICE)
    gains = jnp.zeros(gain_ref.shape, F32)
    for z in range(N_Z):
        low, high = tiles_got_ref[z], tiles_ref[z]
        gains = gains + low[SLICE:].astype(F32) + high[SLICE:].astype(F32)
        columns = slice(HEAD * z, HEAD * (z + 1))
        qa_ref[:, columns] = pick(lat_ref[wide, columns], low[wide])
        columns = slice(HEAD * (z + 4), HEAD * (z + 5))
        both = pick(lat_ref[wide, columns], high[wide])
        if z < 2:
            qa_ref[:, columns] = both
        else:
            kva_ref[:, HEAD * (z - 2) : HEAD * (z - 1)] = both
    gain_ref[...] = gains
    rope = pick(lat_ref[wide, QR + KVR :], packs_ref[E_ROWS : E_ROWS + SLICE, HEAD : 2 * HEAD])
    kva_ref[:, KVR:] = rope[:, :ROPE]
    at = WO - HEADS * VD
    low, high = pick(wo1_ref[...], packs_got_ref[wide]), pick(wo1_got_ref[...], packs_ref[wide])
    wo_ref[...] = jnp.concatenate([low[:, at:], high[:, at:]], axis=1)
    heads_ref[...] = jnp.zeros(heads_ref.shape, F32)
    qb_rows, kvb_rows = slice(0, QR // N_DP), slice(QR // N_DP, A_ROWS - SLICE)
    valid = lax.broadcasted_iota(jnp.int32, (QR // N_DP, HEAD), 1) < NOPE + ROPE
    for j in range(HEADS):
        start = SLICE if j < 3 else A_ROWS
        columns, packed = slice(HEAD * j, HEAD * (j + 1)), slice(HEAD * (j % 3), HEAD * (j % 3 + 1))
        for rows in (qb_rows, kvb_rows):
            at_rows = slice(start + rows.start, start + rows.stop)
            low = pick(low_ref[rows, columns], packs_got_ref[at_rows, packed])
            high = pick(low_got_ref[rows, columns], packs_ref[at_rows, packed])
            for k, tile in enumerate((low, high)):
                if rows == kvb_rows:
                    kvb_ref[:, HEAD * (HEADS * k + j) : HEAD * (HEADS * k + j + 1)] = tile
                    continue
                begin = (NOPE + ROPE) * (HEADS * k + j)
                at = begin // HEAD * HEAD
                tile = jnp.where(valid, tile, 0.0)
                window = jnp.concatenate([tile, jnp.zeros_like(tile)], axis=1)
                if begin > at:
                    window = pltpu.roll(window, begin - at, 1)
                heads_ref[:, at : at + 2 * HEAD] += window
    qb_ref[...] = heads_ref[:, : 2 * HEADS * (NOPE + ROPE)]


def home(core, *pieces):
    vmem = pl.BlockSpec(memory_space=pltpu.VMEM)
    shapes = (
        (SLICE, QR),
        (SLICE, KVR + ROPE),
        (QR // N_DP, 2 * HEADS * (NOPE + ROPE)),
        (KVR // N_DP, 2 * LAT),
        (SLICE, 2 * HEADS * VD),
        (16, HEAD),
    )
    return pl.pallas_call(
        home_kernel,
        out_shape=tuple(jax.ShapeDtypeStruct(x, F32) for x in shapes),
        in_specs=[pl.BlockSpec(memory_space=pltpu.SMEM)] + [vmem] * len(pieces),
        out_specs=(vmem,) * len(shapes),
        scratch_shapes=[pltpu.VMEM((QR // N_DP, 1152), F32)],
        compiler_params=pltpu.CompilerParams(vmem_limit_bytes=ATT_VMEM),
        name="home",
    )(core, *pieces)


def attention_pack_kernel(
    core_ref, qa_ref, qb_ref, kva_ref, kvb_ref, wo_ref, ga_ref, gf_ref, gq_ref, gk_ref,
    keep_ref, give_ref, heads_ref,
):
    half = HEADS * VD
    first = core_ref[0] == 0

    def put(rows, columns, zero, one):
        keep_ref[rows, columns] = jnp.where(first, zero, one).astype(BF16)
        give_ref[rows, columns] = jnp.where(first, one, zero).astype(BF16)

    def blank(rows, columns):
        zero = jnp.zeros((rows.stop - rows.start, columns.stop - columns.start), BF16)
        keep_ref[rows, columns] = zero
        give_ref[rows, columns] = zero

    wide = slice(0, SLICE)
    qa = qa_ref[...].astype(F32)
    put(wide, slice(0, 256), qa[:, :256], qa[:, 512:])
    put(wide, slice(256, 512), qa[:, 256:512], kva_ref[:, :256].astype(F32))
    wo_t = wo_ref[...].astype(F32)
    tail = jnp.zeros((SLICE, WO), F32)
    rope = jnp.concatenate([kva_ref[:, 256:].astype(F32), jnp.zeros((SLICE, WO - ROPE), F32)], axis=1)
    low = jnp.concatenate([tail[:, : WO - half], wo_t[:, :half]], axis=1)
    high = jnp.concatenate([tail[:, : WO - half], wo_t[:, half:]], axis=1)
    put(wide, slice(WO_AT, A_COLS), low, high + rope)
    heads_ref[:, : 2 * HEADS * (NOPE + ROPE)] = qb_ref[...].astype(F32)
    rows = QB_ROWS.stop - QB_ROWS.start
    valid = lax.broadcasted_iota(jnp.int32, (rows, HEAD), 1) < NOPE + ROPE
    tiles = []
    for j in range(2 * HEADS):
        at = (NOPE + ROPE) * j // HEAD * HEAD
        by = (NOPE + ROPE) * j - at
        window = heads_ref[:, at : at + 2 * HEAD]
        if by > 0:
            window = pltpu.roll(window, 2 * HEAD - by, 1)
        tiles.append(jnp.where(valid, window[:, :HEAD], 0.0))
    for j in range(HEADS):
        put(QB_ROWS, slice(HEAD * j, HEAD * (j + 1)), tiles[j], tiles[HEADS + j])
    gain_rows = [jnp.concatenate([g[...].astype(F32), jnp.zeros((1, 256 - SLICE), F32)], axis=1) for g in (ga_ref, gf_ref)]
    last = [gq_ref[...].astype(F32), gk_ref[...].astype(F32), jnp.zeros((1, 256 - 64), F32)]
    gain_rows.append(jnp.concatenate(last, axis=1))
    gains = jnp.concatenate(gain_rows + [jnp.zeros((rows - 3, 256), F32)], axis=0)
    put(QB_ROWS, slice(LAT, A_COLS), gains, gains)
    kvb = kvb_ref[...].astype(F32)
    put(KVB_ROWS, slice(0, LAT), kvb[:, :LAT], kvb[:, LAT:])
    blank(KVB_ROWS, slice(LAT, A_COLS))


def attention_packs(core, *weights):
    vmem = pl.BlockSpec(memory_space=pltpu.VMEM)
    return pl.pallas_call(
        attention_pack_kernel,
        out_shape=(jax.ShapeDtypeStruct((A_ROWS, A_COLS), BF16),) * 2,
        in_specs=[pl.BlockSpec(memory_space=pltpu.SMEM)] + [vmem] * len(weights),
        out_specs=(vmem, vmem),
        scratch_shapes=[pltpu.VMEM((QR // N_DP, 1152), F32)],
        compiler_params=pltpu.CompilerParams(vmem_limit_bytes=ATT_VMEM),
        name="attention_pack",
    )(core, *weights)


def attention_gains(pack):
    gains = pack[:, SLICE : SLICE + 3, LAT:].astype(F32)
    return dict(
        attn=gains[:, 0, :SLICE].reshape(1, D),
        ffn=gains[:, 1, :SLICE].reshape(1, D),
        q=gains[:, 2, : QR // N_DP].reshape(1, QR),
        kv=gains[:, 2, QR // N_DP : QR // N_DP + KVR // N_DP].reshape(1, KVR),
    )


def head_tables(seq_lengths):
    core, t = lax.axis_index("section"), lax.axis_index("tensor")
    at = jnp.arange(ROWS, dtype=jnp.int32)
    pack = (core + at // PACK) % 2
    row = (t + at % PACK // SHARD) % N_Z * SHARD + at % SHARD
    lengths = jnp.where(pack[:, None] == 0, seq_lengths[:1], seq_lengths[1:])
    past_end = row[:, None] >= jnp.cumsum(lengths, axis=1)
    segment = jnp.sum(past_end.astype(jnp.int32), axis=1)
    position = (row - jnp.sum(jnp.where(past_end, lengths, 0), axis=1)).astype(F32)
    frequency = 10000.0 ** (-2.0 * jnp.arange(ROPE // 2, dtype=F32) / ROPE)
    angles = position[:, None] * frequency[None, :]
    cosine, sine = jnp.cos(angles), jnp.sin(angles)
    sequence = pack * PACK + segment
    allowed = (sequence[:, None] == sequence[None, :]) & (row[None, :] <= row[:, None])

    def tile(*pieces):
        x = jnp.concatenate(pieces, axis=1)
        return jnp.pad(x, ((0, 0), (0, HEAD - x.shape[1])))

    ones, none = jnp.ones((ROWS, NOPE), F32), jnp.zeros((ROWS, NOPE), F32)
    bias = jnp.where(allowed, 0.0, -1.0).astype(F32)
    return jnp.stack(
        [tile(ones, cosine, cosine), tile(none, -sine), tile(none, jnp.zeros_like(sine), sine), bias]
    )


def ring_hop(x, by):
    pairs = [
        (c * N_Z + t, c * N_Z + (t + (by if c == 0 else -by)) % N_Z) for c in range(2) for t in range(N_Z)
    ]
    return lax.ppermute(x, ("section", "tensor"), pairs)


def add(*terms):
    return sum(x.astype(F32) for x in terms).astype(BF16)


def ring_pairs(pieces):
    got = [to_core(x) for x in pieces[N_Z:]]
    return add(pieces[3], got[3]), add(pieces[2], got[2]), (pieces[1], got[1]), (pieces[0], got[0])


def ring_first(pairs):
    far, after, near, mine = pairs
    return ring_hop(far, -1), ring_hop(after, 1), near, mine


def ring_last(first):
    far, after, near, mine = first
    return add(*mine, after, ring_hop(add(*near, far), -1))


tie = lax.optimization_barrier


def attention_forward(normed, latent, x_own, pack, gains, tab):
    core = lax.axis_index("section").reshape(1)
    part, *saved, latent_own = attend(
        core, latent, to_core(latent), tab, gains["q"], gains["kv"], pack
    )
    middle = x_own + RES_SCALE * scatter_tokens(part)
    return middle, (normed, latent_own, saved)


def layer_forward(own, x_own, middle, saved, gains, ffn_weights, far=None):
    ffn_rows = gather_dp(norm(middle, gains["ffn"]).astype(BF16))
    if far is not None:
        ffn_rows, far = tie((ffn_rows, far))
        ffn_weights = ffn_weights[:3] + [far] + ffn_weights[3:] + [to_core(far)]
    part, gu, hidden = ffn_forward(own, ffn_rows, ffn_weights)
    return part, (x_own, middle, ffn_rows, gu, hidden) + saved, ffn_weights


def layer_out_rows(part, saved):
    return (saved[1] + RES_SCALE * part).astype(BF16)


def middle_backward(grad_own, d_normed_two, saved, gains):
    d_middle, ffn_gain = norm_back(saved[1], gains["ffn"], d_normed_two)
    return d_middle + grad_own, ffn_gain


def attention_backward(part, d_middle, saved, pack, gains, also=()):
    core = lax.axis_index("section")
    t = lax.axis_index("tensor")
    x_own, _, _, _, _, _, latent_own, _ = saved
    d_latent, also = tie((scatter_tokens(part), also))
    d_q, q_gain = norm_back(latent_own[:, :QR], gains["q"], d_latent[:, :QR])
    d_c, kv_gain = norm_back(latent_own[:, QR:], gains["kv"], d_latent[:, QR : QR + KVR])
    d_rope = d_latent[:, QR + KVR + NOPE : QR + KVR + NOPE + ROPE]
    blank = jnp.zeros((SHARD, HEAD), F32)
    d_first = jnp.concatenate([d_q[:, :512], blank], axis=1).astype(BF16)
    d_second = jnp.concatenate([d_q[:, 512:], d_c, d_rope, blank[:, ROPE:]], axis=1).astype(BF16)
    mine = jnp.where(core == 0, d_first, d_second)
    other = to_core(jnp.where(core == 0, d_second, d_first))
    both = jnp.concatenate([mine, other], axis=0)
    part = normed_back(both, pack)
    d_normed = part[:SHARD] + to_core(part[SHARD:])
    d_block, attn_gain = norm_back(x_own, gains["attn"], d_normed)
    d_block = (d_block + d_middle).astype(BF16)
    columns = both.reshape(2 * SHARD, LAT // HEAD, HEAD).transpose(1, 0, 2)

    def piece(by):
        tile = lax.dynamic_index_in_dim(columns, (t + by) % N_Z, 0, keepdims=False)
        return jnp.concatenate([tile, columns[N_Z]], axis=1)

    rows = jnp.stack([piece(0), z_hop(piece(3), -1), z_hop(piece(2), 2), z_hop(piece(1), 1)])
    rows = rows.reshape(N_Z, 2, SHARD, 2 * HEAD).transpose(1, 0, 2, 3).reshape(ROWS, 2 * HEAD)
    return d_block, rows, jnp.concatenate([d_q, d_c, d_rope, blank[:, ROPE:]], axis=1), (attn_gain, q_gain, kv_gain), also


def scatter_sum(x):
    return jnp.sum(lax.all_to_all(x, "dp", 0, 0).astype(F32), axis=0)


def body(
    layer_input,
    cotangent,
    seq_lengths,
    g_attn,
    w_qa,
    g_q,
    w_qb,
    w_kva,
    g_kv,
    w_kvb,
    w_o,
    g_ffn,
    w_gate,
    w_up,
    w_down,
):
    core = lax.axis_index("section")
    blocks = ffn_pack(w_gate[0], w_up[0], w_down[0].T)
    blocks, w_qa = tie((blocks, w_qa))
    keep, give = attention_packs(
        core.reshape(1), w_qa[0], w_qb[0], w_kva[0], w_kvb[0], w_o[0].T, g_attn, g_ffn, g_q, g_kv
    )
    attn_one, attn_two = by_core(core, keep, to_core(give))
    attn_one = lax.all_gather(attn_one, "dp")

    blocks = lax.all_to_all(blocks, "dp", 0, 0)
    tab = head_tables(seq_lengths)
    blocks, cotangent, layer_input = lax.optimization_barrier((blocks, cotangent, layer_input))
    weights = blocks.reshape(D, MATS)
    near, after = ring_hop(weights, 1), ring_hop(weights, -1)

    def token_rows(x):
        packs = x.reshape(2, N_Z, SHARD, D)
        first, second = by_core(core, packs[0], packs[1])
        return from_here(first).reshape(PACK, D), from_here(second).reshape(PACK, D)

    def d_mlp_rows(grad):
        return gather_dp((RES_SCALE * grad).astype(BF16))

    def d_attended_rows(d_middle):
        return gather_tokens((RES_SCALE * d_middle).astype(BF16))

    cot_own = token_rows(cotangent)[0][:SHARD].astype(F32)
    attn_one, tab, near, after = tie((attn_one, tab, near, after))
    gains_one = attention_gains(attn_one)
    own_one = jnp.stack([(core == 0).astype(jnp.int32), core])
    own_two = jnp.stack([(core == 1).astype(jnp.int32), core])

    rows = token_rows(layer_input)
    x_own = rows[0][:SHARD].astype(F32)
    normed, latent = latents(rows, gains_one["attn"], attn_one)
    wide = (A_COLS, A_COLS, D - 2 * A_COLS)
    shared = jnp.concatenate([(RES_SCALE * cot_own).astype(BF16), normed[:SHARD]], axis=0)
    shared = [shared[:, :A_COLS], shared[:, A_COLS : 2 * A_COLS], shared[:, 2 * A_COLS :]]
    shared[2] = jnp.pad(shared[2], ((0, 0), (0, A_COLS - wide[2])))
    attn_two = lax.all_gather(jnp.concatenate([attn_two] + shared, axis=0), "dp")
    shared = [
        attn_two[:, A_ROWS + 2 * SHARD * i : A_ROWS + 2 * SHARD * (i + 1), : wide[i]] for i in range(3)
    ]
    shared = jnp.concatenate(shared, axis=2)
    d_rows_two = shared[:, :SHARD].reshape(TOKENS, D)
    normed_one = lax.dynamic_slice_in_dim(shared[:, SHARD:], lax.axis_index("dp") * SLICE, SLICE, 2)
    gains_two = attention_gains(attn_two)
    middle, saved = attention_forward(normed, latent, x_own, attn_one, gains_one, tab)
    mine = [weights, near, after]
    ffn_weights = mine + [to_core(piece) for piece in mine]
    part, saved_one, ffn_weights = layer_forward(
        own_one, x_own, middle, saved, gains_one, ffn_weights, ring_hop(near, 1)
    )
    out_one = layer_out_rows(scatter_dp(part), saved_one)
    rows_one = gather_tokens(out_one)
    x_own = out_one.astype(F32)
    normed, latent = latents(rows_one, gains_two["attn"], attn_two)
    middle, saved = attention_forward(normed, latent, x_own, attn_two, gains_two, tab)
    part_two, saved_two, _ = layer_forward(own_two, x_own, middle, saved, gains_two, ffn_weights)

    mixed_one = lax.all_gather(saved_one[-1][5], "dp")

    ffn_rows, gu, hidden = saved_two[2:5]
    part, d_gu = ffn_backward(own_two, d_rows_two, gu, ffn_weights)
    grads_two = ffn_gradients(own_two, d_rows_two, ffn_rows, d_gu, hidden)
    d_normed_two = scatter_dp(part)
    d_normed_two, mixed_one = tie((d_normed_two, mixed_one))
    ring_two = ring_pairs(grads_two)
    d_middle, ffn_gain_two = middle_backward(cot_own, d_normed_two, saved_two, gains_two)
    d_attended = d_attended_rows(d_middle)
    part, d_query, d_key_value = attend_back(d_attended, tab, saved_two[-1], attn_two)
    packs_two = attend_gradients(d_attended, saved_two[-1], d_query, d_key_value)
    in_grad_two, rows, _, dg_two, part_two = attention_backward(
        part, d_middle, saved_two, attn_two, gains_two, scatter_dp(part_two)
    )
    packs_two = late_pack(saved_two[5], rows, (*dg_two, ffn_gain_two), packs_two).reshape(-1, WO)
    in_grad_two, ring_two = tie((in_grad_two, ring_two))
    ring_two = ring_first(ring_two)

    grad_one = in_grad_two.astype(F32)
    d_rows, packs_two = tie((d_mlp_rows(grad_one), packs_two))
    packs_two = lax.psum_scatter(packs_two, "dp", scatter_dimension=0, tiled=True)
    ffn_rows, gu, hidden = saved_one[2:5]
    part, d_gu = ffn_backward(own_one, d_rows, gu, ffn_weights)
    grads_one = ffn_gradients(own_one, d_rows, ffn_rows, d_gu, hidden)
    d_normed_two = scatter_dp(part)
    total_two = ring_last(ring_two)
    rows_two = gather_tokens(layer_out_rows(part_two, saved_two))
    d_normed_two, total_two, rows_two = tie((d_normed_two, total_two, rows_two))
    d_middle, ffn_gain_one = middle_backward(grad_one, d_normed_two, saved_one, gains_one)
    d_att_own = (RES_SCALE * d_middle).astype(BF16)
    columns = d_att_own.reshape(SHARD, N_DP, SLICE).transpose(1, 0, 2)
    home_two = lax.all_to_all(total_two, "dp", 0, 0)
    d_attended, grads_one, columns, home_two = tie(
        (gather_tokens(d_att_own), grads_one, columns, home_two)
    )
    part, d_query, d_key_value = attend_back(d_attended, tab, saved_one[-1], attn_one)
    low_one = low_gradients(saved_one[-1], d_query, d_key_value, columns)
    part, low_one = tie((part, low_one))
    low_one = lax.all_to_all(low_one, "dp", 0, 0)
    in_grad_one, _, d_lat_own, dg_one, pairs = attention_backward(
        part, d_middle, saved_one, attn_one, gains_one, ring_pairs(grads_one)
    )
    d_lat = jnp.broadcast_to(d_lat_own.astype(BF16)[None], (N_DP, SHARD, LAT_ALL))
    d_lat, low_one, first = tie((d_lat, low_one, ring_first(pairs)))
    columns = gather_tokens(low_one[:, LOW_ROWS:, :SLICE].reshape(TOKENS, SLICE))
    wo_one = wo_gradient(columns, mixed_one)
    low_one = jnp.sum(low_one[:, :LOW_ROWS].astype(F32), axis=0)
    d_lat = lax.all_to_all(d_lat, "dp", 0, 0)
    lat_one = latent_gradient(d_lat, normed_one)
    total_one, lat_one, in_grad_one = tie((ring_last(first), lat_one, in_grad_one))

    total_one = total_one.reshape(N_DP, HALF_ROWS, MATS)
    attn, q, kv = dg_one
    dg_one = jnp.concatenate([attn, ffn_gain_one, q, kv]).astype(BF16).reshape(-1, HEAD)
    dg_one = add(dg_one, to_core(dg_one))
    dg_one = sum(x.astype(F32) for x in gather_z(dg_one)).reshape(-1)
    row = [dg_one[:D], dg_one[D : 2 * D], dg_one[2 * D : 2 * D + QR], dg_one[2 * D + QR :]]
    row = jnp.concatenate([x.reshape(N_DP, -1) for x in row], axis=1).astype(BF16)
    row = jnp.pad(row[:, None], ((0, 0), (0, 15), (0, 0)))
    home_one = lax.all_to_all(jnp.concatenate([total_one, row], axis=1), "dp", 0, 0)
    dg_one = jnp.sum(home_one[:, HALF_ROWS].astype(F32), axis=0)
    got_one = lax.ppermute(home_one, "section", [(1, 0)])
    got_two = lax.ppermute(home_two, "section", [(0, 1)])
    gate_grad, up_grad, down_grad = ffn_unpack(core.reshape(1), home_one, got_one, home_two, got_two)

    def from_other(x, layer):
        return lax.ppermute(x, "section", [(1 - layer, layer)])

    lat_one = add(lat_one, from_other(lat_one, 0))
    lat_one = sum(x.astype(F32) for x in gather_z(lat_one))
    packs_two, lat_one = tie((packs_two, lat_one))
    tiles = from_zero(jnp.stack(gather_z(packs_two[E_ROWS:, :HEAD])))
    qa_grad, kva_grad, qb_grad, kvb_grad, wo_grad, gains = home(
        core.reshape(1),
        lat_one,
        wo_one,
        from_other(wo_one, 0),
        low_one,
        from_other(low_one, 0),
        tiles,
        from_other(tiles, 1),
        packs_two,
        from_other(packs_two, 1),
    )
    gains = gains.reshape(-1)

    def gain_part(one, two, width):
        return jnp.where(core == 0, dg_one[one : one + width], gains[two : two + width])[None]

    layer_out = in_order(*(jnp.where(core == 0, one, two) for one, two in zip(rows_one, rows_two)))[None]
    give = jnp.where(core == 0, in_grad_two, in_grad_one)
    mine = jnp.where(core == 0, in_grad_one, in_grad_two)
    both = jnp.concatenate([mine, to_core(give)], axis=1)
    both = jnp.concatenate(gather_z(both), axis=0)
    input_grad = in_order(both[:, :D], both[:, D:])[None]
    return (
        layer_out,
        input_grad,
        gain_part(0, 0, SLICE),
        qa_grad[None],
        gain_part(2 * SLICE, 4 * HEAD, QR // N_DP),
        qb_grad[None],
        kva_grad[None],
        gain_part(2 * SLICE + QR // N_DP, 4 * HEAD + QR // N_DP, KVR // N_DP),
        kvb_grad[None],
        wo_grad.T[None],
        gain_part(SLICE, 2 * HEAD, SLICE),
        gate_grad[None],
        up_grad[None],
        down_grad.T[None],
    )


def solution(mesh):
    in_specs = (
        P("dp", None),
        P("dp", None),
        P("dp", None),
        P("section", "dp"),
        P("section", "dp", None),
        P("section", "dp"),
        P("section", "dp", "tensor"),
        P("section", "dp", None),
        P("section", "dp"),
        P("section", "dp", "tensor"),
        P("section", "tensor", "dp"),
        P("section", "dp"),
        P("section", "dp", "tensor"),
        P("section", "dp", "tensor"),
        P("section", "tensor", "dp"),
    )
    out_specs = (
        P("section", "dp", None),
        P("section", "dp", None),
        P("section", "dp"),
        P("section", "dp", None),
        P("section", "dp"),
        P("section", "dp", "tensor"),
        P("section", "dp", None),
        P("section", "dp"),
        P("section", "dp", "tensor"),
        P("section", "tensor", "dp"),
        P("section", "dp"),
        P("section", "dp", "tensor"),
        P("section", "dp", "tensor"),
        P("section", "tensor", "dp"),
    )
    return jax.shard_map(body, mesh=mesh, in_specs=in_specs, out_specs=out_specs, check_vma=False)
```

```python
import math

import jax
import jax.numpy as jnp
from jax import lax
from jax.experimental import pallas as pl
from jax.experimental.pallas import tpu as pltpu
from jax.sharding import PartitionSpec as P

D = 2560
NOPE = 64
ROPE = 32
VD = 64
QR = 768
KVR = 256
PACK = 64
MB = 2
N_DP = 16
N_Z = 4
HEADS = 5
SLICE = D // N_DP
FF_PART = 100
LANES = 128
SHARD = 16
RES_SCALE = 1.4 / math.sqrt(62.0)
EPSILON = 1e-05
SCORE_SCALE = (NOPE + ROPE) ** (-0.5)
BF16 = jnp.bfloat16
F32 = jnp.float32


def dot(a, b):
    return jnp.dot(a, b, preferred_element_type=F32)


def dot_tn(a, b):
    return lax.dot_general(a, b, (((0,), (0,)), ((), ())), preferred_element_type=F32)


def dot_nt(a, b):
    return lax.dot_general(a, b, (((1,), (1,)), ((), ())), preferred_element_type=F32)


def to_core(x):
    return lax.ppermute(x, "section", [(0, 1), (1, 0)])


def z_hop(x, by):
    return lax.ppermute(x, "tensor", [(i, (i + by) % N_Z) for i in range(N_Z)])


def by_core(core, mine, other):
    return jnp.where(core == 0, mine, other), jnp.where(core == 0, other, mine)


def from_here(x):
    return lax.dynamic_slice_in_dim(jnp.concatenate([x, x]), lax.axis_index("tensor"), N_Z, 0)


def from_zero(x):
    at = (N_Z - lax.axis_index("tensor")) % N_Z
    return lax.dynamic_slice_in_dim(jnp.concatenate([x, x]), at, N_Z, 0)


def gather_z(x):
    return [x, z_hop(x, -1), z_hop(x, 2), z_hop(x, 1)]


def gather_tokens(x):
    mine = jnp.concatenate(gather_z(x), axis=0)
    return mine, to_core(mine)


def in_order(mine, other):
    core = lax.axis_index("section")
    shape = (N_Z, SHARD, mine.shape[-1])
    mine, other = from_zero(mine.reshape(shape)), from_zero(other.reshape(shape))
    return jnp.concatenate(by_core(core, mine, other), axis=0).reshape(-1, shape[-1])


def scatter_tokens(part):
    half = part[:PACK].astype(F32) + to_core(part[PACK:]).astype(F32)
    sent = half.astype(BF16)
    total = half[:SHARD]
    for by in (2, 1, 3):
        total = total + z_hop(sent[SHARD * by : SHARD * (by + 1)], by).astype(F32)
    return total


def gather_dp(x):
    copies = jnp.broadcast_to(x[None], (N_DP,) + x.shape)
    return lax.all_to_all(copies, "dp", 0, 0).reshape(N_DP * x.shape[0], x.shape[1])


def scatter_dp(part):
    pieces = lax.all_to_all(part.reshape(N_DP, SHARD, D), "dp", 0, 0)
    return jnp.sum(pieces.astype(F32), axis=0)


def norm_scale(x):
    return lax.rsqrt(jnp.mean(x * x, axis=-1, keepdims=True) + EPSILON)


def norm(x, gain):
    return x * norm_scale(x) * gain


def norm_back(x, gain, d):
    q = norm_scale(x)
    along = jnp.mean(gain * d * x, axis=-1, keepdims=True)
    return q * gain * d - x * (q * q * q) * along, jnp.sum(d * x * q, axis=0)


MATS = 3 * LANES
TOKENS = N_DP * SHARD
FF_VMEM = 56 * 1024 * 1024
FF_SCRATCH = [pltpu.VMEM((N_Z, D, MATS), BF16), pltpu.SemaphoreType.DMA((N_Z,))]


def ffn_copies(own_ref, mine, other, w_ref, sems):
    copies = [pltpu.make_async_copy(mine[z], w_ref.at[z], sems.at[z]) for z in range(N_Z)]
    others = [pltpu.make_async_copy(other[z], w_ref.at[z], sems.at[z]) for z in range(N_Z)]

    @pl.when(own_ref[0] == 1)
    def _():
        for copy in copies:
            copy.start()

    @pl.when(own_ref[0] != 1)
    def _():
        for copy in others:
            copy.start()

    return copies


def down_pair(w_ref, z):
    return jnp.concatenate([w_ref[z, :, 2 * LANES :], w_ref[z + 1, :, 2 * LANES :]], axis=1)


def ffn_forward_kernel(own_ref, n_ref, *refs):
    mine, other = refs[:N_Z], refs[N_Z : 2 * N_Z]
    part_ref, gu_ref, hid_ref, w_ref, sems = refs[2 * N_Z :]
    copies = ffn_copies(own_ref, mine, other, w_ref, sems)
    for z in range(N_Z):
        copies[z].wait()
        gu = dot(n_ref[...], w_ref[z, :, : 2 * LANES])
        gu_ref[:, 2 * LANES * z : 2 * LANES * (z + 1)] = gu
        gate, up = gu[:, :LANES], gu[:, LANES:]
        hid_ref[:, LANES * z : LANES * (z + 1)] = (gate * jax.nn.sigmoid(gate) * up).astype(BF16)
    out = dot_nt(hid_ref[:, : 2 * LANES], down_pair(w_ref, 0))
    part_ref[...] = (out + dot_nt(hid_ref[:, 2 * LANES :], down_pair(w_ref, 2))).astype(BF16)


def ffn_specs(arrays):
    vmem = pl.BlockSpec(memory_space=pltpu.VMEM)
    smem = pl.BlockSpec(memory_space=pltpu.SMEM)
    return [smem] + [vmem] * arrays + [pl.BlockSpec(memory_space=pl.ANY)] * (2 * N_Z)


def ffn_forward(own, rows, weights):
    return pl.pallas_call(
        ffn_forward_kernel,
        out_shape=(
            jax.ShapeDtypeStruct((TOKENS, D), BF16),
            jax.ShapeDtypeStruct((TOKENS, 2 * LANES * N_Z), F32),
            jax.ShapeDtypeStruct((TOKENS, LANES * N_Z), BF16),
        ),
        in_specs=ffn_specs(1),
        out_specs=(pl.BlockSpec(memory_space=pltpu.VMEM),) * 3,
        scratch_shapes=FF_SCRATCH,
        compiler_params=pltpu.CompilerParams(vmem_limit_bytes=FF_VMEM),
        name="ffn_forward",
    )(own, rows, *weights)


HALF_ROWS = SLICE // 2


def ffn_backward_kernel(own_ref, dm_ref, gu_ref, *refs):
    mine, other = refs[:N_Z], refs[N_Z : 2 * N_Z]
    part_ref, dgu_ref, w_ref, sems = refs[2 * N_Z :]
    copies = ffn_copies(own_ref, mine, other, w_ref, sems)
    out = None
    for z in range(0, N_Z, 2):
        copies[z].wait()
        copies[z + 1].wait()
        d_hidden = dot(dm_ref[...], down_pair(w_ref, z))
        for k in range(2):
            columns = slice(2 * LANES * (z + k), 2 * LANES * (z + k) + LANES)
            more = slice(columns.stop, columns.stop + LANES)
            gate, up = gu_ref[:, columns], gu_ref[:, more]
            d_h = d_hidden[:, LANES * k : LANES * (k + 1)]
            s = jax.nn.sigmoid(gate)
            dgu_ref[:, columns] = (d_h * up * (s + gate * s * (1.0 - s))).astype(BF16)
            dgu_ref[:, more] = (d_h * (gate * s)).astype(BF16)
    for z in range(N_Z):
        term = dot_nt(dgu_ref[:, 2 * LANES * z : 2 * LANES * (z + 1)], w_ref[z, :, : 2 * LANES])
        out = term if z == 0 else out + term
    part_ref[...] = out.astype(BF16)


def ffn_backward(own, d_rows, gu, weights):
    return pl.pallas_call(
        ffn_backward_kernel,
        out_shape=(
            jax.ShapeDtypeStruct((TOKENS, D), BF16),
            jax.ShapeDtypeStruct((TOKENS, 2 * LANES * N_Z), BF16),
        ),
        in_specs=ffn_specs(2),
        out_specs=(pl.BlockSpec(memory_space=pltpu.VMEM),) * 2,
        scratch_shapes=FF_SCRATCH,
        compiler_params=pltpu.CompilerParams(vmem_limit_bytes=FF_VMEM),
        name="ffn_backward",
    )(own, d_rows, gu, *weights)


HALF_ROWS = SLICE // 2


def ffn_gradients_kernel(own_ref, dm_ref, n_ref, dgu_ref, hid_ref, *refs):
    outs, grad_ref, out_sems = refs[: 2 * N_Z], refs[2 * N_Z], refs[2 * N_Z + 1]
    core = own_ref[1]

    def store(z, columns, grad):
        grad_ref[z, :, :, :, columns] = grad.reshape(N_DP, 2, HALF_ROWS, grad.shape[1])

    def send(z, keep_at, give_at):
        return [
            pltpu.make_async_copy(grad_ref.at[z, :, core], outs[keep_at], out_sems.at[keep_at]),
            pltpu.make_async_copy(
                grad_ref.at[z, :, 1 - core], outs[N_Z + give_at], out_sems.at[N_Z + give_at]
            ),
        ]

    for z in (2, 0):
        hidden = hid_ref[:, LANES * z : LANES * (z + 2)]
        grad = dot_tn(dm_ref[...], hidden).astype(BF16)
        store(z, slice(2 * LANES, MATS), grad[:, :LANES])
        store(z + 1, slice(2 * LANES, MATS), grad[:, LANES:])
        for k in range(2):
            d_gu = dgu_ref[:, 2 * LANES * (z + k) : 2 * LANES * (z + k + 1)]
            store(z + k, slice(0, 2 * LANES), dot_tn(n_ref[...], d_gu).astype(BF16))
            if z + k in (0, N_Z - 1):
                for copy in send(z + k, z + k, z + k):
                    copy.start()
            else:
                for owner in (1, 0):
                    keep_at = z + k if owner == 1 else 3 - z - k

                    @pl.when(own_ref[0] == owner)
                    def _(at=z + k, keep_at=keep_at):
                        for copy in send(at, keep_at, 3 - keep_at):
                            copy.start()

    for z in range(N_Z):
        for copy in send(z, z, z):
            copy.wait()


def ffn_gradients(own, d_rows, rows, d_gu, hidden):
    vmem = pl.BlockSpec(memory_space=pltpu.VMEM)
    return pl.pallas_call(
        ffn_gradients_kernel,
        out_shape=tuple(jax.ShapeDtypeStruct((N_DP, HALF_ROWS, MATS), BF16) for _ in range(2 * N_Z)),
        in_specs=[pl.BlockSpec(memory_space=pltpu.SMEM)] + [vmem] * 4,
        out_specs=(pl.BlockSpec(memory_space=pl.ANY),) * (2 * N_Z),
        scratch_shapes=[
            pltpu.VMEM((N_Z, N_DP, 2, HALF_ROWS, MATS), BF16),
            pltpu.SemaphoreType.DMA((2 * N_Z,)),
        ],
        compiler_params=pltpu.CompilerParams(vmem_limit_bytes=FF_VMEM),
        cost_estimate=pl.CostEstimate(flops=2 * TOKENS * D * MATS * N_Z, bytes_accessed=1 << 24, transcendentals=0),
        name="ffn_gradients",
    )(own, d_rows, rows, d_gu, hidden)


FF = N_DP * FF_PART
WINDOW = 2 * LANES
FF_PADDED = (FF - FF_PART) // LANES * LANES + WINDOW


def ffn_pack_kernel(gate_ref, up_ref, down_ref, out_ref, wide_ref):
    wide_ref[0, :, :FF] = gate_ref[...].astype(F32)
    wide_ref[1, :, :FF] = up_ref[...].astype(F32)
    wide_ref[2, :, :FF] = down_ref[...].astype(F32)
    valid = lax.broadcasted_iota(jnp.int32, (SLICE, LANES), 1) < FF_PART
    for p in range(N_DP):
        at = FF_PART * p // LANES * LANES
        by = FF_PART * p - at
        for m in range(3):
            window = wide_ref[m, :, at : at + WINDOW]
            if by > 0:
                window = pltpu.roll(window, WINDOW - by, 1)
            block = jnp.where(valid, window[:, :LANES], 0.0)
            out_ref[p, :, LANES * m : LANES * (m + 1)] = block.astype(BF16)


def ffn_pack(w_gate, w_up, w_down):
    return pl.pallas_call(
        ffn_pack_kernel,
        out_shape=jax.ShapeDtypeStruct((N_DP, SLICE, MATS), BF16),
        scratch_shapes=[pltpu.VMEM((3, SLICE, FF_PADDED), F32)],
        compiler_params=pltpu.CompilerParams(vmem_limit_bytes=FF_VMEM),
        name="ffn_pack",
    )(w_gate, w_up, w_down)


def ffn_unpack_kernel(core_ref, blocks_ref, got_ref, gate_ref, up_ref, down_ref):
    first = core_ref[0] == 0
    one, two = slice(0, HALF_ROWS), slice(HALF_ROWS, SLICE)
    for p in range(N_DP):
        columns = slice(FF_PART * p, FF_PART * (p + 1))
        for m, out_ref in enumerate((gate_ref, up_ref, down_ref)):
            lanes = slice(LANES * m, LANES * (m + 1))
            low = jnp.where(first, blocks_ref[p, one, lanes], got_ref[p, two, lanes])
            high = jnp.where(first, got_ref[p, one, lanes], blocks_ref[p, two, lanes])
            out_ref[one, columns] = low[:, :FF_PART].astype(F32)
            out_ref[two, columns] = high[:, :FF_PART].astype(F32)


def ffn_unpack(core, *blocks):
    vmem = pl.BlockSpec(memory_space=pltpu.VMEM)
    return pl.pallas_call(
        ffn_unpack_kernel,
        out_shape=(jax.ShapeDtypeStruct((SLICE, FF), F32),) * 3,
        in_specs=[pl.BlockSpec(memory_space=pltpu.SMEM), vmem, vmem],
        out_specs=(vmem,) * 3,
        compiler_params=pltpu.CompilerParams(vmem_limit_bytes=FF_VMEM),
        name="ffn_unpack",
    )(core, *blocks)


A_ROWS = SLICE + QR // N_DP + KVR // N_DP
A_COLS = 896
LAT = 640
WO_AT = 512
WO = 384
HEAD = 128
ROWS = MB * PACK
QB_ROWS = slice(SLICE, SLICE + QR // N_DP)
KVB_ROWS = slice(SLICE + QR // N_DP, A_ROWS)
E_ROWS = 2 * A_ROWS - SLICE
ATT_VMEM = 48 * 1024 * 1024


def latent_kernel(mine_ref, other_ref, gain_ref, pack_ref, normed_ref, lat_ref, w_ref, sem):
    copy = pltpu.make_async_copy(pack_ref.at[:, 0:SLICE, 0:LAT], w_ref, sem)
    copy.start()
    normed_ref[:PACK] = norm(mine_ref[...].astype(F32), gain_ref[...]).astype(BF16)
    normed_ref[PACK:] = norm(other_ref[...].astype(F32), gain_ref[...]).astype(BF16)
    copy.wait()
    lat_ref[...] = dot(normed_ref[...], w_ref[...].reshape(D, LAT))


def latents(rows, gain, pack):
    vmem = pl.BlockSpec(memory_space=pltpu.VMEM)
    return pl.pallas_call(
        latent_kernel,
        out_shape=(
            jax.ShapeDtypeStruct((ROWS, D), BF16),
            jax.ShapeDtypeStruct((ROWS, LAT), F32),
        ),
        in_specs=[vmem, vmem, vmem, pl.BlockSpec(memory_space=pl.ANY)],
        out_specs=(vmem, vmem),
        scratch_shapes=[pltpu.VMEM((N_DP, SLICE, LAT), BF16), pltpu.SemaphoreType.DMA],
        compiler_params=pltpu.CompilerParams(vmem_limit_bytes=ATT_VMEM),
        name="latents",
    )(*rows, gain, pack)


def weight_copies(pack_ref, qb_ref, kvb_ref, wo_ref, sems):
    sources = (
        pack_ref.at[:, QB_ROWS, 0:LAT],
        pack_ref.at[:, KVB_ROWS, 0:LAT],
        pack_ref.at[:, 0:SLICE, WO_AT : WO_AT + WO],
    )
    targets = (qb_ref, kvb_ref, wo_ref)
    copies = [pltpu.make_async_copy(a, b, sems.at[i]) for i, (a, b) in enumerate(zip(sources, targets))]
    for copy in copies:
        copy.start()
    return copies


def weight_scratch():
    return [
        pltpu.VMEM((N_DP, QR // N_DP, LAT), BF16),
        pltpu.VMEM((N_DP, KVR // N_DP, LAT), BF16),
        pltpu.VMEM((N_DP, SLICE, WO), BF16),
        pltpu.SemaphoreType.DMA((3,)),
    ]


def lanes_of(x):
    return lax.broadcasted_iota(jnp.int32, x.shape, 1)


def turn(x, tab_ref):
    return (
        x * tab_ref[0]
        + pltpu.roll(x, HEAD - ROPE // 2, 1) * tab_ref[1]
        + pltpu.roll(x, ROPE // 2, 1) * tab_ref[2]
    )


def turn_back(x, tab_ref):
    return (
        x * tab_ref[0]
        - pltpu.roll(x, HEAD - ROPE // 2, 1) * tab_ref[1]
        - pltpu.roll(x, ROPE // 2, 1) * tab_ref[2]
    )


def head_columns(h):
    return slice(HEAD * h, HEAD * (h + 1))


def probs_of(query, key, tab_ref):
    scores = jnp.where(tab_ref[3] < 0.0, -1e30, dot_nt(query, key) * SCORE_SCALE)
    weight = jnp.exp(scores - jnp.max(scores, axis=-1, keepdims=True))
    return weight / jnp.sum(weight, axis=-1, keepdims=True)


def attend_kernel(
    core_ref, mine_ref, other_ref, tab_ref, gq_ref, gkv_ref, pack_ref,
    part_ref, sq_ref, comp_ref, q_ref, kv_ref, kr_ref, mixed_ref, lat_ref,
    qb_ref, kvb_ref, wo_ref, sems,
):
    copies = weight_copies(pack_ref, qb_ref, kvb_ref, wo_ref, sems)
    zero = core_ref[0] == 0
    other = jnp.concatenate([other_ref[PACK:], other_ref[:PACK]], axis=0)
    second = jnp.where(zero, other, mine_ref[...])
    first = jnp.where(zero, mine_ref[:, :512], other[:, :512])
    latent_q = jnp.concatenate([first, second[:, :256]], axis=1)
    lat_ref[:, :QR] = latent_q[:SHARD]
    lat_ref[:, QR:] = second[:SHARD, 256:512]
    sq_ref[...] = norm(latent_q, gq_ref[...]).astype(BF16)
    comp_ref[...] = norm(second[:, 256:512], gkv_ref[...]).astype(BF16)
    rope = pltpu.roll(second[:, 512:640], NOPE, 1)
    rope = jnp.where(lanes_of(rope) < NOPE, 0.0, turn(rope, tab_ref)).astype(BF16)
    kr_ref[...] = rope
    copies[0].wait()
    query = dot(sq_ref[...], qb_ref[...].reshape(QR, LAT))
    for h in range(HEADS):
        q_ref[:, head_columns(h)] = turn(query[:, head_columns(h)], tab_ref).astype(BF16)
    copies[1].wait()
    kv_ref[...] = dot(comp_ref[...], kvb_ref[...].reshape(KVR, LAT)).astype(BF16)
    heads = []
    for h in range(HEADS):
        kv = kv_ref[:, head_columns(h)]
        key = jnp.where(lanes_of(kv) < NOPE, kv, rope)
        probs = probs_of(q_ref[:, head_columns(h)], key, tab_ref)
        heads.append(dot(probs.astype(BF16), kv))
    low = lanes_of(heads[0]) < NOPE
    tiles = [jnp.where(low, 0.0, heads[0])]
    tiles += [jnp.where(low, pltpu.roll(heads[i], NOPE, 1), heads[i + 1]) for i in (1, 3)]
    mixed_ref[...] = jnp.concatenate(tiles, axis=1).astype(BF16)
    copies[2].wait()
    part_ref[...] = dot_nt(mixed_ref[...], wo_ref[...].reshape(D, WO)).astype(BF16)


def attend(core, mine, other, tab, g_q, g_kv, pack):
    vmem = pl.BlockSpec(memory_space=pltpu.VMEM)
    widths = (D, QR, KVR, LAT, LAT, HEAD, WO)
    return pl.pallas_call(
        attend_kernel,
        out_shape=tuple(jax.ShapeDtypeStruct((ROWS, w), BF16) for w in widths)
        + (jax.ShapeDtypeStruct((SHARD, QR + KVR), F32),),
        in_specs=[pl.BlockSpec(memory_space=pltpu.SMEM)] + [vmem] * 5 + [pl.BlockSpec(memory_space=pl.ANY)],
        out_specs=(vmem,) * (len(widths) + 1),
        scratch_shapes=weight_scratch(),
        compiler_params=pltpu.CompilerParams(vmem_limit_bytes=ATT_VMEM),
        name="attend",
    )(core, mine, other, tab, g_q, g_kv, pack)


def attend_back_kernel(
    mine_ref, other_ref, tab_hbm, q_hbm, kv_hbm, kr_hbm, pack_ref,
    part_ref, dq_ref, dkv_ref,
    tab_ref, q_ref, kv_ref, kr_ref, in_sems, qb_ref, kvb_ref, wo_ref, sems,
):
    pairs = ((kv_hbm, kv_ref), (kr_hbm, kr_ref), (q_hbm, q_ref), (tab_hbm, tab_ref))
    inputs = [pltpu.make_async_copy(a, b, in_sems.at[i]) for i, (a, b) in enumerate(pairs)]
    for copy in inputs:
        copy.start()
    copies = weight_copies(pack_ref, qb_ref, kvb_ref, wo_ref, sems)
    d_att = jnp.concatenate([mine_ref[...], other_ref[...]], axis=0)
    copies[2].wait()
    d_mixed = dot(d_att, wo_ref[...].reshape(D, WO))
    for copy in inputs:
        copy.wait()
    rope = kr_ref[...]
    d_rope = jnp.zeros((ROWS, HEAD), F32)
    for h in range(HEADS):
        kv = kv_ref[:, head_columns(h)]
        low = lanes_of(kv) < NOPE
        key = jnp.where(low, kv, rope)
        query = q_ref[:, head_columns(h)]
        probs = probs_of(query, key, tab_ref)
        tile = d_mixed[:, head_columns((h + 1) // 2)]
        if h % 2 == 1:
            tile = pltpu.roll(tile, NOPE, 1)
        tile = jnp.where(low, 0.0, tile).astype(BF16)
        d_probs = dot_nt(tile, kv)
        d_scores = probs * (d_probs - jnp.sum(probs * d_probs, axis=-1, keepdims=True))
        d_scores = d_scores.astype(BF16)
        d_query = dot(d_scores, key) * SCORE_SCALE
        d_key = dot_tn(d_scores, query) * SCORE_SCALE
        d_value = dot_tn(probs.astype(BF16), tile)
        dq_ref[:, head_columns(h)] = turn_back(d_query, tab_ref).astype(BF16)
        dkv_ref[:, head_columns(h)] = jnp.where(low, d_key, d_value).astype(BF16)
        d_rope = d_rope + d_key
    d_rope = jnp.where(lanes_of(d_rope) < NOPE, 0.0, turn_back(jnp.where(lanes_of(d_rope) < NOPE, 0.0, d_rope), tab_ref))
    copies[0].wait()
    copies[1].wait()
    part_ref[:, :QR] = dot_nt(dq_ref[...], qb_ref[...].reshape(QR, LAT)).astype(BF16)
    part_ref[:, QR : QR + KVR] = dot_nt(dkv_ref[...], kvb_ref[...].reshape(KVR, LAT)).astype(BF16)
    part_ref[:, QR + KVR :] = d_rope.astype(BF16)


def attend_back(d_attended, tab, saved, pack):
    vmem = pl.BlockSpec(memory_space=pltpu.VMEM)
    return pl.pallas_call(
        attend_back_kernel,
        out_shape=(
            jax.ShapeDtypeStruct((ROWS, QR + KVR + HEAD), BF16),
            jax.ShapeDtypeStruct((ROWS, LAT), BF16),
            jax.ShapeDtypeStruct((ROWS, LAT), BF16),
        ),
        in_specs=[vmem] * 2 + [pl.BlockSpec(memory_space=pl.ANY)] * 5,
        out_specs=(vmem,) * 3,
        scratch_shapes=[
            pltpu.VMEM((4, ROWS, HEAD), F32),
            pltpu.VMEM((ROWS, LAT), BF16),
            pltpu.VMEM((ROWS, LAT), BF16),
            pltpu.VMEM((ROWS, HEAD), BF16),
            pltpu.SemaphoreType.DMA((4,)),
        ]
        + weight_scratch(),
        compiler_params=pltpu.CompilerParams(vmem_limit_bytes=ATT_VMEM),
        name="attend_back",
    )(*d_attended, tab, *saved[2:5], pack)


def attend_gradients_kernel(
    mine_ref, other_ref, dq_ref, dkv_ref, sq_hbm, comp_hbm, mixed_hbm,
    out_ref,
    early_ref, sq_ref, comp_ref, mixed_ref, sems,
):
    pairs = ((mixed_hbm, mixed_ref), (sq_hbm, sq_ref), (comp_hbm, comp_ref))
    copies = [pltpu.make_async_copy(a, b, sems.at[i]) for i, (a, b) in enumerate(pairs)]
    for copy in copies:
        copy.start()
    d_att = jnp.concatenate([mine_ref[...], other_ref[...]], axis=0)
    copies[0].wait()
    wo_grad = dot_tn(d_att, mixed_ref[...]).astype(BF16)
    early_ref[:, :SLICE, :] = wo_grad.reshape(N_DP, SLICE, WO)
    copies[1].wait()
    qb_grad = dot_tn(sq_ref[...], dq_ref[...]).astype(BF16).reshape(N_DP, QR // N_DP, LAT)
    copies[2].wait()
    kvb_grad = dot_tn(comp_ref[...], dkv_ref[...]).astype(BF16).reshape(N_DP, KVR // N_DP, LAT)
    early_ref[:, QB_ROWS, :] = qb_grad[:, :, :WO]
    early_ref[:, KVB_ROWS, :] = kvb_grad[:, :, :WO]
    more = slice(A_ROWS, A_ROWS + QR // N_DP)
    early_ref[:, more, : LAT - WO] = qb_grad[:, :, WO:]
    early_ref[:, more.stop :, : LAT - WO] = kvb_grad[:, :, WO:]
    early_ref[:, A_ROWS:, LAT - WO :] = jnp.zeros((N_DP, E_ROWS - A_ROWS, 2 * WO - LAT), BF16)
    copy = pltpu.make_async_copy(early_ref, out_ref.at[:, :E_ROWS], sems.at[3])
    copy.start()
    copy.wait()


def attend_gradients(d_attended, saved, d_query, d_key_value):
    vmem = pl.BlockSpec(memory_space=pltpu.VMEM)
    hbm = pl.BlockSpec(memory_space=pl.ANY)
    return pl.pallas_call(
        attend_gradients_kernel,
        out_shape=jax.ShapeDtypeStruct((N_DP, E_ROWS + L_ROWS, WO), BF16),
        in_specs=[vmem] * 4 + [hbm] * 3,
        out_specs=hbm,
        scratch_shapes=[
            pltpu.VMEM((N_DP, E_ROWS, WO), BF16),
            pltpu.VMEM((ROWS, QR), BF16),
            pltpu.VMEM((ROWS, KVR), BF16),
            pltpu.VMEM((ROWS, WO), BF16),
            pltpu.SemaphoreType.DMA((4,)),
        ],
        compiler_params=pltpu.CompilerParams(vmem_limit_bytes=ATT_VMEM),
        name="attend_gradients",
    )(*d_attended, d_query, d_key_value, saved[0], saved[1], saved[5])


def low_gradients_kernel(
    dq_ref, dkv_ref, columns_ref, sq_hbm, comp_hbm, out_ref, sq_ref, comp_ref, sems
):
    copies = [
        pltpu.make_async_copy(sq_hbm, sq_ref, sems.at[0]),
        pltpu.make_async_copy(comp_hbm, comp_ref, sems.at[1]),
    ]
    for copy in copies:
        copy.start()
    copies[0].wait()
    grad = dot_tn(sq_ref[...], dq_ref[...]).astype(BF16)
    out_ref[:, : QR // N_DP, :] = grad.reshape(N_DP, QR // N_DP, LAT)
    copies[1].wait()
    grad = dot_tn(comp_ref[...], dkv_ref[...]).astype(BF16)
    out_ref[:, QR // N_DP : LOW_ROWS, :] = grad.reshape(N_DP, KVR // N_DP, LAT)
    out_ref[:, LOW_ROWS:, :SLICE] = columns_ref[...]
    out_ref[:, LOW_ROWS:, SLICE:] = jnp.zeros((N_DP, SHARD, LAT - SLICE), BF16)


LOW_ROWS = A_ROWS - SLICE


def low_gradients(saved, d_query, d_key_value, columns):
    vmem = pl.BlockSpec(memory_space=pltpu.VMEM)
    hbm = pl.BlockSpec(memory_space=pl.ANY)
    return pl.pallas_call(
        low_gradients_kernel,
        out_shape=jax.ShapeDtypeStruct((N_DP, LOW_ROWS + SHARD, LAT), BF16),
        in_specs=[vmem, vmem, vmem, hbm, hbm],
        out_specs=vmem,
        scratch_shapes=[
            pltpu.VMEM((ROWS, QR), BF16),
            pltpu.VMEM((ROWS, KVR), BF16),
            pltpu.SemaphoreType.DMA((2,)),
        ],
        compiler_params=pltpu.CompilerParams(vmem_limit_bytes=ATT_VMEM),
        name="low_gradients",
    )(d_query, d_key_value, columns, saved[0], saved[1])


def wo_gradient_kernel(mine_ref, other_ref, mixed_hbm, out_ref, mixed_ref, sem):
    copy = pltpu.make_async_copy(mixed_hbm, mixed_ref, sem)
    copy.start()
    copy.wait()
    total = None
    for i in range(2 * N_Z):
        d_ref = mine_ref if i < N_Z else other_ref
        d_att = d_ref[TOKENS * (i % N_Z) : TOKENS * (i % N_Z + 1)]
        mixed = mixed_ref[:, SHARD * i : SHARD * (i + 1), :].reshape(TOKENS, WO)
        term = dot_tn(d_att, mixed)
        total = term if total is None else total + term
    out_ref[...] = total


def wo_gradient(d_attended, mixed):
    vmem = pl.BlockSpec(memory_space=pltpu.VMEM)
    return pl.pallas_call(
        wo_gradient_kernel,
        out_shape=jax.ShapeDtypeStruct((SLICE, WO), F32),
        in_specs=[vmem, vmem, pl.BlockSpec(memory_space=pl.ANY)],
        out_specs=vmem,
        scratch_shapes=[pltpu.VMEM((N_DP, ROWS, WO), BF16), pltpu.SemaphoreType.DMA],
        compiler_params=pltpu.CompilerParams(vmem_limit_bytes=ATT_VMEM),
        name="wo_gradient",
    )(*d_attended, mixed)


LAT_ALL = QR + KVR + HEAD


def latent_gradient_kernel(rows_ref, normed_ref, out_ref):
    rows = rows_ref[...].reshape(TOKENS, LAT_ALL)
    out_ref[...] = dot_tn(normed_ref[...].reshape(TOKENS, SLICE), rows).astype(BF16)


def latent_gradient(rows, normed):
    return pl.pallas_call(
        latent_gradient_kernel,
        out_shape=jax.ShapeDtypeStruct((SLICE, LAT_ALL), BF16),
        compiler_params=pltpu.CompilerParams(vmem_limit_bytes=ATT_VMEM),
        name="latent_gradient",
    )(rows, normed)


L_ROWS = 2 * SLICE


def late_kernel(rows_ref, gains_ref, normed_hbm, packs_ref, out_ref, late_ref, normed_ref, sem, out_sem):
    copy = pltpu.make_async_copy(normed_hbm, normed_ref, sem)
    copy.start()
    late_ref[:, SLICE : SLICE + 16, 2 * HEAD :] = gains_ref[...]
    late_ref[:, SLICE + 16 :, 2 * HEAD :] = jnp.zeros((N_DP, SLICE - 16, HEAD), BF16)
    copy.wait()
    grad = dot_tn(normed_ref[...], rows_ref[...]).astype(BF16)
    late_ref[:, :SLICE, :] = grad[:, :WO].reshape(N_DP, SLICE, WO)
    late_ref[:, SLICE:, : 2 * HEAD] = grad[:, WO:].reshape(N_DP, SLICE, 2 * HEAD)
    copy = pltpu.make_async_copy(late_ref, out_ref.at[:, E_ROWS:], out_sem)
    copy.start()
    copy.wait()


def gain_vectors(gains):
    parts = (gains[:D], gains[D : 2 * D], gains[2 * D : 2 * D + QR], gains[2 * D + QR : 2 * D + QR + KVR])
    return [x.reshape(N_DP, -1) for x in parts]


def late_pack(normed, rows, gains, packs):
    attn, ffn, q, kv = gain_vectors(gains)
    wide = ((0, 0), (0, 2 * HEAD - SLICE))
    row = jnp.concatenate([jnp.pad(attn, wide), jnp.pad(ffn, wide), q, kv], axis=1)
    row = jnp.pad(row, ((0, 0), (0, 16 * HEAD - row.shape[1]))).reshape(N_DP, 16, HEAD).astype(BF16)
    vmem = pl.BlockSpec(memory_space=pltpu.VMEM)
    hbm = pl.BlockSpec(memory_space=pl.ANY)
    return pl.pallas_call(
        late_kernel,
        out_shape=jax.ShapeDtypeStruct(packs.shape, BF16),
        in_specs=[vmem, vmem, hbm, hbm],
        out_specs=hbm,
        scratch_shapes=[
            pltpu.VMEM((N_DP, L_ROWS, WO), BF16),
            pltpu.VMEM((ROWS, D), BF16),
            pltpu.SemaphoreType.DMA,
            pltpu.SemaphoreType.DMA,
        ],
        input_output_aliases={3: 0},
        compiler_params=pltpu.CompilerParams(vmem_limit_bytes=ATT_VMEM),
        name="late_in_packs",
    )(rows, row, normed, packs)


def normed_back_kernel(d_ref, pack_ref, out_ref, w_ref, sem):
    copy = pltpu.make_async_copy(pack_ref.at[:, 0:SLICE, 0:LAT], w_ref, sem)
    copy.start()
    copy.wait()
    out_ref[...] = dot_nt(d_ref[...], w_ref[...].reshape(D, LAT))


def normed_back(d_latent, pack):
    vmem = pl.BlockSpec(memory_space=pltpu.VMEM)
    return pl.pallas_call(
        normed_back_kernel,
        out_shape=jax.ShapeDtypeStruct((d_latent.shape[0], D), F32),
        in_specs=[vmem, pl.BlockSpec(memory_space=pl.ANY)],
        out_specs=vmem,
        scratch_shapes=[pltpu.VMEM((N_DP, SLICE, LAT), BF16), pltpu.SemaphoreType.DMA],
        compiler_params=pltpu.CompilerParams(vmem_limit_bytes=ATT_VMEM),
        name="normed_back",
    )(d_latent, pack)


def home_kernel(
    core_ref, lat_ref, wo1_ref, wo1_got_ref, low_ref, low_got_ref, packs_ref, packs_got_ref,
    qa_ref, kva_ref, qb_ref, kvb_ref, wo_ref, gain_ref, heads_ref,
):
    first = core_ref[0] == 0

    def pick(one, two):
        return jnp.where(first, one.astype(F32), two.astype(F32))

    wide = slice(0, SLICE)
    late, more = slice(E_ROWS, E_ROWS + SLICE), slice(E_ROWS + SLICE, E_ROWS + L_ROWS)
    gain_rows = slice(E_ROWS + SLICE, E_ROWS + SLICE + 16)
    gain_ref[...] = (
        packs_ref[gain_rows, 2 * HEAD :].astype(F32) + packs_got_ref[gain_rows, 2 * HEAD :].astype(F32)
    )
    qa_ref[:, :WO] = pick(lat_ref[wide, :WO], packs_got_ref[late])
    qa_ref[:, WO:512] = pick(lat_ref[wide, WO:512], packs_got_ref[more, :HEAD])
    qa_ref[:, 512:] = pick(lat_ref[wide, 512:QR], packs_ref[late, : 2 * HEAD])
    kva_ref[:, :HEAD] = pick(lat_ref[wide, QR : QR + HEAD], packs_ref[late, 2 * HEAD :])
    kva_ref[:, HEAD:KVR] = pick(lat_ref[wide, QR + HEAD : QR + KVR], packs_ref[more, :HEAD])
    kva_ref[:, KVR:] = pick(lat_ref[wide, QR + KVR :], packs_ref[more, HEAD : 2 * HEAD])[:, :ROPE]
    at = WO - HEADS * VD
    low, high = pick(wo1_ref[...], packs_got_ref[wide]), pick(wo1_got_ref[...], packs_ref[wide])
    wo_ref[...] = jnp.concatenate([low[:, at:], high[:, at:]], axis=1)
    heads_ref[...] = jnp.zeros(heads_ref.shape, F32)
    qb_rows, kvb_rows = slice(0, QR // N_DP), slice(QR // N_DP, A_ROWS - SLICE)
    valid = lax.broadcasted_iota(jnp.int32, (QR // N_DP, HEAD), 1) < NOPE + ROPE
    for j in range(HEADS):
        start = SLICE if j < 3 else A_ROWS
        columns, packed = slice(HEAD * j, HEAD * (j + 1)), slice(HEAD * (j % 3), HEAD * (j % 3 + 1))
        for rows in (qb_rows, kvb_rows):
            at_rows = slice(start + rows.start, start + rows.stop)
            low = pick(low_ref[rows, columns], packs_got_ref[at_rows, packed])
            high = pick(low_got_ref[rows, columns], packs_ref[at_rows, packed])
            for k, tile in enumerate((low, high)):
                if rows == kvb_rows:
                    kvb_ref[:, HEAD * (HEADS * k + j) : HEAD * (HEADS * k + j + 1)] = tile
                    continue
                begin = (NOPE + ROPE) * (HEADS * k + j)
                at = begin // HEAD * HEAD
                tile = jnp.where(valid, tile, 0.0)
                window = jnp.concatenate([tile, jnp.zeros_like(tile)], axis=1)
                if begin > at:
                    window = pltpu.roll(window, begin - at, 1)
                heads_ref[:, at : at + 2 * HEAD] += window
    qb_ref[...] = heads_ref[:, : 2 * HEADS * (NOPE + ROPE)]


def home(core, *pieces):
    vmem = pl.BlockSpec(memory_space=pltpu.VMEM)
    shapes = (
        (SLICE, QR),
        (SLICE, KVR + ROPE),
        (QR // N_DP, 2 * HEADS * (NOPE + ROPE)),
        (KVR // N_DP, 2 * LAT),
        (SLICE, 2 * HEADS * VD),
        (16, HEAD),
    )
    return pl.pallas_call(
        home_kernel,
        out_shape=tuple(jax.ShapeDtypeStruct(x, F32) for x in shapes),
        in_specs=[pl.BlockSpec(memory_space=pltpu.SMEM)] + [vmem] * len(pieces),
        out_specs=(vmem,) * len(shapes),
        scratch_shapes=[pltpu.VMEM((QR // N_DP, 1152), F32)],
        compiler_params=pltpu.CompilerParams(vmem_limit_bytes=ATT_VMEM),
        name="home",
    )(core, *pieces)


def attention_pack_kernel(
    core_ref, qa_ref, qb_ref, kva_ref, kvb_ref, wo_ref, ga_ref, gf_ref, gq_ref, gk_ref,
    keep_ref, give_ref, heads_ref,
):
    half = HEADS * VD
    first = core_ref[0] == 0

    def put(rows, columns, zero, one):
        keep_ref[rows, columns] = jnp.where(first, zero, one).astype(BF16)
        give_ref[rows, columns] = jnp.where(first, one, zero).astype(BF16)

    def blank(rows, columns):
        zero = jnp.zeros((rows.stop - rows.start, columns.stop - columns.start), BF16)
        keep_ref[rows, columns] = zero
        give_ref[rows, columns] = zero

    wide = slice(0, SLICE)
    qa = qa_ref[...].astype(F32)
    put(wide, slice(0, 256), qa[:, :256], qa[:, 512:])
    put(wide, slice(256, 512), qa[:, 256:512], kva_ref[:, :256].astype(F32))
    wo_t = wo_ref[...].astype(F32)
    tail = jnp.zeros((SLICE, WO), F32)
    rope = jnp.concatenate([kva_ref[:, 256:].astype(F32), jnp.zeros((SLICE, WO - ROPE), F32)], axis=1)
    low = jnp.concatenate([tail[:, : WO - half], wo_t[:, :half]], axis=1)
    high = jnp.concatenate([tail[:, : WO - half], wo_t[:, half:]], axis=1)
    put(wide, slice(WO_AT, A_COLS), low, high + rope)
    heads_ref[:, : 2 * HEADS * (NOPE + ROPE)] = qb_ref[...].astype(F32)
    rows = QB_ROWS.stop - QB_ROWS.start
    valid = lax.broadcasted_iota(jnp.int32, (rows, HEAD), 1) < NOPE + ROPE
    tiles = []
    for j in range(2 * HEADS):
        at = (NOPE + ROPE) * j // HEAD * HEAD
        by = (NOPE + ROPE) * j - at
        window = heads_ref[:, at : at + 2 * HEAD]
        if by > 0:
            window = pltpu.roll(window, 2 * HEAD - by, 1)
        tiles.append(jnp.where(valid, window[:, :HEAD], 0.0))
    for j in range(HEADS):
        put(QB_ROWS, slice(HEAD * j, HEAD * (j + 1)), tiles[j], tiles[HEADS + j])
    gain_rows = [jnp.concatenate([g[...].astype(F32), jnp.zeros((1, 256 - SLICE), F32)], axis=1) for g in (ga_ref, gf_ref)]
    last = [gq_ref[...].astype(F32), gk_ref[...].astype(F32), jnp.zeros((1, 256 - 64), F32)]
    gain_rows.append(jnp.concatenate(last, axis=1))
    gains = jnp.concatenate(gain_rows + [jnp.zeros((rows - 3, 256), F32)], axis=0)
    put(QB_ROWS, slice(LAT, A_COLS), gains, gains)
    kvb = kvb_ref[...].astype(F32)
    put(KVB_ROWS, slice(0, LAT), kvb[:, :LAT], kvb[:, LAT:])
    blank(KVB_ROWS, slice(LAT, A_COLS))


def attention_packs(core, *weights):
    vmem = pl.BlockSpec(memory_space=pltpu.VMEM)
    return pl.pallas_call(
        attention_pack_kernel,
        out_shape=(jax.ShapeDtypeStruct((A_ROWS, A_COLS), BF16),) * 2,
        in_specs=[pl.BlockSpec(memory_space=pltpu.SMEM)] + [vmem] * len(weights),
        out_specs=(vmem, vmem),
        scratch_shapes=[pltpu.VMEM((QR // N_DP, 1152), F32)],
        compiler_params=pltpu.CompilerParams(vmem_limit_bytes=ATT_VMEM),
        name="attention_pack",
    )(core, *weights)


def attention_gains(pack):
    gains = pack[:, SLICE : SLICE + 3, LAT:].astype(F32)
    return dict(
        attn=gains[:, 0, :SLICE].reshape(1, D),
        ffn=gains[:, 1, :SLICE].reshape(1, D),
        q=gains[:, 2, : QR // N_DP].reshape(1, QR),
        kv=gains[:, 2, QR // N_DP : QR // N_DP + KVR // N_DP].reshape(1, KVR),
    )


def head_tables(seq_lengths):
    core, t = lax.axis_index("section"), lax.axis_index("tensor")
    at = jnp.arange(ROWS, dtype=jnp.int32)
    pack = (core + at // PACK) % 2
    row = (t + at % PACK // SHARD) % N_Z * SHARD + at % SHARD
    lengths = jnp.where(pack[:, None] == 0, seq_lengths[:1], seq_lengths[1:])
    past_end = row[:, None] >= jnp.cumsum(lengths, axis=1)
    segment = jnp.sum(past_end.astype(jnp.int32), axis=1)
    position = (row - jnp.sum(jnp.where(past_end, lengths, 0), axis=1)).astype(F32)
    frequency = 10000.0 ** (-2.0 * jnp.arange(ROPE // 2, dtype=F32) / ROPE)
    angles = position[:, None] * frequency[None, :]
    cosine, sine = jnp.cos(angles), jnp.sin(angles)
    sequence = pack * PACK + segment
    allowed = (sequence[:, None] == sequence[None, :]) & (row[None, :] <= row[:, None])

    def tile(*pieces):
        x = jnp.concatenate(pieces, axis=1)
        return jnp.pad(x, ((0, 0), (0, HEAD - x.shape[1])))

    ones, none = jnp.ones((ROWS, NOPE), F32), jnp.zeros((ROWS, NOPE), F32)
    bias = jnp.where(allowed, 0.0, -1.0).astype(F32)
    return jnp.stack(
        [tile(ones, cosine, cosine), tile(none, -sine), tile(none, jnp.zeros_like(sine), sine), bias]
    )


def ring_hop(x, by):
    pairs = [
        (c * N_Z + t, c * N_Z + (t + (by if c == 0 else -by)) % N_Z) for c in range(2) for t in range(N_Z)
    ]
    return lax.ppermute(x, ("section", "tensor"), pairs)


def add(*terms):
    return sum(x.astype(F32) for x in terms).astype(BF16)


def ring_pairs(pieces):
    got = [to_core(x) for x in pieces[N_Z:]]
    return add(pieces[3], got[3]), add(pieces[2], got[2]), (pieces[1], got[1]), (pieces[0], got[0])


def ring_first(pairs):
    far, after, near, mine = pairs
    return ring_hop(far, -1), ring_hop(after, 1), near, mine


def ring_last(first):
    far, after, near, mine = first
    return add(*mine, after, ring_hop(add(*near, far), -1))


tie = lax.optimization_barrier


def attention_forward(normed, latent, x_own, pack, gains, tab):
    core = lax.axis_index("section").reshape(1)
    part, *saved, latent_own = attend(
        core, latent, to_core(latent), tab, gains["q"], gains["kv"], pack
    )
    middle = x_own + RES_SCALE * scatter_tokens(part)
    return middle, (normed, latent_own, saved)


def layer_forward(own, x_own, middle, saved, gains, ffn_weights, far=None):
    ffn_rows = gather_dp(norm(middle, gains["ffn"]).astype(BF16))
    if far is not None:
        ffn_rows, far = tie((ffn_rows, far))
        ffn_weights = ffn_weights[:3] + [far] + ffn_weights[3:] + [to_core(far)]
    part, gu, hidden = ffn_forward(own, ffn_rows, ffn_weights)
    return part, (x_own, middle, ffn_rows, gu, hidden) + saved, ffn_weights


def layer_out_rows(part, saved):
    return (saved[1] + RES_SCALE * part).astype(BF16)


def middle_backward(grad_own, d_normed_two, saved, gains):
    d_middle, ffn_gain = norm_back(saved[1], gains["ffn"], d_normed_two)
    return d_middle + grad_own, ffn_gain


def attention_backward(part, d_middle, saved, pack, gains, also=(), after=()):
    core = lax.axis_index("section")
    x_own, _, _, _, _, _, latent_own, _ = saved
    d_latent, also = tie((scatter_tokens(part), also))
    d_q, q_gain = norm_back(latent_own[:, :QR], gains["q"], d_latent[:, :QR])
    d_c, kv_gain = norm_back(latent_own[:, QR:], gains["kv"], d_latent[:, QR : QR + KVR])
    d_rope = d_latent[:, QR + KVR + NOPE : QR + KVR + NOPE + ROPE]
    blank = jnp.zeros((SHARD, HEAD), F32)
    d_first = jnp.concatenate([d_q[:, :512], blank], axis=1).astype(BF16)
    d_second = jnp.concatenate([d_q[:, 512:], d_c, d_rope, blank[:, ROPE:]], axis=1).astype(BF16)
    mine = jnp.where(core == 0, d_first, d_second)
    other = to_core(jnp.where(core == 0, d_second, d_first))
    both = jnp.concatenate([mine, other], axis=0)
    both, after = tie((both, after))
    part = normed_back(both, pack)
    d_normed = part[:SHARD] + to_core(part[SHARD:])
    d_block, attn_gain = norm_back(x_own, gains["attn"], d_normed)
    d_block = (d_block + d_middle).astype(BF16)
    return d_block, both, jnp.concatenate([d_q, d_c, d_rope, blank[:, ROPE:]], axis=1), (attn_gain, q_gain, kv_gain), also, after


def scatter_sum(x):
    return jnp.sum(lax.all_to_all(x, "dp", 0, 0).astype(F32), axis=0)


def body(
    layer_input,
    cotangent,
    seq_lengths,
    g_attn,
    w_qa,
    g_q,
    w_qb,
    w_kva,
    g_kv,
    w_kvb,
    w_o,
    g_ffn,
    w_gate,
    w_up,
    w_down,
):
    core = lax.axis_index("section")
    blocks = ffn_pack(w_gate[0], w_up[0], w_down[0].T)
    blocks, w_qa = tie((blocks, w_qa))
    keep, give = attention_packs(
        core.reshape(1), w_qa[0], w_qb[0], w_kva[0], w_kvb[0], w_o[0].T, g_attn, g_ffn, g_q, g_kv
    )
    attn_one, attn_two = by_core(core, keep, to_core(give))
    attn_one = lax.all_gather(attn_one, "dp")

    blocks = lax.all_to_all(blocks, "dp", 0, 0)
    tab = head_tables(seq_lengths)
    blocks, cotangent, layer_input = lax.optimization_barrier((blocks, cotangent, layer_input))
    weights = blocks.reshape(D, MATS)
    near, after = ring_hop(weights, 1), ring_hop(weights, -1)

    def token_rows(x):
        packs = x.reshape(2, N_Z, SHARD, D)
        first, second = by_core(core, packs[0], packs[1])
        return from_here(first).reshape(PACK, D), from_here(second).reshape(PACK, D)

    def d_mlp_rows(grad):
        return gather_dp((RES_SCALE * grad).astype(BF16))

    def d_attended_rows(d_middle):
        return gather_tokens((RES_SCALE * d_middle).astype(BF16))

    cot_own = token_rows(cotangent)[0][:SHARD].astype(F32)
    attn_one, tab, near, after = tie((attn_one, tab, near, after))
    gains_one = attention_gains(attn_one)
    own_one = jnp.stack([(core == 0).astype(jnp.int32), core])
    own_two = jnp.stack([(core == 1).astype(jnp.int32), core])

    rows = token_rows(layer_input)
    x_own = rows[0][:SHARD].astype(F32)
    normed, latent = latents(rows, gains_one["attn"], attn_one)
    wide = (A_COLS, A_COLS, D - 2 * A_COLS)
    shared = jnp.concatenate([(RES_SCALE * cot_own).astype(BF16), normed[:SHARD]], axis=0)
    shared = [shared[:, :A_COLS], shared[:, A_COLS : 2 * A_COLS], shared[:, 2 * A_COLS :]]
    shared[2] = jnp.pad(shared[2], ((0, 0), (0, A_COLS - wide[2])))
    attn_two = lax.all_gather(jnp.concatenate([attn_two] + shared, axis=0), "dp")
    shared = [
        attn_two[:, A_ROWS + 2 * SHARD * i : A_ROWS + 2 * SHARD * (i + 1), : wide[i]] for i in range(3)
    ]
    shared = jnp.concatenate(shared, axis=2)
    d_rows_two = shared[:, :SHARD].reshape(TOKENS, D)
    normed_one = lax.dynamic_slice_in_dim(shared[:, SHARD:], lax.axis_index("dp") * SLICE, SLICE, 2)
    gains_two = attention_gains(attn_two)
    middle, saved = attention_forward(normed, latent, x_own, attn_one, gains_one, tab)
    mine = [weights, near, after]
    ffn_weights = mine + [to_core(piece) for piece in mine]
    part, saved_one, ffn_weights = layer_forward(
        own_one, x_own, middle, saved, gains_one, ffn_weights, ring_hop(near, 1)
    )
    out_one = layer_out_rows(scatter_dp(part), saved_one)
    rows_one = gather_tokens(out_one)
    x_own = out_one.astype(F32)
    normed, latent = latents(rows_one, gains_two["attn"], attn_two)
    middle, saved = attention_forward(normed, latent, x_own, attn_two, gains_two, tab)
    part_two, saved_two, _ = layer_forward(own_two, x_own, middle, saved, gains_two, ffn_weights)

    mixed_one = lax.all_gather(saved_one[-1][5], "dp")

    ffn_rows, gu, hidden = saved_two[2:5]
    part, d_gu = ffn_backward(own_two, d_rows_two, gu, ffn_weights)
    grads_two = ffn_gradients(own_two, d_rows_two, ffn_rows, d_gu, hidden)
    d_normed_two = scatter_dp(part)
    d_normed_two, mixed_one, normed_one = tie((d_normed_two, mixed_one, normed_one))
    ring_two = ring_pairs(grads_two)
    d_middle, ffn_gain_two = middle_backward(cot_own, d_normed_two, saved_two, gains_two)
    d_attended = d_attended_rows(d_middle)
    part, d_query, d_key_value = attend_back(d_attended, tab, saved_two[-1], attn_two)
    packs_two = attend_gradients(d_attended, saved_two[-1], d_query, d_key_value)
    in_grad_two, rows, _, dg_two, part_two, _ = attention_backward(
        part, d_middle, saved_two, attn_two, gains_two, scatter_dp(part_two)
    )
    attn, q, kv = dg_two
    dg_two = jnp.concatenate([attn, ffn_gain_two, q, kv])
    dg_two = jnp.pad(dg_two, (0, 10 * LAT - dg_two.shape[0])).astype(BF16).reshape(10, LAT)
    rows = jnp.stack(gather_z(jnp.concatenate([rows, dg_two], axis=0)))
    dg_two = jnp.sum(rows[:, 2 * SHARD :].astype(F32), axis=0).reshape(-1)
    rows = rows[:, : 2 * SHARD].reshape(N_Z, 2, SHARD, LAT).transpose(1, 0, 2, 3).reshape(ROWS, LAT)
    packs_two = late_pack(saved_two[5], rows, dg_two, packs_two).reshape(-1, WO)
    in_grad_two, ring_two = tie((in_grad_two, ring_two))
    ring_two = ring_first(ring_two)

    grad_one = in_grad_two.astype(F32)
    d_rows, packs_two = tie((d_mlp_rows(grad_one), packs_two))
    packs_two = lax.psum_scatter(packs_two, "dp", scatter_dimension=0, tiled=True)
    ffn_rows, gu, hidden = saved_one[2:5]
    part, d_gu = ffn_backward(own_one, d_rows, gu, ffn_weights)
    grads_one = ffn_gradients(own_one, d_rows, ffn_rows, d_gu, hidden)
    d_normed_two = scatter_dp(part)
    total_two = ring_last(ring_two)
    rows_two = gather_tokens(layer_out_rows(part_two, saved_two))
    d_normed_two, total_two, rows_two, grads_one = tie((d_normed_two, total_two, rows_two, grads_one))
    d_middle, ffn_gain_one = middle_backward(grad_one, d_normed_two, saved_one, gains_one)
    d_att_own = (RES_SCALE * d_middle).astype(BF16)
    columns = d_att_own.reshape(SHARD, N_DP, SLICE).transpose(1, 0, 2)
    d_attended = gather_tokens(d_att_own)
    part, d_query, d_key_value = attend_back(d_attended, tab, saved_one[-1], attn_one)
    low_one = low_gradients(saved_one[-1], d_query, d_key_value, columns)
    part, low_one = tie((part, low_one))
    low_one = lax.all_to_all(low_one, "dp", 0, 0)
    first = ring_first(ring_pairs(grads_one))
    in_grad_one, _, d_lat_own, dg_one, low_one, first = attention_backward(
        part, d_middle, saved_one, attn_one, gains_one, low_one, first
    )
    d_lat = jnp.broadcast_to(d_lat_own.astype(BF16)[None], (N_DP, SHARD, LAT_ALL))
    columns = gather_tokens(low_one[:, LOW_ROWS:, :SLICE].reshape(TOKENS, SLICE))
    wo_one = wo_gradient(columns, mixed_one)
    low_one = jnp.sum(low_one[:, :LOW_ROWS].astype(F32), axis=0)
    d_lat = lax.all_to_all(d_lat, "dp", 0, 0)
    lat_one = latent_gradient(d_lat, normed_one)
    total_one, lat_one = tie((ring_last(first), lat_one))

    attn, q, kv = dg_one
    dg_one = jnp.concatenate([attn, ffn_gain_one, q, kv])
    dg_one = jnp.pad(dg_one, (0, 3 * D - dg_one.shape[0])).astype(BF16).reshape(3, D)
    got = to_core(jnp.concatenate([jnp.where(core == 0, in_grad_two, in_grad_one), dg_one], axis=0))
    mine = jnp.where(core == 0, in_grad_one, in_grad_two)
    dg_one = add(dg_one, got[SHARD:])
    both = jnp.concatenate(
        [jnp.concatenate([mine, dg_one], axis=0), jnp.pad(got[:SHARD], ((0, 3), (0, 0)))], axis=1
    )
    both = jnp.stack(gather_z(both))
    dg_one = jnp.sum(both[:, SHARD:, :D].astype(F32), axis=0).reshape(-1)
    both = both[:, :SHARD].reshape(PACK, 2 * D)
    input_grad = in_order(both[:, :D], both[:, D:])[None]

    row = jnp.concatenate(gain_vectors(dg_one), axis=1).astype(BF16)
    row = jnp.pad(row[:, None], ((0, 0), (0, 15), (0, 0)))
    total_one = total_one.reshape(N_DP, HALF_ROWS, MATS)
    def from_other(x, layer):
        return lax.ppermute(x, "section", [(1 - layer, layer)])

    layer_out = in_order(*(jnp.where(core == 0, one, two) for one, two in zip(rows_one, rows_two)))
    total_one, pieces, layer_out, input_grad = tie(
        (
            total_one,
            (
                wo_one,
                from_other(wo_one, 0),
                low_one,
                from_other(low_one, 0),
                packs_two,
                from_other(packs_two, 1),
            ),
            layer_out,
            input_grad,
        )
    )
    blocks = jnp.concatenate([total_one, total_two.reshape(N_DP, HALF_ROWS, MATS), row], axis=1)
    blocks = lax.all_to_all(blocks, "dp", 0, 0)
    lat_one = add(lat_one, from_other(lat_one, 0))
    lat_one = sum(x.astype(F32) for x in gather_z(lat_one))
    blocks, attention = tie((blocks, home(core.reshape(1), lat_one, *pieces)))
    qa_grad, kva_grad, qb_grad, kvb_grad, wo_grad, gains = attention
    gains = gains.reshape(-1)
    dg_one = jnp.sum(blocks[:, SLICE].astype(F32), axis=0)
    gate_grad, up_grad, down_grad = ffn_unpack(core.reshape(1), blocks, to_core(blocks))

    def gain_part(one, two, width):
        return jnp.where(core == 0, dg_one[one : one + width], gains[two : two + width])[None]

    return (
        layer_out[None],
        input_grad,
        gain_part(0, 0, SLICE),
        qa_grad[None],
        gain_part(2 * SLICE, 4 * HEAD, QR // N_DP),
        qb_grad[None],
        kva_grad[None],
        gain_part(2 * SLICE + QR // N_DP, 4 * HEAD + QR // N_DP, KVR // N_DP),
        kvb_grad[None],
        wo_grad.T[None],
        gain_part(SLICE, 2 * HEAD, SLICE),
        gate_grad[None],
        up_grad[None],
        down_grad.T[None],
    )


def solution(mesh):
    in_specs = (
        P("dp", None),
        P("dp", None),
        P("dp", None),
        P("section", "dp"),
        P("section", "dp", None),
        P("section", "dp"),
        P("section", "dp", "tensor"),
        P("section", "dp", None),
        P("section", "dp"),
        P("section", "dp", "tensor"),
        P("section", "tensor", "dp"),
        P("section", "dp"),
        P("section", "dp", "tensor"),
        P("section", "dp", "tensor"),
        P("section", "tensor", "dp"),
    )
    out_specs = (
        P("section", "dp", None),
        P("section", "dp", None),
        P("section", "dp"),
        P("section", "dp", None),
        P("section", "dp"),
        P("section", "dp", "tensor"),
        P("section", "dp", None),
        P("section", "dp"),
        P("section", "dp", "tensor"),
        P("section", "tensor", "dp"),
        P("section", "dp"),
        P("section", "dp", "tensor"),
        P("section", "dp", "tensor"),
        P("section", "tensor", "dp"),
    )
    return jax.shard_map(body, mesh=mesh, in_specs=in_specs, out_specs=out_specs, check_vma=False)
```

```python
import math

import jax
import jax.numpy as jnp
from jax import lax
from jax.experimental import pallas as pl
from jax.experimental.pallas import tpu as pltpu
from jax.sharding import PartitionSpec as P

D = 2560
NOPE = 64
ROPE = 32
VD = 64
QR = 768
KVR = 256
PACK = 64
MB = 2
N_DP = 16
N_Z = 4
HEADS = 5
SLICE = D // N_DP
FF_PART = 100
LANES = 128
SHARD = 16
RES_SCALE = 1.4 / math.sqrt(62.0)
EPSILON = 1e-05
SCORE_SCALE = (NOPE + ROPE) ** (-0.5)
BF16 = jnp.bfloat16
F32 = jnp.float32


def dot(a, b):
    return jnp.dot(a, b, preferred_element_type=F32)


def dot_tn(a, b):
    return lax.dot_general(a, b, (((0,), (0,)), ((), ())), preferred_element_type=F32)


def dot_nt(a, b):
    return lax.dot_general(a, b, (((1,), (1,)), ((), ())), preferred_element_type=F32)


def to_core(x):
    return lax.ppermute(x, "section", [(0, 1), (1, 0)])


def z_hop(x, by):
    return lax.ppermute(x, "tensor", [(i, (i + by) % N_Z) for i in range(N_Z)])


def by_core(core, mine, other):
    return jnp.where(core == 0, mine, other), jnp.where(core == 0, other, mine)


def from_here(x):
    return lax.dynamic_slice_in_dim(jnp.concatenate([x, x]), lax.axis_index("tensor"), N_Z, 0)


def from_zero(x):
    at = (N_Z - lax.axis_index("tensor")) % N_Z
    return lax.dynamic_slice_in_dim(jnp.concatenate([x, x]), at, N_Z, 0)


def gather_z(x):
    return [x, z_hop(x, -1), z_hop(x, 2), z_hop(x, 1)]


def gather_tokens(x):
    mine = jnp.concatenate(gather_z(x), axis=0)
    return mine, to_core(mine)


def in_order(mine, other):
    core = lax.axis_index("section")
    shape = (N_Z, SHARD, mine.shape[-1])
    mine, other = from_zero(mine.reshape(shape)), from_zero(other.reshape(shape))
    return jnp.concatenate(by_core(core, mine, other), axis=0).reshape(-1, shape[-1])


def scatter_tokens(part):
    half = part[:PACK].astype(F32) + to_core(part[PACK:]).astype(F32)
    sent = half.astype(BF16)
    total = half[:SHARD]
    for by in (2, 1, 3):
        total = total + z_hop(sent[SHARD * by : SHARD * (by + 1)], by).astype(F32)
    return total


def gather_dp(x):
    copies = jnp.broadcast_to(x[None], (N_DP,) + x.shape)
    return lax.all_to_all(copies, "dp", 0, 0).reshape(N_DP * x.shape[0], x.shape[1])


def scatter_dp(part):
    pieces = lax.all_to_all(part.reshape(N_DP, SHARD, D), "dp", 0, 0)
    return jnp.sum(pieces.astype(F32), axis=0)


def norm_scale(x):
    return lax.rsqrt(jnp.mean(x * x, axis=-1, keepdims=True) + EPSILON)


def norm(x, gain):
    return x * norm_scale(x) * gain


def norm_back(x, gain, d):
    q = norm_scale(x)
    along = jnp.mean(gain * d * x, axis=-1, keepdims=True)
    return q * gain * d - x * (q * q * q) * along, jnp.sum(d * x * q, axis=0)


MATS = 3 * LANES
TOKENS = N_DP * SHARD
FF_VMEM = 56 * 1024 * 1024
FF_SCRATCH = [pltpu.VMEM((N_Z, D, MATS), BF16), pltpu.SemaphoreType.DMA((N_Z,))]


def ffn_copies(own_ref, mine, other, w_ref, sems):
    copies = [pltpu.make_async_copy(mine[z], w_ref.at[z], sems.at[z]) for z in range(N_Z)]
    others = [pltpu.make_async_copy(other[z], w_ref.at[z], sems.at[z]) for z in range(N_Z)]

    @pl.when(own_ref[0] == 1)
    def _():
        for copy in copies:
            copy.start()

    @pl.when(own_ref[0] != 1)
    def _():
        for copy in others:
            copy.start()

    return copies


def down_pair(w_ref, z):
    return jnp.concatenate([w_ref[z, :, 2 * LANES :], w_ref[z + 1, :, 2 * LANES :]], axis=1)


def ffn_forward_kernel(own_ref, n_ref, *refs):
    mine, other = refs[:N_Z], refs[N_Z : 2 * N_Z]
    part_ref, gu_ref, hid_ref, w_ref, sems = refs[2 * N_Z :]
    copies = ffn_copies(own_ref, mine, other, w_ref, sems)
    for z in range(N_Z):
        copies[z].wait()
        gu = dot(n_ref[...], w_ref[z, :, : 2 * LANES])
        gu_ref[:, 2 * LANES * z : 2 * LANES * (z + 1)] = gu
        gate, up = gu[:, :LANES], gu[:, LANES:]
        hid_ref[:, LANES * z : LANES * (z + 1)] = (gate * jax.nn.sigmoid(gate) * up).astype(BF16)
    out = dot_nt(hid_ref[:, : 2 * LANES], down_pair(w_ref, 0))
    part_ref[...] = (out + dot_nt(hid_ref[:, 2 * LANES :], down_pair(w_ref, 2))).astype(BF16)


def ffn_specs(arrays):
    vmem = pl.BlockSpec(memory_space=pltpu.VMEM)
    smem = pl.BlockSpec(memory_space=pltpu.SMEM)
    return [smem] + [vmem] * arrays + [pl.BlockSpec(memory_space=pl.ANY)] * (2 * N_Z)


def ffn_forward(own, rows, weights):
    return pl.pallas_call(
        ffn_forward_kernel,
        out_shape=(
            jax.ShapeDtypeStruct((TOKENS, D), BF16),
            jax.ShapeDtypeStruct((TOKENS, 2 * LANES * N_Z), F32),
            jax.ShapeDtypeStruct((TOKENS, LANES * N_Z), BF16),
        ),
        in_specs=ffn_specs(1),
        out_specs=(pl.BlockSpec(memory_space=pltpu.VMEM),) * 3,
        scratch_shapes=FF_SCRATCH,
        compiler_params=pltpu.CompilerParams(vmem_limit_bytes=FF_VMEM),
        name="ffn_forward",
    )(own, rows, *weights)


def ffn_both_kernel(own_ref, n_ref, dm_ref, *refs):
    mine, other = refs[:N_Z], refs[N_Z : 2 * N_Z]
    part_ref, hid_ref, d_part_ref, dgu_ref, w_ref, sems = refs[2 * N_Z :]
    copies = ffn_copies(own_ref, mine, other, w_ref, sems)
    for z in range(0, N_Z, 2):
        copies[z].wait()
        copies[z + 1].wait()
        d_hidden = dot(dm_ref[...], down_pair(w_ref, z))
        for k in range(2):
            gu = dot(n_ref[...], w_ref[z + k, :, : 2 * LANES])
            gate, up = gu[:, :LANES], gu[:, LANES:]
            s = jax.nn.sigmoid(gate)
            hid_ref[:, LANES * (z + k) : LANES * (z + k + 1)] = (gate * s * up).astype(BF16)
            d_h = d_hidden[:, LANES * k : LANES * (k + 1)]
            at = 2 * LANES * (z + k)
            dgu_ref[:, at : at + LANES] = (d_h * up * (s + gate * s * (1.0 - s))).astype(BF16)
            dgu_ref[:, at + LANES : at + 2 * LANES] = (d_h * (gate * s)).astype(BF16)
    out = None
    for z in range(N_Z):
        term = dot_nt(dgu_ref[:, 2 * LANES * z : 2 * LANES * (z + 1)], w_ref[z, :, : 2 * LANES])
        out = term if z == 0 else out + term
    d_part_ref[...] = out.astype(BF16)
    out = dot_nt(hid_ref[:, : 2 * LANES], down_pair(w_ref, 0))
    part_ref[...] = (out + dot_nt(hid_ref[:, 2 * LANES :], down_pair(w_ref, 2))).astype(BF16)


def ffn_both(own, rows, d_rows, weights):
    widths = (D, LANES * N_Z, D, 2 * LANES * N_Z)
    return pl.pallas_call(
        ffn_both_kernel,
        out_shape=tuple(jax.ShapeDtypeStruct((TOKENS, w), BF16) for w in widths),
        in_specs=ffn_specs(2),
        out_specs=(pl.BlockSpec(memory_space=pltpu.VMEM),) * 4,
        scratch_shapes=FF_SCRATCH,
        compiler_params=pltpu.CompilerParams(vmem_limit_bytes=FF_VMEM),
        name="ffn_both",
    )(own, rows, d_rows, *weights)


HALF_ROWS = SLICE // 2


def ffn_backward_kernel(own_ref, dm_ref, gu_ref, *refs):
    mine, other = refs[:N_Z], refs[N_Z : 2 * N_Z]
    part_ref, dgu_ref, w_ref, sems = refs[2 * N_Z :]
    copies = ffn_copies(own_ref, mine, other, w_ref, sems)
    out = None
    for z in range(0, N_Z, 2):
        copies[z].wait()
        copies[z + 1].wait()
        d_hidden = dot(dm_ref[...], down_pair(w_ref, z))
        for k in range(2):
            columns = slice(2 * LANES * (z + k), 2 * LANES * (z + k) + LANES)
            more = slice(columns.stop, columns.stop + LANES)
            gate, up = gu_ref[:, columns], gu_ref[:, more]
            d_h = d_hidden[:, LANES * k : LANES * (k + 1)]
            s = jax.nn.sigmoid(gate)
            dgu_ref[:, columns] = (d_h * up * (s + gate * s * (1.0 - s))).astype(BF16)
            dgu_ref[:, more] = (d_h * (gate * s)).astype(BF16)
    for z in range(N_Z):
        term = dot_nt(dgu_ref[:, 2 * LANES * z : 2 * LANES * (z + 1)], w_ref[z, :, : 2 * LANES])
        out = term if z == 0 else out + term
    part_ref[...] = out.astype(BF16)


def ffn_backward(own, d_rows, gu, weights):
    return pl.pallas_call(
        ffn_backward_kernel,
        out_shape=(
            jax.ShapeDtypeStruct((TOKENS, D), BF16),
            jax.ShapeDtypeStruct((TOKENS, 2 * LANES * N_Z), BF16),
        ),
        in_specs=ffn_specs(2),
        out_specs=(pl.BlockSpec(memory_space=pltpu.VMEM),) * 2,
        scratch_shapes=FF_SCRATCH,
        compiler_params=pltpu.CompilerParams(vmem_limit_bytes=FF_VMEM),
        name="ffn_backward",
    )(own, d_rows, gu, *weights)


HALF_ROWS = SLICE // 2


def ffn_gradients_kernel(own_ref, dm_ref, n_ref, dgu_ref, hid_ref, *refs):
    outs, grad_ref, out_sems = refs[: 2 * N_Z], refs[2 * N_Z], refs[2 * N_Z + 1]
    core = own_ref[1]

    def store(z, columns, grad):
        grad_ref[z, :, :, :, columns] = grad.reshape(N_DP, 2, HALF_ROWS, grad.shape[1])

    def send(z, keep_at, give_at):
        return [
            pltpu.make_async_copy(grad_ref.at[z, :, core], outs[keep_at], out_sems.at[keep_at]),
            pltpu.make_async_copy(
                grad_ref.at[z, :, 1 - core], outs[N_Z + give_at], out_sems.at[N_Z + give_at]
            ),
        ]

    for z in (2, 0):
        hidden = hid_ref[:, LANES * z : LANES * (z + 2)]
        grad = dot_tn(dm_ref[...], hidden).astype(BF16)
        store(z, slice(2 * LANES, MATS), grad[:, :LANES])
        store(z + 1, slice(2 * LANES, MATS), grad[:, LANES:])
        for k in range(2):
            d_gu = dgu_ref[:, 2 * LANES * (z + k) : 2 * LANES * (z + k + 1)]
            store(z + k, slice(0, 2 * LANES), dot_tn(n_ref[...], d_gu).astype(BF16))
            if z + k in (0, N_Z - 1):
                for copy in send(z + k, z + k, z + k):
                    copy.start()
            else:
                for owner in (1, 0):
                    keep_at = z + k if owner == 1 else 3 - z - k

                    @pl.when(own_ref[0] == owner)
                    def _(at=z + k, keep_at=keep_at):
                        for copy in send(at, keep_at, 3 - keep_at):
                            copy.start()

    for z in range(N_Z):
        for copy in send(z, z, z):
            copy.wait()


def ffn_gradients(own, d_rows, rows, d_gu, hidden):
    vmem = pl.BlockSpec(memory_space=pltpu.VMEM)
    return pl.pallas_call(
        ffn_gradients_kernel,
        out_shape=tuple(jax.ShapeDtypeStruct((N_DP, HALF_ROWS, MATS), BF16) for _ in range(2 * N_Z)),
        in_specs=[pl.BlockSpec(memory_space=pltpu.SMEM)] + [vmem] * 4,
        out_specs=(pl.BlockSpec(memory_space=pl.ANY),) * (2 * N_Z),
        scratch_shapes=[
            pltpu.VMEM((N_Z, N_DP, 2, HALF_ROWS, MATS), BF16),
            pltpu.SemaphoreType.DMA((2 * N_Z,)),
        ],
        compiler_params=pltpu.CompilerParams(vmem_limit_bytes=FF_VMEM),
        cost_estimate=pl.CostEstimate(flops=2 * TOKENS * D * MATS * N_Z, bytes_accessed=1 << 24, transcendentals=0),
        name="ffn_gradients",
    )(own, d_rows, rows, d_gu, hidden)


FF = N_DP * FF_PART
WINDOW = 2 * LANES
FF_PADDED = (FF - FF_PART) // LANES * LANES + WINDOW


def ffn_pack_kernel(gate_ref, up_ref, down_ref, out_ref, wide_ref):
    wide_ref[0, :, :FF] = gate_ref[...].astype(F32)
    wide_ref[1, :, :FF] = up_ref[...].astype(F32)
    wide_ref[2, :, :FF] = down_ref[...].astype(F32)
    valid = lax.broadcasted_iota(jnp.int32, (SLICE, LANES), 1) < FF_PART
    for p in range(N_DP):
        at = FF_PART * p // LANES * LANES
        by = FF_PART * p - at
        for m in range(3):
            window = wide_ref[m, :, at : at + WINDOW]
            if by > 0:
                window = pltpu.roll(window, WINDOW - by, 1)
            block = jnp.where(valid, window[:, :LANES], 0.0)
            out_ref[p, :, LANES * m : LANES * (m + 1)] = block.astype(BF16)


def ffn_pack(w_gate, w_up, w_down):
    return pl.pallas_call(
        ffn_pack_kernel,
        out_shape=jax.ShapeDtypeStruct((N_DP, SLICE, MATS), BF16),
        scratch_shapes=[pltpu.VMEM((3, SLICE, FF_PADDED), F32)],
        compiler_params=pltpu.CompilerParams(vmem_limit_bytes=FF_VMEM),
        name="ffn_pack",
    )(w_gate, w_up, w_down)


def ffn_unpack_kernel(core_ref, blocks_ref, got_ref, gate_ref, up_ref, down_ref):
    first = core_ref[0] == 0
    one, two = slice(0, HALF_ROWS), slice(HALF_ROWS, SLICE)
    for p in range(N_DP):
        columns = slice(FF_PART * p, FF_PART * (p + 1))
        for m, out_ref in enumerate((gate_ref, up_ref, down_ref)):
            lanes = slice(LANES * m, LANES * (m + 1))
            low = jnp.where(first, blocks_ref[p, one, lanes], got_ref[p, two, lanes])
            high = jnp.where(first, got_ref[p, one, lanes], blocks_ref[p, two, lanes])
            out_ref[one, columns] = low[:, :FF_PART].astype(F32)
            out_ref[two, columns] = high[:, :FF_PART].astype(F32)


def ffn_unpack(core, *blocks):
    vmem = pl.BlockSpec(memory_space=pltpu.VMEM)
    return pl.pallas_call(
        ffn_unpack_kernel,
        out_shape=(jax.ShapeDtypeStruct((SLICE, FF), F32),) * 3,
        in_specs=[pl.BlockSpec(memory_space=pltpu.SMEM), vmem, vmem],
        out_specs=(vmem,) * 3,
        compiler_params=pltpu.CompilerParams(vmem_limit_bytes=FF_VMEM),
        name="ffn_unpack",
    )(core, *blocks)


A_ROWS = SLICE + QR // N_DP + KVR // N_DP
A_COLS = 896
LAT = 640
WO_AT = 512
WO = 384
HEAD = 128
ROWS = MB * PACK
QB_ROWS = slice(SLICE, SLICE + QR // N_DP)
KVB_ROWS = slice(SLICE + QR // N_DP, A_ROWS)
E_ROWS = 2 * A_ROWS - SLICE
ATT_VMEM = 48 * 1024 * 1024


def latent_kernel(mine_ref, other_ref, gain_ref, pack_ref, normed_ref, lat_ref, w_ref, sem):
    copy = pltpu.make_async_copy(pack_ref.at[:, 0:SLICE, 0:LAT], w_ref, sem)
    copy.start()
    normed_ref[:PACK] = norm(mine_ref[...].astype(F32), gain_ref[...]).astype(BF16)
    normed_ref[PACK:] = norm(other_ref[...].astype(F32), gain_ref[...]).astype(BF16)
    copy.wait()
    lat_ref[...] = dot(normed_ref[...], w_ref[...].reshape(D, LAT))


def latents(rows, gain, pack):
    vmem = pl.BlockSpec(memory_space=pltpu.VMEM)
    return pl.pallas_call(
        latent_kernel,
        out_shape=(
            jax.ShapeDtypeStruct((ROWS, D), BF16),
            jax.ShapeDtypeStruct((ROWS, LAT), F32),
        ),
        in_specs=[vmem, vmem, vmem, pl.BlockSpec(memory_space=pl.ANY)],
        out_specs=(vmem, vmem),
        scratch_shapes=[pltpu.VMEM((N_DP, SLICE, LAT), BF16), pltpu.SemaphoreType.DMA],
        compiler_params=pltpu.CompilerParams(vmem_limit_bytes=ATT_VMEM),
        name="latents",
    )(*rows, gain, pack)


def weight_copies(pack_ref, qb_ref, kvb_ref, wo_ref, sems):
    sources = (
        pack_ref.at[:, QB_ROWS, 0:LAT],
        pack_ref.at[:, KVB_ROWS, 0:LAT],
        pack_ref.at[:, 0:SLICE, WO_AT : WO_AT + WO],
    )
    targets = (qb_ref, kvb_ref, wo_ref)
    copies = [pltpu.make_async_copy(a, b, sems.at[i]) for i, (a, b) in enumerate(zip(sources, targets))]
    for copy in copies:
        copy.start()
    return copies


def weight_scratch():
    return [
        pltpu.VMEM((N_DP, QR // N_DP, LAT), BF16),
        pltpu.VMEM((N_DP, KVR // N_DP, LAT), BF16),
        pltpu.VMEM((N_DP, SLICE, WO), BF16),
        pltpu.SemaphoreType.DMA((3,)),
    ]


def lanes_of(x):
    return lax.broadcasted_iota(jnp.int32, x.shape, 1)


def turn(x, tab_ref):
    return (
        x * tab_ref[0]
        + pltpu.roll(x, HEAD - ROPE // 2, 1) * tab_ref[1]
        + pltpu.roll(x, ROPE // 2, 1) * tab_ref[2]
    )


def turn_back(x, tab_ref):
    return (
        x * tab_ref[0]
        - pltpu.roll(x, HEAD - ROPE // 2, 1) * tab_ref[1]
        - pltpu.roll(x, ROPE // 2, 1) * tab_ref[2]
    )


def head_columns(h):
    return slice(HEAD * h, HEAD * (h + 1))


def probs_of(query, key, tab_ref):
    scores = jnp.where(tab_ref[3] < 0.0, -1e30, dot_nt(query, key) * SCORE_SCALE)
    weight = jnp.exp(scores - jnp.max(scores, axis=-1, keepdims=True))
    return weight / jnp.sum(weight, axis=-1, keepdims=True)


def attend_kernel(
    core_ref, mine_ref, other_ref, tab_ref, gq_ref, gkv_ref, pack_ref,
    part_ref, sq_ref, comp_ref, q_ref, kv_ref, kr_ref, mixed_ref, lat_ref,
    qb_ref, kvb_ref, wo_ref, sems,
):
    copies = weight_copies(pack_ref, qb_ref, kvb_ref, wo_ref, sems)
    zero = core_ref[0] == 0
    other = jnp.concatenate([other_ref[PACK:], other_ref[:PACK]], axis=0)
    second = jnp.where(zero, other, mine_ref[...])
    first = jnp.where(zero, mine_ref[:, :512], other[:, :512])
    latent_q = jnp.concatenate([first, second[:, :256]], axis=1)
    lat_ref[:, :QR] = latent_q[:SHARD]
    lat_ref[:, QR:] = second[:SHARD, 256:512]
    sq_ref[...] = norm(latent_q, gq_ref[...]).astype(BF16)
    comp_ref[...] = norm(second[:, 256:512], gkv_ref[...]).astype(BF16)
    rope = pltpu.roll(second[:, 512:640], NOPE, 1)
    rope = jnp.where(lanes_of(rope) < NOPE, 0.0, turn(rope, tab_ref)).astype(BF16)
    kr_ref[...] = rope
    copies[0].wait()
    query = dot(sq_ref[...], qb_ref[...].reshape(QR, LAT))
    for h in range(HEADS):
        q_ref[:, head_columns(h)] = turn(query[:, head_columns(h)], tab_ref).astype(BF16)
    copies[1].wait()
    kv_ref[...] = dot(comp_ref[...], kvb_ref[...].reshape(KVR, LAT)).astype(BF16)
    heads = []
    for h in range(HEADS):
        kv = kv_ref[:, head_columns(h)]
        key = jnp.where(lanes_of(kv) < NOPE, kv, rope)
        probs = probs_of(q_ref[:, head_columns(h)], key, tab_ref)
        heads.append(dot(probs.astype(BF16), kv))
    low = lanes_of(heads[0]) < NOPE
    tiles = [jnp.where(low, 0.0, heads[0])]
    tiles += [jnp.where(low, pltpu.roll(heads[i], NOPE, 1), heads[i + 1]) for i in (1, 3)]
    mixed_ref[...] = jnp.concatenate(tiles, axis=1).astype(BF16)
    copies[2].wait()
    part_ref[...] = dot_nt(mixed_ref[...], wo_ref[...].reshape(D, WO)).astype(BF16)


def attend(core, mine, other, tab, g_q, g_kv, pack):
    vmem = pl.BlockSpec(memory_space=pltpu.VMEM)
    widths = (D, QR, KVR, LAT, LAT, HEAD, WO)
    return pl.pallas_call(
        attend_kernel,
        out_shape=tuple(jax.ShapeDtypeStruct((ROWS, w), BF16) for w in widths)
        + (jax.ShapeDtypeStruct((SHARD, QR + KVR), F32),),
        in_specs=[pl.BlockSpec(memory_space=pltpu.SMEM)] + [vmem] * 5 + [pl.BlockSpec(memory_space=pl.ANY)],
        out_specs=(vmem,) * (len(widths) + 1),
        scratch_shapes=weight_scratch(),
        compiler_params=pltpu.CompilerParams(vmem_limit_bytes=ATT_VMEM),
        name="attend",
    )(core, mine, other, tab, g_q, g_kv, pack)


def attend_back_kernel(
    mine_ref, other_ref, tab_hbm, q_hbm, kv_hbm, kr_hbm, pack_ref,
    part_ref, dq_ref, dkv_ref,
    tab_ref, q_ref, kv_ref, kr_ref, in_sems, qb_ref, kvb_ref, wo_ref, sems,
):
    pairs = ((kv_hbm, kv_ref), (kr_hbm, kr_ref), (q_hbm, q_ref), (tab_hbm, tab_ref))
    inputs = [pltpu.make_async_copy(a, b, in_sems.at[i]) for i, (a, b) in enumerate(pairs)]
    for copy in inputs:
        copy.start()
    copies = weight_copies(pack_ref, qb_ref, kvb_ref, wo_ref, sems)
    d_att = jnp.concatenate([mine_ref[...], other_ref[...]], axis=0)
    copies[2].wait()
    d_mixed = dot(d_att, wo_ref[...].reshape(D, WO))
    for copy in inputs:
        copy.wait()
    rope = kr_ref[...]
    d_rope = jnp.zeros((ROWS, HEAD), F32)
    for h in range(HEADS):
        kv = kv_ref[:, head_columns(h)]
        low = lanes_of(kv) < NOPE
        key = jnp.where(low, kv, rope)
        query = q_ref[:, head_columns(h)]
        probs = probs_of(query, key, tab_ref)
        tile = d_mixed[:, head_columns((h + 1) // 2)]
        if h % 2 == 1:
            tile = pltpu.roll(tile, NOPE, 1)
        tile = jnp.where(low, 0.0, tile).astype(BF16)
        d_probs = dot_nt(tile, kv)
        d_scores = probs * (d_probs - jnp.sum(probs * d_probs, axis=-1, keepdims=True))
        d_scores = d_scores.astype(BF16)
        d_query = dot(d_scores, key) * SCORE_SCALE
        d_key = dot_tn(d_scores, query) * SCORE_SCALE
        d_value = dot_tn(probs.astype(BF16), tile)
        dq_ref[:, head_columns(h)] = turn_back(d_query, tab_ref).astype(BF16)
        dkv_ref[:, head_columns(h)] = jnp.where(low, d_key, d_value).astype(BF16)
        d_rope = d_rope + d_key
    d_rope = jnp.where(lanes_of(d_rope) < NOPE, 0.0, turn_back(jnp.where(lanes_of(d_rope) < NOPE, 0.0, d_rope), tab_ref))
    copies[0].wait()
    copies[1].wait()
    part_ref[:, :QR] = dot_nt(dq_ref[...], qb_ref[...].reshape(QR, LAT)).astype(BF16)
    part_ref[:, QR : QR + KVR] = dot_nt(dkv_ref[...], kvb_ref[...].reshape(KVR, LAT)).astype(BF16)
    part_ref[:, QR + KVR :] = d_rope.astype(BF16)


def attend_back(d_attended, tab, saved, pack):
    vmem = pl.BlockSpec(memory_space=pltpu.VMEM)
    return pl.pallas_call(
        attend_back_kernel,
        out_shape=(
            jax.ShapeDtypeStruct((ROWS, QR + KVR + HEAD), BF16),
            jax.ShapeDtypeStruct((ROWS, LAT), BF16),
            jax.ShapeDtypeStruct((ROWS, LAT), BF16),
        ),
        in_specs=[vmem] * 2 + [pl.BlockSpec(memory_space=pl.ANY)] * 5,
        out_specs=(vmem,) * 3,
        scratch_shapes=[
            pltpu.VMEM((4, ROWS, HEAD), F32),
            pltpu.VMEM((ROWS, LAT), BF16),
            pltpu.VMEM((ROWS, LAT), BF16),
            pltpu.VMEM((ROWS, HEAD), BF16),
            pltpu.SemaphoreType.DMA((4,)),
        ]
        + weight_scratch(),
        compiler_params=pltpu.CompilerParams(vmem_limit_bytes=ATT_VMEM),
        name="attend_back",
    )(*d_attended, tab, *saved[2:5], pack)


def attend_gradients_kernel(
    mine_ref, other_ref, dq_ref, dkv_ref, sq_hbm, comp_hbm, mixed_hbm,
    out_ref,
    early_ref, sq_ref, comp_ref, mixed_ref, sems,
):
    pairs = ((mixed_hbm, mixed_ref), (sq_hbm, sq_ref), (comp_hbm, comp_ref))
    copies = [pltpu.make_async_copy(a, b, sems.at[i]) for i, (a, b) in enumerate(pairs)]
    for copy in copies:
        copy.start()
    d_att = jnp.concatenate([mine_ref[...], other_ref[...]], axis=0)
    copies[0].wait()
    wo_grad = dot_tn(d_att, mixed_ref[...]).astype(BF16)
    early_ref[:, :SLICE, :] = wo_grad.reshape(N_DP, SLICE, WO)
    copies[1].wait()
    qb_grad = dot_tn(sq_ref[...], dq_ref[...]).astype(BF16).reshape(N_DP, QR // N_DP, LAT)
    copies[2].wait()
    kvb_grad = dot_tn(comp_ref[...], dkv_ref[...]).astype(BF16).reshape(N_DP, KVR // N_DP, LAT)
    early_ref[:, QB_ROWS, :] = qb_grad[:, :, :WO]
    early_ref[:, KVB_ROWS, :] = kvb_grad[:, :, :WO]
    more = slice(A_ROWS, A_ROWS + QR // N_DP)
    early_ref[:, more, : LAT - WO] = qb_grad[:, :, WO:]
    early_ref[:, more.stop :, : LAT - WO] = kvb_grad[:, :, WO:]
    early_ref[:, A_ROWS:, LAT - WO :] = jnp.zeros((N_DP, E_ROWS - A_ROWS, 2 * WO - LAT), BF16)
    copy = pltpu.make_async_copy(early_ref, out_ref.at[:, :E_ROWS], sems.at[3])
    copy.start()
    copy.wait()


def attend_gradients(d_attended, saved, d_query, d_key_value):
    vmem = pl.BlockSpec(memory_space=pltpu.VMEM)
    hbm = pl.BlockSpec(memory_space=pl.ANY)
    return pl.pallas_call(
        attend_gradients_kernel,
        out_shape=jax.ShapeDtypeStruct((N_DP, E_ROWS + L_ROWS, WO), BF16),
        in_specs=[vmem] * 4 + [hbm] * 3,
        out_specs=hbm,
        scratch_shapes=[
            pltpu.VMEM((N_DP, E_ROWS, WO), BF16),
            pltpu.VMEM((ROWS, QR), BF16),
            pltpu.VMEM((ROWS, KVR), BF16),
            pltpu.VMEM((ROWS, WO), BF16),
            pltpu.SemaphoreType.DMA((4,)),
        ],
        compiler_params=pltpu.CompilerParams(vmem_limit_bytes=ATT_VMEM),
        name="attend_gradients",
    )(*d_attended, d_query, d_key_value, saved[0], saved[1], saved[5])


def low_gradients_kernel(
    dq_ref, dkv_ref, columns_ref, sq_hbm, comp_hbm, out_ref, sq_ref, comp_ref, sems
):
    copies = [
        pltpu.make_async_copy(sq_hbm, sq_ref, sems.at[0]),
        pltpu.make_async_copy(comp_hbm, comp_ref, sems.at[1]),
    ]
    for copy in copies:
        copy.start()
    copies[0].wait()
    grad = dot_tn(sq_ref[...], dq_ref[...]).astype(BF16)
    out_ref[:, : QR // N_DP, :] = grad.reshape(N_DP, QR // N_DP, LAT)
    copies[1].wait()
    grad = dot_tn(comp_ref[...], dkv_ref[...]).astype(BF16)
    out_ref[:, QR // N_DP : LOW_ROWS, :] = grad.reshape(N_DP, KVR // N_DP, LAT)
    out_ref[:, LOW_ROWS:, :SLICE] = columns_ref[...]
    out_ref[:, LOW_ROWS:, SLICE:] = jnp.zeros((N_DP, SHARD, LAT - SLICE), BF16)


LOW_ROWS = A_ROWS - SLICE


def low_gradients(saved, d_query, d_key_value, columns):
    vmem = pl.BlockSpec(memory_space=pltpu.VMEM)
    hbm = pl.BlockSpec(memory_space=pl.ANY)
    return pl.pallas_call(
        low_gradients_kernel,
        out_shape=jax.ShapeDtypeStruct((N_DP, LOW_ROWS + SHARD, LAT), BF16),
        in_specs=[vmem, vmem, vmem, hbm, hbm],
        out_specs=vmem,
        scratch_shapes=[
            pltpu.VMEM((ROWS, QR), BF16),
            pltpu.VMEM((ROWS, KVR), BF16),
            pltpu.SemaphoreType.DMA((2,)),
        ],
        compiler_params=pltpu.CompilerParams(vmem_limit_bytes=ATT_VMEM),
        name="low_gradients",
    )(d_query, d_key_value, columns, saved[0], saved[1])


def wo_gradient_kernel(mine_ref, other_ref, mixed_hbm, out_ref, mixed_ref, sem):
    copy = pltpu.make_async_copy(mixed_hbm, mixed_ref, sem)
    copy.start()
    copy.wait()
    total = None
    for i in range(2 * N_Z):
        d_ref = mine_ref if i < N_Z else other_ref
        d_att = d_ref[TOKENS * (i % N_Z) : TOKENS * (i % N_Z + 1)]
        mixed = mixed_ref[:, SHARD * i : SHARD * (i + 1), :].reshape(TOKENS, WO)
        term = dot_tn(d_att, mixed)
        total = term if total is None else total + term
    out_ref[...] = total


def wo_gradient(d_attended, mixed):
    vmem = pl.BlockSpec(memory_space=pltpu.VMEM)
    return pl.pallas_call(
        wo_gradient_kernel,
        out_shape=jax.ShapeDtypeStruct((SLICE, WO), F32),
        in_specs=[vmem, vmem, pl.BlockSpec(memory_space=pl.ANY)],
        out_specs=vmem,
        scratch_shapes=[pltpu.VMEM((N_DP, ROWS, WO), BF16), pltpu.SemaphoreType.DMA],
        compiler_params=pltpu.CompilerParams(vmem_limit_bytes=ATT_VMEM),
        name="wo_gradient",
    )(*d_attended, mixed)


LAT_ALL = QR + KVR + HEAD


def latent_gradient_kernel(rows_ref, normed_ref, out_ref):
    rows = rows_ref[...].reshape(TOKENS, LAT_ALL)
    out_ref[...] = dot_tn(normed_ref[...].reshape(TOKENS, SLICE), rows).astype(BF16)


def latent_gradient(rows, normed):
    return pl.pallas_call(
        latent_gradient_kernel,
        out_shape=jax.ShapeDtypeStruct((SLICE, LAT_ALL), BF16),
        compiler_params=pltpu.CompilerParams(vmem_limit_bytes=ATT_VMEM),
        name="latent_gradient",
    )(rows, normed)


L_ROWS = 2 * SLICE


def late_kernel(rows_ref, gains_ref, normed_hbm, packs_ref, out_ref, late_ref, normed_ref, sem, out_sem):
    copy = pltpu.make_async_copy(normed_hbm, normed_ref, sem)
    copy.start()
    late_ref[:, SLICE : SLICE + 16, 2 * HEAD :] = gains_ref[...]
    late_ref[:, SLICE + 16 :, 2 * HEAD :] = jnp.zeros((N_DP, SLICE - 16, HEAD), BF16)
    copy.wait()
    grad = dot_tn(normed_ref[...], rows_ref[...]).astype(BF16)
    late_ref[:, :SLICE, :] = grad[:, :WO].reshape(N_DP, SLICE, WO)
    late_ref[:, SLICE:, : 2 * HEAD] = grad[:, WO:].reshape(N_DP, SLICE, 2 * HEAD)
    copy = pltpu.make_async_copy(late_ref, out_ref.at[:, E_ROWS:], out_sem)
    copy.start()
    copy.wait()


def gain_vectors(gains):
    parts = (gains[:D], gains[D : 2 * D], gains[2 * D : 2 * D + QR], gains[2 * D + QR : 2 * D + QR + KVR])
    return [x.reshape(N_DP, -1) for x in parts]


def late_pack(normed, rows, gains, packs):
    attn, ffn, q, kv = gain_vectors(gains)
    wide = ((0, 0), (0, 2 * HEAD - SLICE))
    row = jnp.concatenate([jnp.pad(attn, wide), jnp.pad(ffn, wide), q, kv], axis=1)
    row = jnp.pad(row, ((0, 0), (0, 16 * HEAD - row.shape[1]))).reshape(N_DP, 16, HEAD).astype(BF16)
    vmem = pl.BlockSpec(memory_space=pltpu.VMEM)
    hbm = pl.BlockSpec(memory_space=pl.ANY)
    return pl.pallas_call(
        late_kernel,
        out_shape=jax.ShapeDtypeStruct(packs.shape, BF16),
        in_specs=[vmem, vmem, hbm, hbm],
        out_specs=hbm,
        scratch_shapes=[
            pltpu.VMEM((N_DP, L_ROWS, WO), BF16),
            pltpu.VMEM((ROWS, D), BF16),
            pltpu.SemaphoreType.DMA,
            pltpu.SemaphoreType.DMA,
        ],
        input_output_aliases={3: 0},
        compiler_params=pltpu.CompilerParams(vmem_limit_bytes=ATT_VMEM),
        name="late_in_packs",
    )(rows, row, normed, packs)


def normed_back_kernel(d_ref, pack_ref, out_ref, w_ref, sem):
    copy = pltpu.make_async_copy(pack_ref.at[:, 0:SLICE, 0:LAT], w_ref, sem)
    copy.start()
    copy.wait()
    out_ref[...] = dot_nt(d_ref[...], w_ref[...].reshape(D, LAT))


def normed_back(d_latent, pack):
    vmem = pl.BlockSpec(memory_space=pltpu.VMEM)
    return pl.pallas_call(
        normed_back_kernel,
        out_shape=jax.ShapeDtypeStruct((d_latent.shape[0], D), F32),
        in_specs=[vmem, pl.BlockSpec(memory_space=pl.ANY)],
        out_specs=vmem,
        scratch_shapes=[pltpu.VMEM((N_DP, SLICE, LAT), BF16), pltpu.SemaphoreType.DMA],
        compiler_params=pltpu.CompilerParams(vmem_limit_bytes=ATT_VMEM),
        name="normed_back",
    )(d_latent, pack)


def home_kernel(
    core_ref, lat_ref, wo1_ref, wo1_got_ref, low_ref, low_got_ref, packs_ref, packs_got_ref,
    qa_ref, kva_ref, qb_ref, kvb_ref, wo_ref, gain_ref, heads_ref,
):
    first = core_ref[0] == 0

    def pick(one, two):
        return jnp.where(first, one.astype(F32), two.astype(F32))

    wide = slice(0, SLICE)
    late, more = slice(E_ROWS, E_ROWS + SLICE), slice(E_ROWS + SLICE, E_ROWS + L_ROWS)
    gain_rows = slice(E_ROWS + SLICE, E_ROWS + SLICE + 16)
    gain_ref[...] = (
        packs_ref[gain_rows, 2 * HEAD :].astype(F32) + packs_got_ref[gain_rows, 2 * HEAD :].astype(F32)
    )
    qa_ref[:, :WO] = pick(lat_ref[wide, :WO], packs_got_ref[late])
    qa_ref[:, WO:512] = pick(lat_ref[wide, WO:512], packs_got_ref[more, :HEAD])
    qa_ref[:, 512:] = pick(lat_ref[wide, 512:QR], packs_ref[late, : 2 * HEAD])
    kva_ref[:, :HEAD] = pick(lat_ref[wide, QR : QR + HEAD], packs_ref[late, 2 * HEAD :])
    kva_ref[:, HEAD:KVR] = pick(lat_ref[wide, QR + HEAD : QR + KVR], packs_ref[more, :HEAD])
    kva_ref[:, KVR:] = pick(lat_ref[wide, QR + KVR :], packs_ref[more, HEAD : 2 * HEAD])[:, :ROPE]
    at = WO - HEADS * VD
    low, high = pick(wo1_ref[...], packs_got_ref[wide]), pick(wo1_got_ref[...], packs_ref[wide])
    wo_ref[...] = jnp.concatenate([low[:, at:], high[:, at:]], axis=1)
    heads_ref[...] = jnp.zeros(heads_ref.shape, F32)
    qb_rows, kvb_rows = slice(0, QR // N_DP), slice(QR // N_DP, A_ROWS - SLICE)
    valid = lax.broadcasted_iota(jnp.int32, (QR // N_DP, HEAD), 1) < NOPE + ROPE
    for j in range(HEADS):
        start = SLICE if j < 3 else A_ROWS
        columns, packed = slice(HEAD * j, HEAD * (j + 1)), slice(HEAD * (j % 3), HEAD * (j % 3 + 1))
        for rows in (qb_rows, kvb_rows):
            at_rows = slice(start + rows.start, start + rows.stop)
            low = pick(low_ref[rows, columns], packs_got_ref[at_rows, packed])
            high = pick(low_got_ref[rows, columns], packs_ref[at_rows, packed])
            for k, tile in enumerate((low, high)):
                if rows == kvb_rows:
                    kvb_ref[:, HEAD * (HEADS * k + j) : HEAD * (HEADS * k + j + 1)] = tile
                    continue
                begin = (NOPE + ROPE) * (HEADS * k + j)
                at = begin // HEAD * HEAD
                tile = jnp.where(valid, tile, 0.0)
                window = jnp.concatenate([tile, jnp.zeros_like(tile)], axis=1)
                if begin > at:
                    window = pltpu.roll(window, begin - at, 1)
                heads_ref[:, at : at + 2 * HEAD] += window
    qb_ref[...] = heads_ref[:, : 2 * HEADS * (NOPE + ROPE)]


def home(core, *pieces):
    vmem = pl.BlockSpec(memory_space=pltpu.VMEM)
    shapes = (
        (SLICE, QR),
        (SLICE, KVR + ROPE),
        (QR // N_DP, 2 * HEADS * (NOPE + ROPE)),
        (KVR // N_DP, 2 * LAT),
        (SLICE, 2 * HEADS * VD),
        (16, HEAD),
    )
    return pl.pallas_call(
        home_kernel,
        out_shape=tuple(jax.ShapeDtypeStruct(x, F32) for x in shapes),
        in_specs=[pl.BlockSpec(memory_space=pltpu.SMEM)] + [vmem] * len(pieces),
        out_specs=(vmem,) * len(shapes),
        scratch_shapes=[pltpu.VMEM((QR // N_DP, 1152), F32)],
        compiler_params=pltpu.CompilerParams(vmem_limit_bytes=ATT_VMEM),
        name="home",
    )(core, *pieces)


def attention_pack_kernel(
    core_ref, qa_ref, qb_ref, kva_ref, kvb_ref, wo_ref, ga_ref, gf_ref, gq_ref, gk_ref,
    keep_ref, give_ref, heads_ref,
):
    half = HEADS * VD
    first = core_ref[0] == 0

    def put(rows, columns, zero, one):
        keep_ref[rows, columns] = jnp.where(first, zero, one).astype(BF16)
        give_ref[rows, columns] = jnp.where(first, one, zero).astype(BF16)

    def blank(rows, columns):
        zero = jnp.zeros((rows.stop - rows.start, columns.stop - columns.start), BF16)
        keep_ref[rows, columns] = zero
        give_ref[rows, columns] = zero

    wide = slice(0, SLICE)
    qa = qa_ref[...].astype(F32)
    put(wide, slice(0, 256), qa[:, :256], qa[:, 512:])
    put(wide, slice(256, 512), qa[:, 256:512], kva_ref[:, :256].astype(F32))
    wo_t = wo_ref[...].astype(F32)
    tail = jnp.zeros((SLICE, WO), F32)
    rope = jnp.concatenate([kva_ref[:, 256:].astype(F32), jnp.zeros((SLICE, WO - ROPE), F32)], axis=1)
    low = jnp.concatenate([tail[:, : WO - half], wo_t[:, :half]], axis=1)
    high = jnp.concatenate([tail[:, : WO - half], wo_t[:, half:]], axis=1)
    put(wide, slice(WO_AT, A_COLS), low, high + rope)
    heads_ref[:, : 2 * HEADS * (NOPE + ROPE)] = qb_ref[...].astype(F32)
    rows = QB_ROWS.stop - QB_ROWS.start
    valid = lax.broadcasted_iota(jnp.int32, (rows, HEAD), 1) < NOPE + ROPE
    tiles = []
    for j in range(2 * HEADS):
        at = (NOPE + ROPE) * j // HEAD * HEAD
        by = (NOPE + ROPE) * j - at
        window = heads_ref[:, at : at + 2 * HEAD]
        if by > 0:
            window = pltpu.roll(window, 2 * HEAD - by, 1)
        tiles.append(jnp.where(valid, window[:, :HEAD], 0.0))
    for j in range(HEADS):
        put(QB_ROWS, slice(HEAD * j, HEAD * (j + 1)), tiles[j], tiles[HEADS + j])
    gain_rows = [jnp.concatenate([g[...].astype(F32), jnp.zeros((1, 256 - SLICE), F32)], axis=1) for g in (ga_ref, gf_ref)]
    last = [gq_ref[...].astype(F32), gk_ref[...].astype(F32), jnp.zeros((1, 256 - 64), F32)]
    gain_rows.append(jnp.concatenate(last, axis=1))
    gains = jnp.concatenate(gain_rows + [jnp.zeros((rows - 3, 256), F32)], axis=0)
    put(QB_ROWS, slice(LAT, A_COLS), gains, gains)
    kvb = kvb_ref[...].astype(F32)
    put(KVB_ROWS, slice(0, LAT), kvb[:, :LAT], kvb[:, LAT:])
    blank(KVB_ROWS, slice(LAT, A_COLS))


def attention_packs(core, *weights):
    vmem = pl.BlockSpec(memory_space=pltpu.VMEM)
    return pl.pallas_call(
        attention_pack_kernel,
        out_shape=(jax.ShapeDtypeStruct((A_ROWS, A_COLS), BF16),) * 2,
        in_specs=[pl.BlockSpec(memory_space=pltpu.SMEM)] + [vmem] * len(weights),
        out_specs=(vmem, vmem),
        scratch_shapes=[pltpu.VMEM((QR // N_DP, 1152), F32)],
        compiler_params=pltpu.CompilerParams(vmem_limit_bytes=ATT_VMEM),
        name="attention_pack",
    )(core, *weights)


def attention_gains(pack):
    gains = pack[:, SLICE : SLICE + 3, LAT:].astype(F32)
    return dict(
        attn=gains[:, 0, :SLICE].reshape(1, D),
        ffn=gains[:, 1, :SLICE].reshape(1, D),
        q=gains[:, 2, : QR // N_DP].reshape(1, QR),
        kv=gains[:, 2, QR // N_DP : QR // N_DP + KVR // N_DP].reshape(1, KVR),
    )


def head_tables(seq_lengths):
    core, t = lax.axis_index("section"), lax.axis_index("tensor")
    at = jnp.arange(ROWS, dtype=jnp.int32)
    pack = (core + at // PACK) % 2
    row = (t + at % PACK // SHARD) % N_Z * SHARD + at % SHARD
    lengths = jnp.where(pack[:, None] == 0, seq_lengths[:1], seq_lengths[1:])
    past_end = row[:, None] >= jnp.cumsum(lengths, axis=1)
    segment = jnp.sum(past_end.astype(jnp.int32), axis=1)
    position = (row - jnp.sum(jnp.where(past_end, lengths, 0), axis=1)).astype(F32)
    frequency = 10000.0 ** (-2.0 * jnp.arange(ROPE // 2, dtype=F32) / ROPE)
    angles = position[:, None] * frequency[None, :]
    cosine, sine = jnp.cos(angles), jnp.sin(angles)
    sequence = pack * PACK + segment
    allowed = (sequence[:, None] == sequence[None, :]) & (row[None, :] <= row[:, None])

    def tile(*pieces):
        x = jnp.concatenate(pieces, axis=1)
        return jnp.pad(x, ((0, 0), (0, HEAD - x.shape[1])))

    ones, none = jnp.ones((ROWS, NOPE), F32), jnp.zeros((ROWS, NOPE), F32)
    bias = jnp.where(allowed, 0.0, -1.0).astype(F32)
    return jnp.stack(
        [tile(ones, cosine, cosine), tile(none, -sine), tile(none, jnp.zeros_like(sine), sine), bias]
    )


def ring_hop(x, by):
    pairs = [
        (c * N_Z + t, c * N_Z + (t + (by if c == 0 else -by)) % N_Z) for c in range(2) for t in range(N_Z)
    ]
    return lax.ppermute(x, ("section", "tensor"), pairs)


def add(*terms):
    return sum(x.astype(F32) for x in terms).astype(BF16)


def ring_pairs(pieces):
    got = [to_core(x) for x in pieces[N_Z:]]
    return add(pieces[3], got[3]), add(pieces[2], got[2]), (pieces[1], got[1]), (pieces[0], got[0])


def ring_first(pairs):
    far, after, near, mine = pairs
    return ring_hop(far, -1), ring_hop(after, 1), near, mine


def ring_last(first):
    far, after, near, mine = first
    return add(*mine, after, ring_hop(add(*near, far), -1))


tie = lax.optimization_barrier


def attention_forward(normed, latent, x_own, pack, gains, tab):
    core = lax.axis_index("section").reshape(1)
    part, *saved, latent_own = attend(
        core, latent, to_core(latent), tab, gains["q"], gains["kv"], pack
    )
    middle = x_own + RES_SCALE * scatter_tokens(part)
    return middle, (normed, latent_own, saved)


def layer_forward(own, x_own, middle, saved, gains, ffn_weights, far=None):
    ffn_rows = gather_dp(norm(middle, gains["ffn"]).astype(BF16))
    if far is not None:
        ffn_rows, far = tie((ffn_rows, far))
        ffn_weights = ffn_weights[:3] + [far] + ffn_weights[3:] + [to_core(far)]
    part, gu, hidden = ffn_forward(own, ffn_rows, ffn_weights)
    return part, (x_own, middle, ffn_rows, gu, hidden) + saved, ffn_weights


def layer_out_rows(part, saved):
    return (saved[1] + RES_SCALE * part).astype(BF16)


def middle_backward(grad_own, d_normed_two, saved, gains):
    d_middle, ffn_gain = norm_back(saved[1], gains["ffn"], d_normed_two)
    return d_middle + grad_own, ffn_gain


def attention_backward(part, d_middle, saved, pack, gains, also=(), after=()):
    core = lax.axis_index("section")
    x_own, _, _, _, _, _, latent_own, _ = saved
    d_latent, also = tie((scatter_tokens(part), also))
    d_q, q_gain = norm_back(latent_own[:, :QR], gains["q"], d_latent[:, :QR])
    d_c, kv_gain = norm_back(latent_own[:, QR:], gains["kv"], d_latent[:, QR : QR + KVR])
    d_rope = d_latent[:, QR + KVR + NOPE : QR + KVR + NOPE + ROPE]
    blank = jnp.zeros((SHARD, HEAD), F32)
    d_first = jnp.concatenate([d_q[:, :512], blank], axis=1).astype(BF16)
    d_second = jnp.concatenate([d_q[:, 512:], d_c, d_rope, blank[:, ROPE:]], axis=1).astype(BF16)
    mine = jnp.where(core == 0, d_first, d_second)
    other = to_core(jnp.where(core == 0, d_second, d_first))
    both = jnp.concatenate([mine, other], axis=0)
    both, after = tie((both, after))
    part = normed_back(both, pack)
    d_normed = part[:SHARD] + to_core(part[SHARD:])
    d_block, attn_gain = norm_back(x_own, gains["attn"], d_normed)
    d_block = (d_block + d_middle).astype(BF16)
    return d_block, both, jnp.concatenate([d_q, d_c, d_rope, blank[:, ROPE:]], axis=1), (attn_gain, q_gain, kv_gain), also, after


def scatter_sum(x):
    return jnp.sum(lax.all_to_all(x, "dp", 0, 0).astype(F32), axis=0)


def body(
    layer_input,
    cotangent,
    seq_lengths,
    g_attn,
    w_qa,
    g_q,
    w_qb,
    w_kva,
    g_kv,
    w_kvb,
    w_o,
    g_ffn,
    w_gate,
    w_up,
    w_down,
):
    core = lax.axis_index("section")
    blocks = ffn_pack(w_gate[0], w_up[0], w_down[0].T)
    blocks, w_qa = tie((blocks, w_qa))
    keep, give = attention_packs(
        core.reshape(1), w_qa[0], w_qb[0], w_kva[0], w_kvb[0], w_o[0].T, g_attn, g_ffn, g_q, g_kv
    )
    attn_one, attn_two = by_core(core, keep, to_core(give))
    attn_one = lax.all_gather(attn_one, "dp")

    blocks = lax.all_to_all(blocks, "dp", 0, 0)
    tab = head_tables(seq_lengths)
    blocks, cotangent, layer_input = lax.optimization_barrier((blocks, cotangent, layer_input))
    weights = blocks.reshape(D, MATS)
    near, after = ring_hop(weights, 1), ring_hop(weights, -1)

    def token_rows(x):
        packs = x.reshape(2, N_Z, SHARD, D)
        first, second = by_core(core, packs[0], packs[1])
        return from_here(first).reshape(PACK, D), from_here(second).reshape(PACK, D)

    def d_mlp_rows(grad):
        return gather_dp((RES_SCALE * grad).astype(BF16))

    def d_attended_rows(d_middle):
        return gather_tokens((RES_SCALE * d_middle).astype(BF16))

    cot_own = token_rows(cotangent)[0][:SHARD].astype(F32)
    attn_one, tab, near, after = tie((attn_one, tab, near, after))
    gains_one = attention_gains(attn_one)
    own_one = jnp.stack([(core == 0).astype(jnp.int32), core])
    own_two = jnp.stack([(core == 1).astype(jnp.int32), core])

    rows = token_rows(layer_input)
    x_own = rows[0][:SHARD].astype(F32)
    normed, latent = latents(rows, gains_one["attn"], attn_one)
    wide = (A_COLS, A_COLS, D - 2 * A_COLS)
    shared = jnp.concatenate([(RES_SCALE * cot_own).astype(BF16), normed[:SHARD]], axis=0)
    shared = [shared[:, :A_COLS], shared[:, A_COLS : 2 * A_COLS], shared[:, 2 * A_COLS :]]
    shared[2] = jnp.pad(shared[2], ((0, 0), (0, A_COLS - wide[2])))
    attn_two = lax.all_gather(jnp.concatenate([attn_two] + shared, axis=0), "dp")
    shared = [
        attn_two[:, A_ROWS + 2 * SHARD * i : A_ROWS + 2 * SHARD * (i + 1), : wide[i]] for i in range(3)
    ]
    shared = jnp.concatenate(shared, axis=2)
    d_rows_two = shared[:, :SHARD].reshape(TOKENS, D)
    normed_one = lax.dynamic_slice_in_dim(shared[:, SHARD:], lax.axis_index("dp") * SLICE, SLICE, 2)
    gains_two = attention_gains(attn_two)
    middle, saved = attention_forward(normed, latent, x_own, attn_one, gains_one, tab)
    mine = [weights, near, after]
    ffn_weights = mine + [to_core(piece) for piece in mine]
    part, saved_one, ffn_weights = layer_forward(
        own_one, x_own, middle, saved, gains_one, ffn_weights, ring_hop(near, 1)
    )
    out_one = layer_out_rows(scatter_dp(part), saved_one)
    rows_one = gather_tokens(out_one)
    x_own = out_one.astype(F32)
    normed, latent = latents(rows_one, gains_two["attn"], attn_two)
    middle, saved = attention_forward(normed, latent, x_own, attn_two, gains_two, tab)
    rows_ffn = gather_dp(norm(middle, gains_two["ffn"]).astype(BF16))
    part_two, hidden, part, d_gu = ffn_both(own_two, rows_ffn, d_rows_two, ffn_weights)
    saved_two = (x_own, middle, rows_ffn, None, hidden) + saved

    mixed_one = lax.all_gather(saved_one[-1][5], "dp")

    grads_two = ffn_gradients(own_two, d_rows_two, rows_ffn, d_gu, hidden)
    d_normed_two = scatter_dp(part)
    d_normed_two, mixed_one, normed_one = tie((d_normed_two, mixed_one, normed_one))
    ring_two = ring_pairs(grads_two)
    d_middle, ffn_gain_two = middle_backward(cot_own, d_normed_two, saved_two, gains_two)
    d_attended = d_attended_rows(d_middle)
    part, d_query, d_key_value = attend_back(d_attended, tab, saved_two[-1], attn_two)
    packs_two = attend_gradients(d_attended, saved_two[-1], d_query, d_key_value)
    in_grad_two, rows, _, dg_two, part_two, _ = attention_backward(
        part, d_middle, saved_two, attn_two, gains_two, scatter_dp(part_two)
    )
    attn, q, kv = dg_two
    dg_two = jnp.concatenate([attn, ffn_gain_two, q, kv])
    dg_two = jnp.pad(dg_two, (0, 10 * LAT - dg_two.shape[0])).astype(BF16).reshape(10, LAT)
    rows = jnp.stack(gather_z(jnp.concatenate([rows, dg_two], axis=0)))
    dg_two = jnp.sum(rows[:, 2 * SHARD :].astype(F32), axis=0).reshape(-1)
    rows = rows[:, : 2 * SHARD].reshape(N_Z, 2, SHARD, LAT).transpose(1, 0, 2, 3).reshape(ROWS, LAT)
    packs_two = late_pack(saved_two[5], rows, dg_two, packs_two).reshape(-1, WO)
    in_grad_two, ring_two = tie((in_grad_two, ring_two))
    ring_two = ring_first(ring_two)

    grad_one = in_grad_two.astype(F32)
    d_rows, packs_two = tie((d_mlp_rows(grad_one), packs_two))
    packs_two = lax.psum_scatter(packs_two, "dp", scatter_dimension=0, tiled=True)
    ffn_rows, gu, hidden = saved_one[2:5]
    part, d_gu = ffn_backward(own_one, d_rows, gu, ffn_weights)
    grads_one = ffn_gradients(own_one, d_rows, ffn_rows, d_gu, hidden)
    d_normed_two = scatter_dp(part)
    total_two = ring_last(ring_two)
    rows_two = gather_tokens(layer_out_rows(part_two, saved_two))
    d_normed_two, total_two, rows_two, grads_one = tie((d_normed_two, total_two, rows_two, grads_one))
    d_middle, ffn_gain_one = middle_backward(grad_one, d_normed_two, saved_one, gains_one)
    d_att_own = (RES_SCALE * d_middle).astype(BF16)
    columns = d_att_own.reshape(SHARD, N_DP, SLICE).transpose(1, 0, 2)
    d_attended = gather_tokens(d_att_own)
    part, d_query, d_key_value = attend_back(d_attended, tab, saved_one[-1], attn_one)
    low_one = low_gradients(saved_one[-1], d_query, d_key_value, columns)
    part, low_one = tie((part, low_one))
    low_one = lax.all_to_all(low_one, "dp", 0, 0)
    first = ring_first(ring_pairs(grads_one))
    in_grad_one, _, d_lat_own, dg_one, low_one, first = attention_backward(
        part, d_middle, saved_one, attn_one, gains_one, low_one, first
    )
    d_lat = jnp.broadcast_to(d_lat_own.astype(BF16)[None], (N_DP, SHARD, LAT_ALL))
    columns = gather_tokens(low_one[:, LOW_ROWS:, :SLICE].reshape(TOKENS, SLICE))
    wo_one = wo_gradient(columns, mixed_one)
    low_one = jnp.sum(low_one[:, :LOW_ROWS].astype(F32), axis=0)
    d_lat = lax.all_to_all(d_lat, "dp", 0, 0)
    lat_one = latent_gradient(d_lat, normed_one)
    total_one, lat_one = tie((ring_last(first), lat_one))

    attn, q, kv = dg_one
    dg_one = jnp.concatenate([attn, ffn_gain_one, q, kv])
    dg_one = jnp.pad(dg_one, (0, 3 * D - dg_one.shape[0])).astype(BF16).reshape(3, D)
    got = to_core(jnp.concatenate([jnp.where(core == 0, in_grad_two, in_grad_one), dg_one], axis=0))
    mine = jnp.where(core == 0, in_grad_one, in_grad_two)
    dg_one = add(dg_one, got[SHARD:])
    both = jnp.concatenate(
        [jnp.concatenate([mine, dg_one], axis=0), jnp.pad(got[:SHARD], ((0, 3), (0, 0)))], axis=1
    )
    both = jnp.stack(gather_z(both))
    dg_one = jnp.sum(both[:, SHARD:, :D].astype(F32), axis=0).reshape(-1)
    both = both[:, :SHARD].reshape(PACK, 2 * D)
    input_grad = in_order(both[:, :D], both[:, D:])[None]

    row = jnp.concatenate(gain_vectors(dg_one), axis=1).astype(BF16)
    row = jnp.pad(row[:, None], ((0, 0), (0, 15), (0, 0)))
    total_one = total_one.reshape(N_DP, HALF_ROWS, MATS)
    def from_other(x, layer):
        return lax.ppermute(x, "section", [(1 - layer, layer)])

    layer_out = in_order(*(jnp.where(core == 0, one, two) for one, two in zip(rows_one, rows_two)))
    total_one, pieces, layer_out, input_grad = tie(
        (
            total_one,
            (
                wo_one,
                from_other(wo_one, 0),
                low_one,
                from_other(low_one, 0),
                packs_two,
                from_other(packs_two, 1),
            ),
            layer_out,
            input_grad,
        )
    )
    blocks = jnp.concatenate([total_one, total_two.reshape(N_DP, HALF_ROWS, MATS), row], axis=1)
    blocks = lax.all_to_all(blocks, "dp", 0, 0)
    lat_one = add(lat_one, from_other(lat_one, 0))
    lat_one = sum(x.astype(F32) for x in gather_z(lat_one))
    blocks, attention = tie((blocks, home(core.reshape(1), lat_one, *pieces)))
    qa_grad, kva_grad, qb_grad, kvb_grad, wo_grad, gains = attention
    gains = gains.reshape(-1)
    dg_one = jnp.sum(blocks[:, SLICE].astype(F32), axis=0)
    gate_grad, up_grad, down_grad = ffn_unpack(core.reshape(1), blocks, to_core(blocks))

    def gain_part(one, two, width):
        return jnp.where(core == 0, dg_one[one : one + width], gains[two : two + width])[None]

    return (
        layer_out[None],
        input_grad,
        gain_part(0, 0, SLICE),
        qa_grad[None],
        gain_part(2 * SLICE, 4 * HEAD, QR // N_DP),
        qb_grad[None],
        kva_grad[None],
        gain_part(2 * SLICE + QR // N_DP, 4 * HEAD + QR // N_DP, KVR // N_DP),
        kvb_grad[None],
        wo_grad.T[None],
        gain_part(SLICE, 2 * HEAD, SLICE),
        gate_grad[None],
        up_grad[None],
        down_grad.T[None],
    )


def solution(mesh):
    in_specs = (
        P("dp", None),
        P("dp", None),
        P("dp", None),
        P("section", "dp"),
        P("section", "dp", None),
        P("section", "dp"),
        P("section", "dp", "tensor"),
        P("section", "dp", None),
        P("section", "dp"),
        P("section", "dp", "tensor"),
        P("section", "tensor", "dp"),
        P("section", "dp"),
        P("section", "dp", "tensor"),
        P("section", "dp", "tensor"),
        P("section", "tensor", "dp"),
    )
    out_specs = (
        P("section", "dp", None),
        P("section", "dp", None),
        P("section", "dp"),
        P("section", "dp", None),
        P("section", "dp"),
        P("section", "dp", "tensor"),
        P("section", "dp", None),
        P("section", "dp"),
        P("section", "dp", "tensor"),
        P("section", "tensor", "dp"),
        P("section", "dp"),
        P("section", "dp", "tensor"),
        P("section", "dp", "tensor"),
        P("section", "tensor", "dp"),
    )
    return jax.shard_map(body, mesh=mesh, in_specs=in_specs, out_specs=out_specs, check_vma=False)
```

```python
import math

import jax
import jax.numpy as jnp
from jax import lax
from jax.experimental import pallas as pl
from jax.experimental.pallas import tpu as pltpu
from jax.sharding import PartitionSpec as P

D = 2560
NOPE = 64
ROPE = 32
VD = 64
QR = 768
KVR = 256
PACK = 64
MB = 2
N_DP = 16
N_Z = 4
HEADS = 5
SLICE = D // N_DP
FF_PART = 100
LANES = 128
SHARD = 16
RES_SCALE = 1.4 / math.sqrt(62.0)
EPSILON = 1e-05
SCORE_SCALE = (NOPE + ROPE) ** (-0.5)
BF16 = jnp.bfloat16
F32 = jnp.float32


def dot(a, b):
    return jnp.dot(a, b, preferred_element_type=F32)


def dot_tn(a, b):
    return lax.dot_general(a, b, (((0,), (0,)), ((), ())), preferred_element_type=F32)


def dot_nt(a, b):
    return lax.dot_general(a, b, (((1,), (1,)), ((), ())), preferred_element_type=F32)


def to_core(x):
    return lax.ppermute(x, "section", [(0, 1), (1, 0)])


def z_hop(x, by):
    return lax.ppermute(x, "tensor", [(i, (i + by) % N_Z) for i in range(N_Z)])


def by_core(core, mine, other):
    return jnp.where(core == 0, mine, other), jnp.where(core == 0, other, mine)


def from_here(x):
    return lax.dynamic_slice_in_dim(jnp.concatenate([x, x]), lax.axis_index("tensor"), N_Z, 0)


def from_zero(x):
    at = (N_Z - lax.axis_index("tensor")) % N_Z
    return lax.dynamic_slice_in_dim(jnp.concatenate([x, x]), at, N_Z, 0)


def gather_z(x):
    return [x, z_hop(x, -1), z_hop(x, 2), z_hop(x, 1)]


def gather_tokens(x):
    mine = jnp.concatenate(gather_z(x), axis=0)
    return mine, to_core(mine)


def in_order(mine, other):
    core = lax.axis_index("section")
    shape = (N_Z, SHARD, mine.shape[-1])
    mine, other = from_zero(mine.reshape(shape)), from_zero(other.reshape(shape))
    return jnp.concatenate(by_core(core, mine, other), axis=0).reshape(-1, shape[-1])


def scatter_tokens(part):
    half = part[:PACK].astype(F32) + to_core(part[PACK:]).astype(F32)
    sent = half.astype(BF16)
    total = half[:SHARD]
    for by in (2, 1, 3):
        total = total + z_hop(sent[SHARD * by : SHARD * (by + 1)], by).astype(F32)
    return total


def gather_dp(x):
    copies = jnp.broadcast_to(x[None], (N_DP,) + x.shape)
    return lax.all_to_all(copies, "dp", 0, 0).reshape(N_DP * x.shape[0], x.shape[1])


def swap_dp(part):
    return lax.all_to_all(part.reshape(N_DP, SHARD, D), "dp", 0, 0)


def scatter_dp(part):
    return jnp.sum(swap_dp(part).astype(F32), axis=0)


def norm_scale(x):
    return lax.rsqrt(jnp.mean(x * x, axis=-1, keepdims=True) + EPSILON)


def norm(x, gain):
    return x * norm_scale(x) * gain


def norm_back(x, gain, d):
    q = norm_scale(x)
    along = jnp.mean(gain * d * x, axis=-1, keepdims=True)
    return q * gain * d - x * (q * q * q) * along, jnp.sum(d * x * q, axis=0)


MATS = 3 * LANES
TOKENS = N_DP * SHARD
FF_VMEM = 56 * 1024 * 1024
FF_SCRATCH = [pltpu.VMEM((N_Z, D, MATS), BF16), pltpu.SemaphoreType.DMA((N_Z,))]


def ffn_copies(own_ref, mine, other, w_ref, sems):
    copies = [pltpu.make_async_copy(mine[z], w_ref.at[z], sems.at[z]) for z in range(N_Z)]
    others = [pltpu.make_async_copy(other[z], w_ref.at[z], sems.at[z]) for z in range(N_Z)]

    @pl.when(own_ref[0] == 1)
    def _():
        for copy in copies:
            copy.start()

    @pl.when(own_ref[0] != 1)
    def _():
        for copy in others:
            copy.start()

    return copies


def down_pair(w_ref, z):
    return jnp.concatenate([w_ref[z, :, 2 * LANES :], w_ref[z + 1, :, 2 * LANES :]], axis=1)


def ffn_forward_kernel(own_ref, n_ref, *refs):
    mine, other = refs[:N_Z], refs[N_Z : 2 * N_Z]
    part_ref, gu_ref, hid_ref, w_ref, sems = refs[2 * N_Z :]
    copies = ffn_copies(own_ref, mine, other, w_ref, sems)
    for z in range(N_Z):
        copies[z].wait()
        gu = dot(n_ref[...], w_ref[z, :, : 2 * LANES])
        gu_ref[:, 2 * LANES * z : 2 * LANES * (z + 1)] = gu
        gate, up = gu[:, :LANES], gu[:, LANES:]
        hid_ref[:, LANES * z : LANES * (z + 1)] = (gate * jax.nn.sigmoid(gate) * up).astype(BF16)
    out = dot_nt(hid_ref[:, : 2 * LANES], down_pair(w_ref, 0))
    part_ref[...] = (out + dot_nt(hid_ref[:, 2 * LANES :], down_pair(w_ref, 2))).astype(BF16)


def ffn_specs(arrays):
    vmem = pl.BlockSpec(memory_space=pltpu.VMEM)
    smem = pl.BlockSpec(memory_space=pltpu.SMEM)
    return [smem] + [vmem] * arrays + [pl.BlockSpec(memory_space=pl.ANY)] * (2 * N_Z)


def ffn_forward(own, rows, weights):
    return pl.pallas_call(
        ffn_forward_kernel,
        out_shape=(
            jax.ShapeDtypeStruct((TOKENS, D), BF16),
            jax.ShapeDtypeStruct((TOKENS, 2 * LANES * N_Z), F32),
            jax.ShapeDtypeStruct((TOKENS, LANES * N_Z), BF16),
        ),
        in_specs=ffn_specs(1),
        out_specs=(pl.BlockSpec(memory_space=pltpu.VMEM),) * 3,
        scratch_shapes=FF_SCRATCH,
        compiler_params=pltpu.CompilerParams(vmem_limit_bytes=FF_VMEM),
        name="ffn_forward",
    )(own, rows, *weights)


def ffn_both_kernel(own_ref, n_ref, dm_ref, *refs):
    mine, other = refs[:N_Z], refs[N_Z : 2 * N_Z]
    part_ref, hid_ref, d_part_ref, dgu_ref, w_ref, sems = refs[2 * N_Z :]
    copies = ffn_copies(own_ref, mine, other, w_ref, sems)
    for z in range(0, N_Z, 2):
        copies[z].wait()
        copies[z + 1].wait()
        d_hidden = dot(dm_ref[...], down_pair(w_ref, z))
        for k in range(2):
            gu = dot(n_ref[...], w_ref[z + k, :, : 2 * LANES])
            gate, up = gu[:, :LANES], gu[:, LANES:]
            s = jax.nn.sigmoid(gate)
            hid_ref[:, LANES * (z + k) : LANES * (z + k + 1)] = (gate * s * up).astype(BF16)
            d_h = d_hidden[:, LANES * k : LANES * (k + 1)]
            at = 2 * LANES * (z + k)
            dgu_ref[:, at : at + LANES] = (d_h * up * (s + gate * s * (1.0 - s))).astype(BF16)
            dgu_ref[:, at + LANES : at + 2 * LANES] = (d_h * (gate * s)).astype(BF16)
    out = None
    for z in range(N_Z):
        term = dot_nt(dgu_ref[:, 2 * LANES * z : 2 * LANES * (z + 1)], w_ref[z, :, : 2 * LANES])
        out = term if z == 0 else out + term
    d_part_ref[...] = out.astype(BF16)
    out = dot_nt(hid_ref[:, : 2 * LANES], down_pair(w_ref, 0))
    part_ref[...] = (out + dot_nt(hid_ref[:, 2 * LANES :], down_pair(w_ref, 2))).astype(BF16)


def ffn_both(own, rows, d_rows, weights):
    widths = (D, LANES * N_Z, D, 2 * LANES * N_Z)
    return pl.pallas_call(
        ffn_both_kernel,
        out_shape=tuple(jax.ShapeDtypeStruct((TOKENS, w), BF16) for w in widths),
        in_specs=ffn_specs(2),
        out_specs=(pl.BlockSpec(memory_space=pltpu.VMEM),) * 4,
        scratch_shapes=FF_SCRATCH,
        compiler_params=pltpu.CompilerParams(vmem_limit_bytes=FF_VMEM),
        name="ffn_both",
    )(own, rows, d_rows, *weights)


HALF_ROWS = SLICE // 2


def ffn_backward_kernel(own_ref, dm_ref, gu_ref, *refs):
    mine, other = refs[:N_Z], refs[N_Z : 2 * N_Z]
    part_ref, dgu_ref, w_ref, sems = refs[2 * N_Z :]
    copies = ffn_copies(own_ref, mine, other, w_ref, sems)
    out = None
    for z in range(0, N_Z, 2):
        copies[z].wait()
        copies[z + 1].wait()
        d_hidden = dot(dm_ref[...], down_pair(w_ref, z))
        for k in range(2):
            columns = slice(2 * LANES * (z + k), 2 * LANES * (z + k) + LANES)
            more = slice(columns.stop, columns.stop + LANES)
            gate, up = gu_ref[:, columns], gu_ref[:, more]
            d_h = d_hidden[:, LANES * k : LANES * (k + 1)]
            s = jax.nn.sigmoid(gate)
            dgu_ref[:, columns] = (d_h * up * (s + gate * s * (1.0 - s))).astype(BF16)
            dgu_ref[:, more] = (d_h * (gate * s)).astype(BF16)
    for z in range(N_Z):
        term = dot_nt(dgu_ref[:, 2 * LANES * z : 2 * LANES * (z + 1)], w_ref[z, :, : 2 * LANES])
        out = term if z == 0 else out + term
    part_ref[...] = out.astype(BF16)


def ffn_backward(own, d_rows, gu, weights):
    return pl.pallas_call(
        ffn_backward_kernel,
        out_shape=(
            jax.ShapeDtypeStruct((TOKENS, D), BF16),
            jax.ShapeDtypeStruct((TOKENS, 2 * LANES * N_Z), BF16),
        ),
        in_specs=ffn_specs(2),
        out_specs=(pl.BlockSpec(memory_space=pltpu.VMEM),) * 2,
        scratch_shapes=FF_SCRATCH,
        compiler_params=pltpu.CompilerParams(vmem_limit_bytes=FF_VMEM),
        name="ffn_backward",
    )(own, d_rows, gu, *weights)


HALF_ROWS = SLICE // 2


def ffn_gradients_kernel(own_ref, dm_ref, n_ref, dgu_ref, hid_ref, *refs):
    outs, grad_ref, out_sems = refs[: 2 * N_Z], refs[2 * N_Z], refs[2 * N_Z + 1]
    core = own_ref[1]

    def store(z, columns, grad):
        grad_ref[z, :, :, :, columns] = grad.reshape(N_DP, 2, HALF_ROWS, grad.shape[1])

    def send(z, keep_at, give_at):
        return [
            pltpu.make_async_copy(grad_ref.at[z, :, core], outs[keep_at], out_sems.at[keep_at]),
            pltpu.make_async_copy(
                grad_ref.at[z, :, 1 - core], outs[N_Z + give_at], out_sems.at[N_Z + give_at]
            ),
        ]

    for z in (2, 0):
        hidden = hid_ref[:, LANES * z : LANES * (z + 2)]
        grad = dot_tn(dm_ref[...], hidden).astype(BF16)
        store(z, slice(2 * LANES, MATS), grad[:, :LANES])
        store(z + 1, slice(2 * LANES, MATS), grad[:, LANES:])
        for k in range(2):
            d_gu = dgu_ref[:, 2 * LANES * (z + k) : 2 * LANES * (z + k + 1)]
            store(z + k, slice(0, 2 * LANES), dot_tn(n_ref[...], d_gu).astype(BF16))
            if z + k in (0, N_Z - 1):
                for copy in send(z + k, z + k, z + k):
                    copy.start()
            else:
                for owner in (1, 0):
                    keep_at = z + k if owner == 1 else 3 - z - k

                    @pl.when(own_ref[0] == owner)
                    def _(at=z + k, keep_at=keep_at):
                        for copy in send(at, keep_at, 3 - keep_at):
                            copy.start()

    for z in range(N_Z):
        for copy in send(z, z, z):
            copy.wait()


def ffn_gradients(own, d_rows, rows, d_gu, hidden):
    vmem = pl.BlockSpec(memory_space=pltpu.VMEM)
    return pl.pallas_call(
        ffn_gradients_kernel,
        out_shape=tuple(jax.ShapeDtypeStruct((N_DP, HALF_ROWS, MATS), BF16) for _ in range(2 * N_Z)),
        in_specs=[pl.BlockSpec(memory_space=pltpu.SMEM)] + [vmem] * 4,
        out_specs=(pl.BlockSpec(memory_space=pl.ANY),) * (2 * N_Z),
        scratch_shapes=[
            pltpu.VMEM((N_Z, N_DP, 2, HALF_ROWS, MATS), BF16),
            pltpu.SemaphoreType.DMA((2 * N_Z,)),
        ],
        compiler_params=pltpu.CompilerParams(vmem_limit_bytes=FF_VMEM),
        cost_estimate=pl.CostEstimate(flops=2 * TOKENS * D * MATS * N_Z, bytes_accessed=1 << 24, transcendentals=0),
        name="ffn_gradients",
    )(own, d_rows, rows, d_gu, hidden)


FF = N_DP * FF_PART
WINDOW = 2 * LANES
FF_PADDED = (FF - FF_PART) // LANES * LANES + WINDOW


def ffn_pack_kernel(gate_ref, up_ref, down_ref, out_ref, wide_ref):
    wide_ref[0, :, :FF] = gate_ref[...].astype(F32)
    wide_ref[1, :, :FF] = up_ref[...].astype(F32)
    wide_ref[2, :, :FF] = down_ref[...].astype(F32)
    valid = lax.broadcasted_iota(jnp.int32, (SLICE, LANES), 1) < FF_PART
    for p in range(N_DP):
        at = FF_PART * p // LANES * LANES
        by = FF_PART * p - at
        for m in range(3):
            window = wide_ref[m, :, at : at + WINDOW]
            if by > 0:
                window = pltpu.roll(window, WINDOW - by, 1)
            block = jnp.where(valid, window[:, :LANES], 0.0)
            out_ref[p, :, LANES * m : LANES * (m + 1)] = block.astype(BF16)


def ffn_pack(w_gate, w_up, w_down):
    return pl.pallas_call(
        ffn_pack_kernel,
        out_shape=jax.ShapeDtypeStruct((N_DP, SLICE, MATS), BF16),
        scratch_shapes=[pltpu.VMEM((3, SLICE, FF_PADDED), F32)],
        compiler_params=pltpu.CompilerParams(vmem_limit_bytes=FF_VMEM),
        name="ffn_pack",
    )(w_gate, w_up, w_down)


def ffn_unpack_kernel(core_ref, blocks_ref, got_ref, gate_ref, up_ref, down_ref):
    first = core_ref[0] == 0
    one, two = slice(0, HALF_ROWS), slice(HALF_ROWS, SLICE)
    for p in range(N_DP):
        columns = slice(FF_PART * p, FF_PART * (p + 1))
        for m, out_ref in enumerate((gate_ref, up_ref, down_ref)):
            lanes = slice(LANES * m, LANES * (m + 1))
            low = jnp.where(first, blocks_ref[p, one, lanes], got_ref[p, two, lanes])
            high = jnp.where(first, got_ref[p, one, lanes], blocks_ref[p, two, lanes])
            out_ref[one, columns] = low[:, :FF_PART].astype(F32)
            out_ref[two, columns] = high[:, :FF_PART].astype(F32)


def ffn_unpack(core, *blocks):
    vmem = pl.BlockSpec(memory_space=pltpu.VMEM)
    return pl.pallas_call(
        ffn_unpack_kernel,
        out_shape=(jax.ShapeDtypeStruct((SLICE, FF), F32),) * 3,
        in_specs=[pl.BlockSpec(memory_space=pltpu.SMEM), vmem, vmem],
        out_specs=(vmem,) * 3,
        compiler_params=pltpu.CompilerParams(vmem_limit_bytes=FF_VMEM),
        name="ffn_unpack",
    )(core, *blocks)


A_ROWS = SLICE + QR // N_DP + KVR // N_DP
A_COLS = 896
LAT = 640
WO_AT = 512
WO = 384
HEAD = 128
ROWS = MB * PACK
QB_ROWS = slice(SLICE, SLICE + QR // N_DP)
KVB_ROWS = slice(SLICE + QR // N_DP, A_ROWS)
E_ROWS = 2 * A_ROWS - SLICE
ATT_VMEM = 48 * 1024 * 1024


def latent_kernel(mine_ref, other_ref, gain_ref, pack_ref, normed_ref, lat_ref, w_ref, sem):
    copy = pltpu.make_async_copy(pack_ref.at[:, 0:SLICE, 0:LAT], w_ref, sem)
    copy.start()
    normed_ref[:PACK] = norm(mine_ref[...].astype(F32), gain_ref[...]).astype(BF16)
    normed_ref[PACK:] = norm(other_ref[...].astype(F32), gain_ref[...]).astype(BF16)
    copy.wait()
    lat_ref[...] = dot(normed_ref[...], w_ref[...].reshape(D, LAT))


def latents(rows, gain, pack):
    vmem = pl.BlockSpec(memory_space=pltpu.VMEM)
    return pl.pallas_call(
        latent_kernel,
        out_shape=(
            jax.ShapeDtypeStruct((ROWS, D), BF16),
            jax.ShapeDtypeStruct((ROWS, LAT), F32),
        ),
        in_specs=[vmem, vmem, vmem, pl.BlockSpec(memory_space=pl.ANY)],
        out_specs=(vmem, vmem),
        scratch_shapes=[pltpu.VMEM((N_DP, SLICE, LAT), BF16), pltpu.SemaphoreType.DMA],
        compiler_params=pltpu.CompilerParams(vmem_limit_bytes=ATT_VMEM),
        name="latents",
    )(*rows, gain, pack)


def weight_copies(pack_ref, qb_ref, kvb_ref, wo_ref, sems):
    sources = (
        pack_ref.at[:, QB_ROWS, 0:LAT],
        pack_ref.at[:, KVB_ROWS, 0:LAT],
        pack_ref.at[:, 0:SLICE, WO_AT : WO_AT + WO],
    )
    targets = (qb_ref, kvb_ref, wo_ref)
    copies = [pltpu.make_async_copy(a, b, sems.at[i]) for i, (a, b) in enumerate(zip(sources, targets))]
    for copy in copies:
        copy.start()
    return copies


def weight_scratch():
    return [
        pltpu.VMEM((N_DP, QR // N_DP, LAT), BF16),
        pltpu.VMEM((N_DP, KVR // N_DP, LAT), BF16),
        pltpu.VMEM((N_DP, SLICE, WO), BF16),
        pltpu.SemaphoreType.DMA((3,)),
    ]


def lanes_of(x):
    return lax.broadcasted_iota(jnp.int32, x.shape, 1)


def turn(x, tab_ref):
    return (
        x * tab_ref[0]
        + pltpu.roll(x, HEAD - ROPE // 2, 1) * tab_ref[1]
        + pltpu.roll(x, ROPE // 2, 1) * tab_ref[2]
    )


def turn_back(x, tab_ref):
    return (
        x * tab_ref[0]
        - pltpu.roll(x, HEAD - ROPE // 2, 1) * tab_ref[1]
        - pltpu.roll(x, ROPE // 2, 1) * tab_ref[2]
    )


def head_columns(h):
    return slice(HEAD * h, HEAD * (h + 1))


def probs_of(query, key, tab_ref):
    scores = jnp.where(tab_ref[3] < 0.0, -1e30, dot_nt(query, key) * SCORE_SCALE)
    weight = jnp.exp(scores - jnp.max(scores, axis=-1, keepdims=True))
    return weight / jnp.sum(weight, axis=-1, keepdims=True)


def attend_kernel(
    core_ref, mine_ref, other_ref, tab_ref, gq_ref, gkv_ref, pack_ref,
    part_ref, sq_ref, comp_ref, q_ref, kv_ref, kr_ref, mixed_ref, lat_ref,
    qb_ref, kvb_ref, wo_ref, sems,
):
    copies = weight_copies(pack_ref, qb_ref, kvb_ref, wo_ref, sems)
    zero = core_ref[0] == 0
    other = jnp.concatenate([other_ref[PACK:], other_ref[:PACK]], axis=0)
    second = jnp.where(zero, other, mine_ref[...])
    first = jnp.where(zero, mine_ref[:, :512], other[:, :512])
    latent_q = jnp.concatenate([first, second[:, :256]], axis=1)
    lat_ref[:, :QR] = latent_q[:SHARD]
    lat_ref[:, QR:] = second[:SHARD, 256:512]
    sq_ref[...] = norm(latent_q, gq_ref[...]).astype(BF16)
    comp_ref[...] = norm(second[:, 256:512], gkv_ref[...]).astype(BF16)
    rope = pltpu.roll(second[:, 512:640], NOPE, 1)
    rope = jnp.where(lanes_of(rope) < NOPE, 0.0, turn(rope, tab_ref)).astype(BF16)
    kr_ref[...] = rope
    copies[0].wait()
    query = dot(sq_ref[...], qb_ref[...].reshape(QR, LAT))
    for h in range(HEADS):
        q_ref[:, head_columns(h)] = turn(query[:, head_columns(h)], tab_ref).astype(BF16)
    copies[1].wait()
    kv_ref[...] = dot(comp_ref[...], kvb_ref[...].reshape(KVR, LAT)).astype(BF16)
    heads = []
    for h in range(HEADS):
        kv = kv_ref[:, head_columns(h)]
        key = jnp.where(lanes_of(kv) < NOPE, kv, rope)
        probs = probs_of(q_ref[:, head_columns(h)], key, tab_ref)
        heads.append(dot(probs.astype(BF16), kv))
    low = lanes_of(heads[0]) < NOPE
    tiles = [jnp.where(low, 0.0, heads[0])]
    tiles += [jnp.where(low, pltpu.roll(heads[i], NOPE, 1), heads[i + 1]) for i in (1, 3)]
    mixed_ref[...] = jnp.concatenate(tiles, axis=1).astype(BF16)
    copies[2].wait()
    part_ref[...] = dot_nt(mixed_ref[...], wo_ref[...].reshape(D, WO)).astype(BF16)


def attend(core, mine, other, tab, g_q, g_kv, pack):
    vmem = pl.BlockSpec(memory_space=pltpu.VMEM)
    widths = (D, QR, KVR, LAT, LAT, HEAD, WO)
    return pl.pallas_call(
        attend_kernel,
        out_shape=tuple(jax.ShapeDtypeStruct((ROWS, w), BF16) for w in widths)
        + (jax.ShapeDtypeStruct((SHARD, QR + KVR), F32),),
        in_specs=[pl.BlockSpec(memory_space=pltpu.SMEM)] + [vmem] * 5 + [pl.BlockSpec(memory_space=pl.ANY)],
        out_specs=(vmem,) * (len(widths) + 1),
        scratch_shapes=weight_scratch(),
        compiler_params=pltpu.CompilerParams(vmem_limit_bytes=ATT_VMEM),
        name="attend",
    )(core, mine, other, tab, g_q, g_kv, pack)


def attend_back_kernel(
    mine_ref, other_ref, tab_hbm, q_hbm, kv_hbm, kr_hbm, pack_ref,
    part_ref, dq_ref, dkv_ref,
    tab_ref, q_ref, kv_ref, kr_ref, in_sems, qb_ref, kvb_ref, wo_ref, sems,
):
    pairs = ((kv_hbm, kv_ref), (kr_hbm, kr_ref), (q_hbm, q_ref), (tab_hbm, tab_ref))
    inputs = [pltpu.make_async_copy(a, b, in_sems.at[i]) for i, (a, b) in enumerate(pairs)]
    for copy in inputs:
        copy.start()
    copies = weight_copies(pack_ref, qb_ref, kvb_ref, wo_ref, sems)
    d_att = jnp.concatenate([mine_ref[...], other_ref[...]], axis=0)
    copies[2].wait()
    d_mixed = dot(d_att, wo_ref[...].reshape(D, WO))
    for copy in inputs:
        copy.wait()
    rope = kr_ref[...]
    d_rope = jnp.zeros((ROWS, HEAD), F32)
    for h in range(HEADS):
        kv = kv_ref[:, head_columns(h)]
        low = lanes_of(kv) < NOPE
        key = jnp.where(low, kv, rope)
        query = q_ref[:, head_columns(h)]
        probs = probs_of(query, key, tab_ref)
        tile = d_mixed[:, head_columns((h + 1) // 2)]
        if h % 2 == 1:
            tile = pltpu.roll(tile, NOPE, 1)
        tile = jnp.where(low, 0.0, tile).astype(BF16)
        d_probs = dot_nt(tile, kv)
        d_scores = probs * (d_probs - jnp.sum(probs * d_probs, axis=-1, keepdims=True))
        d_scores = d_scores.astype(BF16)
        d_query = dot(d_scores, key) * SCORE_SCALE
        d_key = dot_tn(d_scores, query) * SCORE_SCALE
        d_value = dot_tn(probs.astype(BF16), tile)
        dq_ref[:, head_columns(h)] = turn_back(d_query, tab_ref).astype(BF16)
        dkv_ref[:, head_columns(h)] = jnp.where(low, d_key, d_value).astype(BF16)
        d_rope = d_rope + d_key
    d_rope = jnp.where(lanes_of(d_rope) < NOPE, 0.0, turn_back(jnp.where(lanes_of(d_rope) < NOPE, 0.0, d_rope), tab_ref))
    copies[0].wait()
    copies[1].wait()
    part_ref[:, :QR] = dot_nt(dq_ref[...], qb_ref[...].reshape(QR, LAT)).astype(BF16)
    part_ref[:, QR : QR + KVR] = dot_nt(dkv_ref[...], kvb_ref[...].reshape(KVR, LAT)).astype(BF16)
    part_ref[:, QR + KVR :] = d_rope.astype(BF16)


def attend_back(d_attended, tab, saved, pack):
    vmem = pl.BlockSpec(memory_space=pltpu.VMEM)
    return pl.pallas_call(
        attend_back_kernel,
        out_shape=(
            jax.ShapeDtypeStruct((ROWS, QR + KVR + HEAD), BF16),
            jax.ShapeDtypeStruct((ROWS, LAT), BF16),
            jax.ShapeDtypeStruct((ROWS, LAT), BF16),
        ),
        in_specs=[vmem] * 2 + [pl.BlockSpec(memory_space=pl.ANY)] * 5,
        out_specs=(vmem,) * 3,
        scratch_shapes=[
            pltpu.VMEM((4, ROWS, HEAD), F32),
            pltpu.VMEM((ROWS, LAT), BF16),
            pltpu.VMEM((ROWS, LAT), BF16),
            pltpu.VMEM((ROWS, HEAD), BF16),
            pltpu.SemaphoreType.DMA((4,)),
        ]
        + weight_scratch(),
        compiler_params=pltpu.CompilerParams(vmem_limit_bytes=ATT_VMEM),
        name="attend_back",
    )(*d_attended, tab, *saved[2:5], pack)


def attend_gradients_kernel(
    mine_ref, other_ref, dq_ref, dkv_ref, sq_hbm, comp_hbm, mixed_hbm,
    out_ref,
    early_ref, sq_ref, comp_ref, mixed_ref, sems,
):
    pairs = ((mixed_hbm, mixed_ref), (sq_hbm, sq_ref), (comp_hbm, comp_ref))
    copies = [pltpu.make_async_copy(a, b, sems.at[i]) for i, (a, b) in enumerate(pairs)]
    for copy in copies:
        copy.start()
    d_att = jnp.concatenate([mine_ref[...], other_ref[...]], axis=0)
    copies[0].wait()
    wo_grad = dot_tn(d_att, mixed_ref[...]).astype(BF16)
    early_ref[:, :SLICE, :] = wo_grad.reshape(N_DP, SLICE, WO)
    copies[1].wait()
    qb_grad = dot_tn(sq_ref[...], dq_ref[...]).astype(BF16).reshape(N_DP, QR // N_DP, LAT)
    copies[2].wait()
    kvb_grad = dot_tn(comp_ref[...], dkv_ref[...]).astype(BF16).reshape(N_DP, KVR // N_DP, LAT)
    early_ref[:, QB_ROWS, :] = qb_grad[:, :, :WO]
    early_ref[:, KVB_ROWS, :] = kvb_grad[:, :, :WO]
    more = slice(A_ROWS, A_ROWS + QR // N_DP)
    early_ref[:, more, : LAT - WO] = qb_grad[:, :, WO:]
    early_ref[:, more.stop :, : LAT - WO] = kvb_grad[:, :, WO:]
    early_ref[:, A_ROWS:, LAT - WO :] = jnp.zeros((N_DP, E_ROWS - A_ROWS, 2 * WO - LAT), BF16)
    copy = pltpu.make_async_copy(early_ref, out_ref.at[:, :E_ROWS], sems.at[3])
    copy.start()
    copy.wait()


def attend_gradients(d_attended, saved, d_query, d_key_value):
    vmem = pl.BlockSpec(memory_space=pltpu.VMEM)
    hbm = pl.BlockSpec(memory_space=pl.ANY)
    return pl.pallas_call(
        attend_gradients_kernel,
        out_shape=jax.ShapeDtypeStruct((N_DP, E_ROWS + L_ROWS, WO), BF16),
        in_specs=[vmem] * 4 + [hbm] * 3,
        out_specs=hbm,
        scratch_shapes=[
            pltpu.VMEM((N_DP, E_ROWS, WO), BF16),
            pltpu.VMEM((ROWS, QR), BF16),
            pltpu.VMEM((ROWS, KVR), BF16),
            pltpu.VMEM((ROWS, WO), BF16),
            pltpu.SemaphoreType.DMA((4,)),
        ],
        compiler_params=pltpu.CompilerParams(vmem_limit_bytes=ATT_VMEM),
        name="attend_gradients",
    )(*d_attended, d_query, d_key_value, saved[0], saved[1], saved[5])


def low_gradients_kernel(
    dq_ref, dkv_ref, columns_ref, sq_hbm, comp_hbm, out_ref, sq_ref, comp_ref, sems
):
    copies = [
        pltpu.make_async_copy(sq_hbm, sq_ref, sems.at[0]),
        pltpu.make_async_copy(comp_hbm, comp_ref, sems.at[1]),
    ]
    for copy in copies:
        copy.start()
    copies[0].wait()
    grad = dot_tn(sq_ref[...], dq_ref[...]).astype(BF16)
    out_ref[:, : QR // N_DP, :] = grad.reshape(N_DP, QR // N_DP, LAT)
    copies[1].wait()
    grad = dot_tn(comp_ref[...], dkv_ref[...]).astype(BF16)
    out_ref[:, QR // N_DP : LOW_ROWS, :] = grad.reshape(N_DP, KVR // N_DP, LAT)
    out_ref[:, LOW_ROWS:, :SLICE] = columns_ref[...]
    out_ref[:, LOW_ROWS:, SLICE:] = jnp.zeros((N_DP, SHARD, LAT - SLICE), BF16)


LOW_ROWS = A_ROWS - SLICE


def low_gradients(saved, d_query, d_key_value, columns):
    vmem = pl.BlockSpec(memory_space=pltpu.VMEM)
    hbm = pl.BlockSpec(memory_space=pl.ANY)
    return pl.pallas_call(
        low_gradients_kernel,
        out_shape=jax.ShapeDtypeStruct((N_DP, LOW_ROWS + SHARD, LAT), BF16),
        in_specs=[vmem, vmem, vmem, hbm, hbm],
        out_specs=vmem,
        scratch_shapes=[
            pltpu.VMEM((ROWS, QR), BF16),
            pltpu.VMEM((ROWS, KVR), BF16),
            pltpu.SemaphoreType.DMA((2,)),
        ],
        compiler_params=pltpu.CompilerParams(vmem_limit_bytes=ATT_VMEM),
        name="low_gradients",
    )(d_query, d_key_value, columns, saved[0], saved[1])


def wo_gradient_kernel(mine_ref, other_ref, mixed_hbm, out_ref, mixed_ref, sem):
    copy = pltpu.make_async_copy(mixed_hbm, mixed_ref, sem)
    copy.start()
    copy.wait()
    total = None
    for i in range(2 * N_Z):
        d_ref = mine_ref if i < N_Z else other_ref
        d_att = d_ref[TOKENS * (i % N_Z) : TOKENS * (i % N_Z + 1)]
        mixed = mixed_ref[:, SHARD * i : SHARD * (i + 1), :].reshape(TOKENS, WO)
        term = dot_tn(d_att, mixed)
        total = term if total is None else total + term
    out_ref[...] = total


def wo_gradient(d_attended, mixed):
    vmem = pl.BlockSpec(memory_space=pltpu.VMEM)
    return pl.pallas_call(
        wo_gradient_kernel,
        out_shape=jax.ShapeDtypeStruct((SLICE, WO), F32),
        in_specs=[vmem, vmem, pl.BlockSpec(memory_space=pl.ANY)],
        out_specs=vmem,
        scratch_shapes=[pltpu.VMEM((N_DP, ROWS, WO), BF16), pltpu.SemaphoreType.DMA],
        compiler_params=pltpu.CompilerParams(vmem_limit_bytes=ATT_VMEM),
        name="wo_gradient",
    )(*d_attended, mixed)


LAT_ALL = QR + KVR + HEAD


def latent_gradient_kernel(rows_ref, normed_ref, out_ref):
    rows = rows_ref[...].reshape(TOKENS, LAT_ALL)
    out_ref[...] = dot_tn(normed_ref[...].reshape(TOKENS, SLICE), rows).astype(BF16)


def latent_gradient(rows, normed):
    return pl.pallas_call(
        latent_gradient_kernel,
        out_shape=jax.ShapeDtypeStruct((SLICE, LAT_ALL), BF16),
        compiler_params=pltpu.CompilerParams(vmem_limit_bytes=ATT_VMEM),
        name="latent_gradient",
    )(rows, normed)


L_ROWS = 2 * SLICE


def late_kernel(rows_ref, gains_ref, normed_hbm, packs_ref, out_ref, late_ref, normed_ref, sem, out_sem):
    copy = pltpu.make_async_copy(normed_hbm, normed_ref, sem)
    copy.start()
    late_ref[:, SLICE : SLICE + 16, 2 * HEAD :] = gains_ref[...]
    late_ref[:, SLICE + 16 :, 2 * HEAD :] = jnp.zeros((N_DP, SLICE - 16, HEAD), BF16)
    copy.wait()
    grad = dot_tn(normed_ref[...], rows_ref[...]).astype(BF16)
    late_ref[:, :SLICE, :] = grad[:, :WO].reshape(N_DP, SLICE, WO)
    late_ref[:, SLICE:, : 2 * HEAD] = grad[:, WO:].reshape(N_DP, SLICE, 2 * HEAD)
    copy = pltpu.make_async_copy(late_ref, out_ref.at[:, E_ROWS:], out_sem)
    copy.start()
    copy.wait()


def gain_vectors(gains):
    parts = (gains[:D], gains[D : 2 * D], gains[2 * D : 2 * D + QR], gains[2 * D + QR : 2 * D + QR + KVR])
    return [x.reshape(N_DP, -1) for x in parts]


def late_pack(normed, rows, gains, packs):
    attn, ffn, q, kv = gain_vectors(gains)
    wide = ((0, 0), (0, 2 * HEAD - SLICE))
    row = jnp.concatenate([jnp.pad(attn, wide), jnp.pad(ffn, wide), q, kv], axis=1)
    row = jnp.pad(row, ((0, 0), (0, 16 * HEAD - row.shape[1]))).reshape(N_DP, 16, HEAD).astype(BF16)
    vmem = pl.BlockSpec(memory_space=pltpu.VMEM)
    hbm = pl.BlockSpec(memory_space=pl.ANY)
    return pl.pallas_call(
        late_kernel,
        out_shape=jax.ShapeDtypeStruct(packs.shape, BF16),
        in_specs=[vmem, vmem, hbm, hbm],
        out_specs=hbm,
        scratch_shapes=[
            pltpu.VMEM((N_DP, L_ROWS, WO), BF16),
            pltpu.VMEM((ROWS, D), BF16),
            pltpu.SemaphoreType.DMA,
            pltpu.SemaphoreType.DMA,
        ],
        input_output_aliases={3: 0},
        compiler_params=pltpu.CompilerParams(vmem_limit_bytes=ATT_VMEM),
        name="late_in_packs",
    )(rows, row, normed, packs)


def normed_back_kernel(d_ref, pack_ref, out_ref, w_ref, sem):
    copy = pltpu.make_async_copy(pack_ref.at[:, 0:SLICE, 0:LAT], w_ref, sem)
    copy.start()
    copy.wait()
    out_ref[...] = dot_nt(d_ref[...], w_ref[...].reshape(D, LAT))


def normed_back(d_latent, pack):
    vmem = pl.BlockSpec(memory_space=pltpu.VMEM)
    return pl.pallas_call(
        normed_back_kernel,
        out_shape=jax.ShapeDtypeStruct((d_latent.shape[0], D), F32),
        in_specs=[vmem, pl.BlockSpec(memory_space=pl.ANY)],
        out_specs=vmem,
        scratch_shapes=[pltpu.VMEM((N_DP, SLICE, LAT), BF16), pltpu.SemaphoreType.DMA],
        compiler_params=pltpu.CompilerParams(vmem_limit_bytes=ATT_VMEM),
        name="normed_back",
    )(d_latent, pack)


def home_kernel(
    core_ref, lat_ref, wo1_ref, wo1_got_ref, low_ref, low_got_ref, packs_ref, packs_got_ref,
    qa_ref, kva_ref, qb_ref, kvb_ref, wo_ref, gain_ref, heads_ref,
):
    first = core_ref[0] == 0

    def pick(one, two):
        return jnp.where(first, one.astype(F32), two.astype(F32))

    wide = slice(0, SLICE)
    late, more = slice(E_ROWS, E_ROWS + SLICE), slice(E_ROWS + SLICE, E_ROWS + L_ROWS)
    gain_rows = slice(E_ROWS + SLICE, E_ROWS + SLICE + 16)
    gain_ref[...] = (
        packs_ref[gain_rows, 2 * HEAD :].astype(F32) + packs_got_ref[gain_rows, 2 * HEAD :].astype(F32)
    )
    qa_ref[:, :WO] = pick(lat_ref[wide, :WO], packs_got_ref[late])
    qa_ref[:, WO:512] = pick(lat_ref[wide, WO:512], packs_got_ref[more, :HEAD])
    qa_ref[:, 512:] = pick(lat_ref[wide, 512:QR], packs_ref[late, : 2 * HEAD])
    kva_ref[:, :HEAD] = pick(lat_ref[wide, QR : QR + HEAD], packs_ref[late, 2 * HEAD :])
    kva_ref[:, HEAD:KVR] = pick(lat_ref[wide, QR + HEAD : QR + KVR], packs_ref[more, :HEAD])
    kva_ref[:, KVR:] = pick(lat_ref[wide, QR + KVR :], packs_ref[more, HEAD : 2 * HEAD])[:, :ROPE]
    at = WO - HEADS * VD
    low, high = pick(wo1_ref[...], packs_got_ref[wide]), pick(wo1_got_ref[...], packs_ref[wide])
    wo_ref[...] = jnp.concatenate([low[:, at:], high[:, at:]], axis=1)
    heads_ref[...] = jnp.zeros(heads_ref.shape, F32)
    qb_rows, kvb_rows = slice(0, QR // N_DP), slice(QR // N_DP, A_ROWS - SLICE)
    valid = lax.broadcasted_iota(jnp.int32, (QR // N_DP, HEAD), 1) < NOPE + ROPE
    for j in range(HEADS):
        start = SLICE if j < 3 else A_ROWS
        columns, packed = slice(HEAD * j, HEAD * (j + 1)), slice(HEAD * (j % 3), HEAD * (j % 3 + 1))
        for rows in (qb_rows, kvb_rows):
            at_rows = slice(start + rows.start, start + rows.stop)
            low = pick(low_ref[rows, columns], packs_got_ref[at_rows, packed])
            high = pick(low_got_ref[rows, columns], packs_ref[at_rows, packed])
            for k, tile in enumerate((low, high)):
                if rows == kvb_rows:
                    kvb_ref[:, HEAD * (HEADS * k + j) : HEAD * (HEADS * k + j + 1)] = tile
                    continue
                begin = (NOPE + ROPE) * (HEADS * k + j)
                at = begin // HEAD * HEAD
                tile = jnp.where(valid, tile, 0.0)
                window = jnp.concatenate([tile, jnp.zeros_like(tile)], axis=1)
                if begin > at:
                    window = pltpu.roll(window, begin - at, 1)
                heads_ref[:, at : at + 2 * HEAD] += window
    qb_ref[...] = heads_ref[:, : 2 * HEADS * (NOPE + ROPE)]


def home(core, *pieces):
    vmem = pl.BlockSpec(memory_space=pltpu.VMEM)
    shapes = (
        (SLICE, QR),
        (SLICE, KVR + ROPE),
        (QR // N_DP, 2 * HEADS * (NOPE + ROPE)),
        (KVR // N_DP, 2 * LAT),
        (SLICE, 2 * HEADS * VD),
        (16, HEAD),
    )
    return pl.pallas_call(
        home_kernel,
        out_shape=tuple(jax.ShapeDtypeStruct(x, F32) for x in shapes),
        in_specs=[pl.BlockSpec(memory_space=pltpu.SMEM)] + [vmem] * len(pieces),
        out_specs=(vmem,) * len(shapes),
        scratch_shapes=[pltpu.VMEM((QR // N_DP, 1152), F32)],
        compiler_params=pltpu.CompilerParams(vmem_limit_bytes=ATT_VMEM),
        name="home",
    )(core, *pieces)


def attention_pack_kernel(
    core_ref, qa_ref, qb_ref, kva_ref, kvb_ref, wo_ref, ga_ref, gf_ref, gq_ref, gk_ref,
    keep_ref, give_ref, heads_ref,
):
    half = HEADS * VD
    first = core_ref[0] == 0

    def put(rows, columns, zero, one):
        keep_ref[rows, columns] = jnp.where(first, zero, one).astype(BF16)
        give_ref[rows, columns] = jnp.where(first, one, zero).astype(BF16)

    def blank(rows, columns):
        zero = jnp.zeros((rows.stop - rows.start, columns.stop - columns.start), BF16)
        keep_ref[rows, columns] = zero
        give_ref[rows, columns] = zero

    wide = slice(0, SLICE)
    qa = qa_ref[...].astype(F32)
    put(wide, slice(0, 256), qa[:, :256], qa[:, 512:])
    put(wide, slice(256, 512), qa[:, 256:512], kva_ref[:, :256].astype(F32))
    wo_t = wo_ref[...].astype(F32)
    tail = jnp.zeros((SLICE, WO), F32)
    rope = jnp.concatenate([kva_ref[:, 256:].astype(F32), jnp.zeros((SLICE, WO - ROPE), F32)], axis=1)
    low = jnp.concatenate([tail[:, : WO - half], wo_t[:, :half]], axis=1)
    high = jnp.concatenate([tail[:, : WO - half], wo_t[:, half:]], axis=1)
    put(wide, slice(WO_AT, A_COLS), low, high + rope)
    heads_ref[:, : 2 * HEADS * (NOPE + ROPE)] = qb_ref[...].astype(F32)
    rows = QB_ROWS.stop - QB_ROWS.start
    valid = lax.broadcasted_iota(jnp.int32, (rows, HEAD), 1) < NOPE + ROPE
    tiles = []
    for j in range(2 * HEADS):
        at = (NOPE + ROPE) * j // HEAD * HEAD
        by = (NOPE + ROPE) * j - at
        window = heads_ref[:, at : at + 2 * HEAD]
        if by > 0:
            window = pltpu.roll(window, 2 * HEAD - by, 1)
        tiles.append(jnp.where(valid, window[:, :HEAD], 0.0))
    for j in range(HEADS):
        put(QB_ROWS, slice(HEAD * j, HEAD * (j + 1)), tiles[j], tiles[HEADS + j])
    gain_rows = [jnp.concatenate([g[...].astype(F32), jnp.zeros((1, 256 - SLICE), F32)], axis=1) for g in (ga_ref, gf_ref)]
    last = [gq_ref[...].astype(F32), gk_ref[...].astype(F32), jnp.zeros((1, 256 - 64), F32)]
    gain_rows.append(jnp.concatenate(last, axis=1))
    gains = jnp.concatenate(gain_rows + [jnp.zeros((rows - 3, 256), F32)], axis=0)
    put(QB_ROWS, slice(LAT, A_COLS), gains, gains)
    kvb = kvb_ref[...].astype(F32)
    put(KVB_ROWS, slice(0, LAT), kvb[:, :LAT], kvb[:, LAT:])
    blank(KVB_ROWS, slice(LAT, A_COLS))


def attention_packs(core, *weights):
    vmem = pl.BlockSpec(memory_space=pltpu.VMEM)
    return pl.pallas_call(
        attention_pack_kernel,
        out_shape=(jax.ShapeDtypeStruct((A_ROWS, A_COLS), BF16),) * 2,
        in_specs=[pl.BlockSpec(memory_space=pltpu.SMEM)] + [vmem] * len(weights),
        out_specs=(vmem, vmem),
        scratch_shapes=[pltpu.VMEM((QR // N_DP, 1152), F32)],
        compiler_params=pltpu.CompilerParams(vmem_limit_bytes=ATT_VMEM),
        name="attention_pack",
    )(core, *weights)


def attention_gains(pack):
    gains = pack[:, SLICE : SLICE + 3, LAT:].astype(F32)
    return dict(
        attn=gains[:, 0, :SLICE].reshape(1, D),
        ffn=gains[:, 1, :SLICE].reshape(1, D),
        q=gains[:, 2, : QR // N_DP].reshape(1, QR),
        kv=gains[:, 2, QR // N_DP : QR // N_DP + KVR // N_DP].reshape(1, KVR),
    )


def head_tables(seq_lengths):
    core, t = lax.axis_index("section"), lax.axis_index("tensor")
    at = jnp.arange(ROWS, dtype=jnp.int32)
    pack = (core + at // PACK) % 2
    row = (t + at % PACK // SHARD) % N_Z * SHARD + at % SHARD
    lengths = jnp.where(pack[:, None] == 0, seq_lengths[:1], seq_lengths[1:])
    past_end = row[:, None] >= jnp.cumsum(lengths, axis=1)
    segment = jnp.sum(past_end.astype(jnp.int32), axis=1)
    position = (row - jnp.sum(jnp.where(past_end, lengths, 0), axis=1)).astype(F32)
    frequency = 10000.0 ** (-2.0 * jnp.arange(ROPE // 2, dtype=F32) / ROPE)
    angles = position[:, None] * frequency[None, :]
    cosine, sine = jnp.cos(angles), jnp.sin(angles)
    sequence = pack * PACK + segment
    allowed = (sequence[:, None] == sequence[None, :]) & (row[None, :] <= row[:, None])

    def tile(*pieces):
        x = jnp.concatenate(pieces, axis=1)
        return jnp.pad(x, ((0, 0), (0, HEAD - x.shape[1])))

    ones, none = jnp.ones((ROWS, NOPE), F32), jnp.zeros((ROWS, NOPE), F32)
    bias = jnp.where(allowed, 0.0, -1.0).astype(F32)
    return jnp.stack(
        [tile(ones, cosine, cosine), tile(none, -sine), tile(none, jnp.zeros_like(sine), sine), bias]
    )


def ring_hop(x, by):
    pairs = [
        (c * N_Z + t, c * N_Z + (t + (by if c == 0 else -by)) % N_Z) for c in range(2) for t in range(N_Z)
    ]
    return lax.ppermute(x, ("section", "tensor"), pairs)


def add(*terms):
    return sum(x.astype(F32) for x in terms).astype(BF16)


def ring_pairs(pieces):
    got = [to_core(x) for x in pieces[N_Z:]]
    return add(pieces[3], got[3]), add(pieces[2], got[2]), (pieces[1], got[1]), (pieces[0], got[0])


def ring_first(pairs):
    far, after, near, mine = pairs
    return ring_hop(far, -1), ring_hop(after, 1), near, mine


def ring_last(first):
    far, after, near, mine = first
    return add(*mine, after, ring_hop(add(*near, far), -1))


tie = lax.optimization_barrier


def attention_forward(normed, latent, x_own, pack, gains, tab):
    core = lax.axis_index("section").reshape(1)
    part, *saved, latent_own = attend(
        core, latent, to_core(latent), tab, gains["q"], gains["kv"], pack
    )
    middle = x_own + RES_SCALE * scatter_tokens(part)
    return middle, (normed, latent_own, saved)


def layer_forward(own, x_own, middle, saved, gains, ffn_weights, far=None):
    ffn_rows = gather_dp(norm(middle, gains["ffn"]).astype(BF16))
    if far is not None:
        ffn_rows, far = tie((ffn_rows, far))
        ffn_weights = ffn_weights[:3] + [far] + ffn_weights[3:] + [to_core(far)]
    part, gu, hidden = ffn_forward(own, ffn_rows, ffn_weights)
    return part, (x_own, middle, ffn_rows, gu, hidden) + saved, ffn_weights


def layer_out_rows(part, saved):
    return (saved[1] + RES_SCALE * part).astype(BF16)


def middle_backward(grad_own, d_normed_two, saved, gains):
    d_middle, ffn_gain = norm_back(saved[1], gains["ffn"], d_normed_two)
    return d_middle + grad_own, ffn_gain


def attention_backward(part, d_middle, saved, pack, gains, also=(), after=()):
    core = lax.axis_index("section")
    x_own, _, _, _, _, _, latent_own, _ = saved
    d_latent, also = tie((scatter_tokens(part), also))
    d_q, q_gain = norm_back(latent_own[:, :QR], gains["q"], d_latent[:, :QR])
    d_c, kv_gain = norm_back(latent_own[:, QR:], gains["kv"], d_latent[:, QR : QR + KVR])
    d_rope = d_latent[:, QR + KVR + NOPE : QR + KVR + NOPE + ROPE]
    blank = jnp.zeros((SHARD, HEAD), F32)
    d_first = jnp.concatenate([d_q[:, :512], blank], axis=1).astype(BF16)
    d_second = jnp.concatenate([d_q[:, 512:], d_c, d_rope, blank[:, ROPE:]], axis=1).astype(BF16)
    mine = jnp.where(core == 0, d_first, d_second)
    other = to_core(jnp.where(core == 0, d_second, d_first))
    both = jnp.concatenate([mine, other], axis=0)
    both, after = tie((both, after))
    part = normed_back(both, pack)
    d_normed = part[:SHARD] + to_core(part[SHARD:])
    d_block, attn_gain = norm_back(x_own, gains["attn"], d_normed)
    d_block = (d_block + d_middle).astype(BF16)
    return d_block, both, jnp.concatenate([d_q, d_c, d_rope, blank[:, ROPE:]], axis=1), (attn_gain, q_gain, kv_gain), also, after


def scatter_sum(x):
    return jnp.sum(lax.all_to_all(x, "dp", 0, 0).astype(F32), axis=0)


def body(
    layer_input,
    cotangent,
    seq_lengths,
    g_attn,
    w_qa,
    g_q,
    w_qb,
    w_kva,
    g_kv,
    w_kvb,
    w_o,
    g_ffn,
    w_gate,
    w_up,
    w_down,
):
    core = lax.axis_index("section")
    blocks = ffn_pack(w_gate[0], w_up[0], w_down[0].T)
    blocks, w_qa = tie((blocks, w_qa))
    keep, give = attention_packs(
        core.reshape(1), w_qa[0], w_qb[0], w_kva[0], w_kvb[0], w_o[0].T, g_attn, g_ffn, g_q, g_kv
    )
    attn_one, attn_two = by_core(core, keep, to_core(give))
    attn_one = lax.all_gather(attn_one, "dp")

    blocks = lax.all_to_all(blocks, "dp", 0, 0)
    tab = head_tables(seq_lengths)
    blocks, cotangent, layer_input = lax.optimization_barrier((blocks, cotangent, layer_input))
    weights = blocks.reshape(D, MATS)
    near, after = ring_hop(weights, 1), ring_hop(weights, -1)

    def token_rows(x):
        packs = x.reshape(2, N_Z, SHARD, D)
        first, second = by_core(core, packs[0], packs[1])
        return from_here(first).reshape(PACK, D), from_here(second).reshape(PACK, D)

    def d_mlp_rows(grad):
        return gather_dp((RES_SCALE * grad).astype(BF16))

    def d_attended_rows(d_middle):
        return gather_tokens((RES_SCALE * d_middle).astype(BF16))

    cot_own = token_rows(cotangent)[0][:SHARD].astype(F32)
    attn_one, tab, near, after = tie((attn_one, tab, near, after))
    gains_one = attention_gains(attn_one)
    own_one = jnp.stack([(core == 0).astype(jnp.int32), core])
    own_two = jnp.stack([(core == 1).astype(jnp.int32), core])

    rows = token_rows(layer_input)
    x_own = rows[0][:SHARD].astype(F32)
    normed, latent = latents(rows, gains_one["attn"], attn_one)
    wide = (A_COLS, A_COLS, D - 2 * A_COLS)
    shared = jnp.concatenate([(RES_SCALE * cot_own).astype(BF16), normed[:SHARD]], axis=0)
    shared = [shared[:, :A_COLS], shared[:, A_COLS : 2 * A_COLS], shared[:, 2 * A_COLS :]]
    shared[2] = jnp.pad(shared[2], ((0, 0), (0, A_COLS - wide[2])))
    attn_two = lax.all_gather(jnp.concatenate([attn_two] + shared, axis=0), "dp")
    shared = [
        attn_two[:, A_ROWS + 2 * SHARD * i : A_ROWS + 2 * SHARD * (i + 1), : wide[i]] for i in range(3)
    ]
    shared = jnp.concatenate(shared, axis=2)
    d_rows_two = shared[:, :SHARD].reshape(TOKENS, D)
    normed_one = lax.dynamic_slice_in_dim(shared[:, SHARD:], lax.axis_index("dp") * SLICE, SLICE, 2)
    gains_two = attention_gains(attn_two)
    middle, saved = attention_forward(normed, latent, x_own, attn_one, gains_one, tab)
    mine = [weights, near, after]
    ffn_weights = mine + [to_core(piece) for piece in mine]
    part, saved_one, ffn_weights = layer_forward(
        own_one, x_own, middle, saved, gains_one, ffn_weights, ring_hop(near, 1)
    )
    out_one = layer_out_rows(scatter_dp(part), saved_one)
    rows_one = gather_tokens(out_one)
    x_own = out_one.astype(F32)
    normed, latent = latents(rows_one, gains_two["attn"], attn_two)
    middle, saved = attention_forward(normed, latent, x_own, attn_two, gains_two, tab)
    rows_ffn = gather_dp(norm(middle, gains_two["ffn"]).astype(BF16))
    part_two, hidden, part, d_gu = ffn_both(own_two, rows_ffn, d_rows_two, ffn_weights)
    saved_two = (x_own, middle, rows_ffn, None, hidden) + saved

    mixed_one = lax.all_gather(saved_one[-1][5], "dp")

    grads_two = ffn_gradients(own_two, d_rows_two, rows_ffn, d_gu, hidden)
    d_normed_two = scatter_dp(part)
    d_normed_two, mixed_one, normed_one = tie((d_normed_two, mixed_one, normed_one))
    ring_two = ring_pairs(grads_two)
    d_middle, ffn_gain_two = middle_backward(cot_own, d_normed_two, saved_two, gains_two)
    d_attended = d_attended_rows(d_middle)
    part, d_query, d_key_value = attend_back(d_attended, tab, saved_two[-1], attn_two)
    packs_two = attend_gradients(d_attended, saved_two[-1], d_query, d_key_value)
    in_grad_two, rows, _, dg_two, part_two, _ = attention_backward(
        part, d_middle, saved_two, attn_two, gains_two, swap_dp(part_two)
    )
    attn, q, kv = dg_two
    dg_two = jnp.concatenate([attn, ffn_gain_two, q, kv])
    dg_two = jnp.pad(dg_two, (0, 10 * LAT - dg_two.shape[0])).astype(BF16).reshape(10, LAT)
    rows = jnp.stack(gather_z(jnp.concatenate([rows, dg_two], axis=0)))
    dg_two = jnp.sum(rows[:, 2 * SHARD :].astype(F32), axis=0).reshape(-1)
    rows = rows[:, : 2 * SHARD].reshape(N_Z, 2, SHARD, LAT).transpose(1, 0, 2, 3).reshape(ROWS, LAT)
    packs_two = late_pack(saved_two[5], rows, dg_two, packs_two).reshape(-1, WO)
    in_grad_two, ring_two = tie((in_grad_two, ring_two))
    ring_two = ring_first(ring_two)

    grad_one = in_grad_two.astype(F32)
    d_rows, packs_two = tie((d_mlp_rows(grad_one), packs_two))
    packs_two = lax.psum_scatter(packs_two, "dp", scatter_dimension=0, tiled=True)
    ffn_rows, gu, hidden = saved_one[2:5]
    part, d_gu = ffn_backward(own_one, d_rows, gu, ffn_weights)
    grads_one = ffn_gradients(own_one, d_rows, ffn_rows, d_gu, hidden)
    d_normed_two = scatter_dp(part)
    total_two = ring_last(ring_two)
    d_normed_two, total_two, part_two, grads_one = tie((d_normed_two, total_two, part_two, grads_one))
    d_middle, ffn_gain_one = middle_backward(grad_one, d_normed_two, saved_one, gains_one)
    d_att_own = (RES_SCALE * d_middle).astype(BF16)
    columns = d_att_own.reshape(SHARD, N_DP, SLICE).transpose(1, 0, 2)
    d_attended = gather_tokens(d_att_own)
    part, d_query, d_key_value = attend_back(d_attended, tab, saved_one[-1], attn_one)
    low_one = low_gradients(saved_one[-1], d_query, d_key_value, columns)
    part, low_one = tie((part, low_one))
    low_one = lax.all_to_all(low_one, "dp", 0, 0)
    first = ring_first(ring_pairs(grads_one))
    part, part_two = tie((part, part_two))
    rows_two = gather_tokens(layer_out_rows(jnp.sum(part_two.astype(F32), axis=0), saved_two))
    in_grad_one, _, d_lat_own, dg_one, (low_one, rows_two), first = attention_backward(
        part, d_middle, saved_one, attn_one, gains_one, (low_one, rows_two), first
    )
    d_lat = jnp.broadcast_to(d_lat_own.astype(BF16)[None], (N_DP, SHARD, LAT_ALL))
    columns = gather_tokens(low_one[:, LOW_ROWS:, :SLICE].reshape(TOKENS, SLICE))
    wo_one = wo_gradient(columns, mixed_one)
    low_one = jnp.sum(low_one[:, :LOW_ROWS].astype(F32), axis=0)
    d_lat = lax.all_to_all(d_lat, "dp", 0, 0)
    lat_one = latent_gradient(d_lat, normed_one)
    total_one, lat_one = tie((ring_last(first), lat_one))

    attn, q, kv = dg_one
    dg_one = jnp.concatenate([attn, ffn_gain_one, q, kv])
    dg_one = jnp.pad(dg_one, (0, 3 * D - dg_one.shape[0])).astype(BF16).reshape(3, D)
    got = to_core(jnp.concatenate([jnp.where(core == 0, in_grad_two, in_grad_one), dg_one], axis=0))
    mine = jnp.where(core == 0, in_grad_one, in_grad_two)
    dg_one = add(dg_one, got[SHARD:])
    both = jnp.concatenate(
        [jnp.concatenate([mine, dg_one], axis=0), jnp.pad(got[:SHARD], ((0, 3), (0, 0)))], axis=1
    )
    both = jnp.stack(gather_z(both))
    dg_one = jnp.sum(both[:, SHARD:, :D].astype(F32), axis=0).reshape(-1)
    both = both[:, :SHARD].reshape(PACK, 2 * D)
    input_grad = in_order(both[:, :D], both[:, D:])[None]

    row = jnp.concatenate(gain_vectors(dg_one), axis=1).astype(BF16)
    row = jnp.pad(row[:, None], ((0, 0), (0, 15), (0, 0)))
    total_one = total_one.reshape(N_DP, HALF_ROWS, MATS)
    def from_other(x, layer):
        return lax.ppermute(x, "section", [(1 - layer, layer)])

    layer_out = in_order(*(jnp.where(core == 0, one, two) for one, two in zip(rows_one, rows_two)))
    total_one, pieces, layer_out, input_grad = tie(
        (
            total_one,
            (
                wo_one,
                from_other(wo_one, 0),
                low_one,
                from_other(low_one, 0),
                packs_two,
                from_other(packs_two, 1),
            ),
            layer_out,
            input_grad,
        )
    )
    blocks = jnp.concatenate([total_one, total_two.reshape(N_DP, HALF_ROWS, MATS), row], axis=1)
    blocks = lax.all_to_all(blocks, "dp", 0, 0)
    lat_one = add(lat_one, from_other(lat_one, 0))
    lat_one = sum(x.astype(F32) for x in gather_z(lat_one))
    blocks, attention = tie((blocks, home(core.reshape(1), lat_one, *pieces)))
    qa_grad, kva_grad, qb_grad, kvb_grad, wo_grad, gains = attention
    gains = gains.reshape(-1)
    dg_one = jnp.sum(blocks[:, SLICE].astype(F32), axis=0)
    gate_grad, up_grad, down_grad = ffn_unpack(core.reshape(1), blocks, to_core(blocks))

    def gain_part(one, two, width):
        return jnp.where(core == 0, dg_one[one : one + width], gains[two : two + width])[None]

    return (
        layer_out[None],
        input_grad,
        gain_part(0, 0, SLICE),
        qa_grad[None],
        gain_part(2 * SLICE, 4 * HEAD, QR // N_DP),
        qb_grad[None],
        kva_grad[None],
        gain_part(2 * SLICE + QR // N_DP, 4 * HEAD + QR // N_DP, KVR // N_DP),
        kvb_grad[None],
        wo_grad.T[None],
        gain_part(SLICE, 2 * HEAD, SLICE),
        gate_grad[None],
        up_grad[None],
        down_grad.T[None],
    )


def solution(mesh):
    in_specs = (
        P("dp", None),
        P("dp", None),
        P("dp", None),
        P("section", "dp"),
        P("section", "dp", None),
        P("section", "dp"),
        P("section", "dp", "tensor"),
        P("section", "dp", None),
        P("section", "dp"),
        P("section", "dp", "tensor"),
        P("section", "tensor", "dp"),
        P("section", "dp"),
        P("section", "dp", "tensor"),
        P("section", "dp", "tensor"),
        P("section", "tensor", "dp"),
    )
    out_specs = (
        P("section", "dp", None),
        P("section", "dp", None),
        P("section", "dp"),
        P("section", "dp", None),
        P("section", "dp"),
        P("section", "dp", "tensor"),
        P("section", "dp", None),
        P("section", "dp"),
        P("section", "dp", "tensor"),
        P("section", "tensor", "dp"),
        P("section", "dp"),
        P("section", "dp", "tensor"),
        P("section", "dp", "tensor"),
        P("section", "tensor", "dp"),
    )
    return jax.shard_map(body, mesh=mesh, in_specs=in_specs, out_specs=out_specs, check_vma=False)
```
